256 devices in a mesh: lat: 16 (over z, x_hi), lon: 4 (over x_lo, core), rep: 4 (over y).
Axes of the slice: x: 4 (x_hi: 2, x_lo: 2; x = x_hi * 2 + x_lo), y: 4, z: 8, core: 2. Of those that a mesh axis runs over, the one named last changes fastest.
Arguments:
- fields: bfloat16 [4, 2, 96, 48, 192], P('rep', None, 'lat', 'lon'), may hold values from -6 to 6
- upstream: bfloat16 [4, 2, 96, 48, 192], P('rep', None, 'lat', 'lon'), may hold values from -6 to 6
- scales: float32 [2, 2, 192], replicated, may hold values from 0.5 to 1.5
- offsets: float32 [2, 2, 192], replicated, may hold values from -1.5 to 1.5
- inward: float32 [2, 192, 576], replicated, may hold values from -0.4375 to 0.4375
- inbias: float32 [2, 576], replicated, may hold values from -1.5 to 1.5
- outward: float32 [2, 192, 192], replicated, may hold values from -0.4375 to 0.4375
- outbias: float32 [2, 192], replicated, may hold values from -1.5 to 1.5
- expand: float32 [2, 192, 768], replicated, may hold values from -0.4375 to 0.4375
- upbias: float32 [2, 768], replicated, may hold values from -1.5 to 1.5
- narrow: float32 [2, 768, 192], replicated, may hold values from -0.21875 to 0.21875
- downbias: float32 [2, 192], replicated, may hold values from -1.5 to 1.5
- tables: float32 [2, 16, 6, 3312], replicated, may hold values from -6 to 224
- window_type: int32 [2, 1, 16], replicated, may hold values from 0 to 15, as said below
- row_valid: int32 [96], replicated, may hold values from 0 to 1, as said below
Outputs:
- result: bfloat16 [4, 2, 96, 48, 192], P('rep', None, 'lat', 'lon')
- adjoint: bfloat16 [4, 2, 96, 48, 192], P('rep', None, 'lat', 'lon')
- adjoint_scales: float32 [2, 2, 192], replicated
- adjoint_offsets: float32 [2, 2, 192], replicated
- adjoint_inward: float32 [2, 192, 576], replicated
- adjoint_inbias: float32 [2, 576], replicated
- adjoint_outward: float32 [2, 192, 192], replicated
- adjoint_outbias: float32 [2, 192], replicated
- adjoint_expand: float32 [2, 192, 768], replicated
- adjoint_upbias: float32 [2, 768], replicated
- adjoint_narrow: float32 [2, 768, 192], replicated
- adjoint_downbias: float32 [2, 192], replicated
- adjoint_tables: float32 [2, 16, 6, 3312], replicated
The draws below stay inside these ranges and needn't reach their ends.
Inputs may be any that keep to these rules, and one draw needn't show every extreme that they name: `row_valid`: in every aligned group of three rows at least one row is 1. `window_type`: for each block, every table number is named by exactly one pair of level window and latitude window.
All inputs are finite; a program needn't handle non-finite values.
Results may differ from the reference program's by a relative error of at most 0.025.
Values may be sent and summed in bfloat16 or wider, within the bound.
No kernel may reach another device: no remote copies, remote signals or barrier semaphores. Data moves between devices by JAX's collectives and lax.ppermute only.
A program may use at most 128 MiB of HBM per device.

```python
import math
import jax
import jax.numpy as jnp
from jax import lax

C = 192
HEADS = 6
FFN = 768
PL = 2
REL = 3312
TYPES = 16
NLAT = 96
NLON = 48
SAMPLES = 4


def draw_tables(key, part):
    key = jax.random.fold_in(key, 7)
    target = (2, TYPES, HEADS, REL)
    return jnp.clip(jax.random.normal(jax.random.fold_in(key, 1), target, jnp.float32), -6.0, 6.0)


def draw_window_type(key, part):
    key = jax.random.fold_in(key, 13)
    first = jax.random.permutation(jax.random.fold_in(key, 1), TYPES)
    second = jax.random.permutation(jax.random.fold_in(key, 2), TYPES)
    return jnp.stack([first, second]).reshape(2, PL // 2, -1).astype(jnp.int32)


def draw_row_valid(key, part):
    key = jax.random.fold_in(key, 11)
    groups = NLAT // 3
    keeper = jax.random.randint(jax.random.fold_in(key, 1), (groups,), 0, 3)
    coins = jax.random.randint(jax.random.fold_in(key, 2), (groups, 3), 0, 2)
    places = jnp.arange(3, dtype=jnp.int32)[None, :]
    forced = (places == keeper[:, None]).astype(jnp.int32)
    return jnp.maximum(coins, forced).reshape(NLAT).astype(jnp.int32)


def steps_of(own_key, extent, cuts, least, high):
    def one(axis_at, blocks):
        steps = jax.random.uniform(jax.random.fold_in(jax.random.fold_in(own_key, 6), axis_at), (blocks,), jnp.float32, least / len(cuts), high / len(cuts))
        return jnp.repeat(jnp.exp(steps), extent[axis_at] // blocks).reshape((-1,) + (1,) * (len(extent) - axis_at - 1))

    gain = one(*cuts[0])
    for cut in cuts[1:]:
        gain = gain * one(*cut)
    return gain


def gaussian(rng, dims, width, most, shards=(), kind=jnp.bfloat16):
    values = jax.random.normal(rng, dims, jnp.float32) * width
    if len(shards) > 0:
        values = steps_of(rng, dims, shards, -0.22, 0.18) * values
    return jnp.clip(values, min=-most, max=most).astype(kind)


def setup_inputs(seed: int = 0) -> dict:
    seeds = jax.random.split(jax.random.key(seed), 16)
    return {
        "fields": gaussian(seeds[0], (SAMPLES, PL, NLAT, NLON, C), 1.0, 6.0, ((0, 4), (2, 16), (3, 4))),
        "upstream": gaussian(seeds[1], (SAMPLES, PL, NLAT, NLON, C), 1.0, 6.0, ((0, 4), (2, 16), (3, 4))),
        "scales": jnp.clip(1.0 + 0.1 * jax.random.normal(seeds[2], (2, 2, C), jnp.float32), 0.5, 1.5),
        "offsets": gaussian(seeds[3], (2, 2, C), 0.3, 1.5, (), jnp.float32),
        "inward": gaussian(seeds[4], (2, C, 3 * C), C ** -0.5, 0.4375, (), jnp.float32),
        "inbias": gaussian(seeds[5], (2, 3 * C), 0.3, 1.5, (), jnp.float32),
        "outward": gaussian(seeds[6], (2, C, C), C ** -0.5, 0.4375, (), jnp.float32),
        "outbias": gaussian(seeds[7], (2, C), 0.3, 1.5, (), jnp.float32),
        "expand": gaussian(seeds[8], (2, C, FFN), C ** -0.5, 0.4375, (), jnp.float32),
        "upbias": gaussian(seeds[9], (2, FFN), 0.3, 1.5, (), jnp.float32),
        "narrow": gaussian(seeds[10], (2, FFN, C), FFN ** -0.5, 0.21875, (), jnp.float32),
        "downbias": gaussian(seeds[11], (2, C), 0.3, 1.5, (), jnp.float32),
        "tables": draw_tables(jax.random.fold_in(seeds[15], 71), 0),
        "window_type": draw_window_type(jax.random.fold_in(seeds[15], 71), 0),
        "row_valid": draw_row_valid(jax.random.fold_in(seeds[15], 71), 0),
    }


epsilon = 1e-05
masked = -1000000000.0

def layer_norm(values, scale_row, offset_row):
    widened = values.astype(jnp.float32)
    average = lax.optimization_barrier(jnp.mean(widened, axis=-1, keepdims=True))
    centred = widened - average
    variance = lax.optimization_barrier(jnp.mean(centred * centred, axis=-1, keepdims=True))
    return (centred * lax.rsqrt(variance + epsilon) * scale_row + offset_row).astype(jnp.bfloat16)

def to_windows(sample):
    levels, row_count, col_count, features = sample.shape
    sample = sample.reshape(levels // 2, 2, row_count // 6, 6, col_count // 12, 12, features)
    sample = sample.transpose(0, 2, 4, 1, 3, 5, 6)
    return sample.reshape(levels // 2, row_count // 6, col_count // 12, 144, features)

def from_windows(blocks):
    level_wins, band_wins, col_wins, tokens, features = blocks.shape
    blocks = blocks.reshape(level_wins, band_wins, col_wins, 2, 6, 12, features)
    blocks = blocks.transpose(0, 3, 1, 4, 2, 5, 6)
    return blocks.reshape(level_wins * 2, band_wins * 6, col_wins * 12, features)

def relative_index():
    tokens = jnp.arange(144, dtype=jnp.int32)
    level_of = tokens // 72
    row_of = tokens // 12 % 6
    col_of = tokens % 12
    pair_rows = (level_of[:, None] * 2 + level_of[None, :]) * 36 + row_of[:, None] * 6 + row_of[None, :]
    return pair_rows * 23 + col_of[:, None] - col_of[None, :] + 11

def window_bias(position_table, type_ids, allowed):
    level_wins, band_wins = type_ids.shape
    type_count, head_count, rel_count = position_table.shape
    choose = (type_ids.reshape(-1, 1) == jnp.arange(type_count, dtype=jnp.int32)[None, :]).astype(jnp.float32)
    chosen = jnp.dot(choose, position_table.reshape(type_count, -1), precision=lax.Precision.HIGHEST)
    chosen = chosen.reshape(level_wins * band_wins, head_count, rel_count)
    spread = jnp.take(chosen, relative_index().reshape(-1), axis=2)
    spread = spread.reshape(level_wins, band_wins, head_count, 144, 144)
    return jnp.where(allowed[:, :, None], spread, masked)

def allowed_pairs(level_region, row_region, row_flags):
    levels = level_region.shape[0]
    row_count = row_region.shape[0]
    target = (levels // 2, row_count // 6, 2, 6, 12)
    final = (levels // 2, row_count // 6, 144)
    level_tag = jnp.broadcast_to(level_region.reshape(levels // 2, 1, 2, 1, 1), target).reshape(final)
    region_tag = jnp.broadcast_to(row_region.reshape(1, row_count // 6, 1, 6, 1), target).reshape(final)
    valid_tag = jnp.broadcast_to(row_flags.reshape(1, row_count // 6, 1, 6, 1), target).reshape(final)
    same_level = level_tag[..., :, None] == level_tag[..., None, :]
    same_region = region_tag[..., :, None] == region_tag[..., None, :]
    return same_level & same_region & (valid_tag[..., None, :] > 0)

def attend(normed, inward, inbias, outward, outbias, bias):
    levels, row_count, col_count, features = normed.shape
    head_count = bias.shape[2]
    head_size = features // head_count
    blocks = to_windows(normed)
    leading = blocks.shape[:4]
    packed = jnp.dot(blocks.reshape(-1, features), inward.astype(jnp.bfloat16), preferred_element_type=jnp.float32) + inbias
    packed = packed.astype(jnp.bfloat16).reshape(leading + (3, head_count, head_size))
    query_block = packed[..., 0, :, :].astype(jnp.float32)
    key_block = packed[..., 1, :, :].astype(jnp.float32)
    value_block = packed[..., 2, :, :].astype(jnp.float32)
    scores = jnp.einsum('plwihd,plwjhd->plwhij', query_block, key_block, precision=lax.Precision.HIGHEST)
    scores = scores * head_size ** (-0.5) + bias[:, :, None]
    row_max = lax.optimization_barrier(jnp.max(scores, axis=-1, keepdims=True))
    weights = jnp.exp(scores - row_max)
    chances = (weights / lax.optimization_barrier(jnp.sum(weights, axis=-1, keepdims=True))).astype(jnp.bfloat16)
    mixture = jnp.einsum('plwhij,plwjhd->plwihd', chances.astype(jnp.float32), value_block, precision=lax.Precision.HIGHEST)
    mixture = mixture.astype(jnp.bfloat16).reshape(-1, features)
    projected = jnp.dot(mixture, outward.astype(jnp.bfloat16), preferred_element_type=jnp.float32) + outbias
    return from_windows(projected.astype(jnp.bfloat16).reshape(leading + (features,)))

def feed_forward(carried, scale_row, offset_row, expand, upbias, narrow, downbias):
    features = carried.shape[-1]
    normed = layer_norm(carried, scale_row, offset_row).reshape(-1, features)
    hidden = jnp.dot(normed, expand.astype(jnp.bfloat16), preferred_element_type=jnp.float32) + upbias
    hidden = jax.nn.gelu(hidden, approximate=False).astype(jnp.bfloat16)
    output = jnp.dot(hidden, narrow.astype(jnp.bfloat16), preferred_element_type=jnp.float32) + downbias
    return (carried.astype(jnp.float32) + output.reshape(carried.shape)).astype(jnp.bfloat16)

def first_block(sample, params, allowed, type_ids):
    scale_set, offset_set, inward, inbias, outward, outbias, expand, upbias, narrow, downbias, position_table = params
    bias = window_bias(position_table, type_ids, allowed)
    branch = attend(layer_norm(sample, scale_set[0], offset_set[0]), inward, inbias, outward, outbias, bias)
    carried = (sample.astype(jnp.float32) + branch.astype(jnp.float32)).astype(jnp.bfloat16)
    return feed_forward(carried, scale_set[1], offset_set[1], expand, upbias, narrow, downbias)

def shifted_attention(rolled, params, allowed, type_ids):
    inward, inbias, outward, outbias, position_table = params
    bias = window_bias(position_table, type_ids, allowed)
    leveled = jnp.roll(rolled, -1, axis=0)
    return jnp.roll(attend(leveled, inward, inbias, outward, outbias, bias), 1, axis=0)

def second_tail(carried, restored, params):
    scale_set, offset_set, expand, upbias, narrow, downbias = params
    merged = (carried.astype(jnp.float32) + restored.astype(jnp.float32)).astype(jnp.bfloat16)
    return feed_forward(merged, scale_set[1], offset_set[1], expand, upbias, narrow, downbias)

def sample_forward(sample, first_params, second_params, mask_set):
    allowed_plain, types_plain, allowed_shift, types_shift = mask_set
    first_out = first_block(sample, first_params, allowed_plain, types_plain)
    normed = layer_norm(first_out, second_params[0][0], second_params[1][0])
    rolled = jnp.roll(normed, (-3, -6), axis=(1, 2))
    branch = shifted_attention(rolled, second_params[2:6] + (second_params[10],), allowed_shift, types_shift)
    restored = jnp.roll(branch, (3, 6), axis=(1, 2))
    return second_tail(first_out, restored, second_params[:2] + second_params[6:10])

def reference(fields, upstream, scales, offsets, inward, inbias, outward, outbias, expand, upbias, narrow, downbias, tables, window_type, row_valid):
    stacked = (scales, offsets, inward, inbias, outward, outbias, expand, upbias, narrow, downbias, tables)
    row_index = jnp.arange(NLAT, dtype=jnp.int32)
    level_order = jnp.arange(PL, dtype=jnp.int32)
    allowed_plain = allowed_pairs(jnp.zeros((PL,), jnp.int32), jnp.zeros((NLAT,), jnp.int32), row_valid)
    allowed_shift = allowed_pairs((level_order == PL - 1).astype(jnp.int32), (row_index >= NLAT - 3).astype(jnp.int32), jnp.take(row_valid, (row_index + 3) % NLAT))
    mask_set = (allowed_plain, window_type[0], allowed_shift, window_type[1])
    all_params = tuple((member[0] for member in stacked)) + tuple((member[1] for member in stacked))

    def one_sample(couple):
        sample, cotangent = couple

        def forward(sample_in, *flat_params):
            return sample_forward(sample_in, flat_params[:11], flat_params[11:], mask_set)
        result, pullback = jax.vjp(forward, sample, *all_params)
        adjoints = pullback(cotangent)
        return (result, adjoints[0], adjoints[1:])
    results, input_adjoint, adjoints = lax.map(one_sample, (fields, upstream))
    factor = 1.0 / math.sqrt(SAMPLES * PL * NLAT * NLON)
    summed = [lax.optimization_barrier(jnp.sum(member, axis=0)) for member in adjoints]
    joined = [jnp.stack([summed[i], summed[i + 11]]) * factor for i in range(11)]
    return (results, input_adjoint, joined[0], joined[1], joined[2], joined[3], joined[4], joined[5], joined[6], joined[7], joined[8], joined[9], joined[10])
```

```python
import math

import jax
import jax.numpy as jnp
import numpy as np
from jax import lax
from jax.experimental import pallas as pl
from jax.experimental.pallas import tpu as pltpu
from jax.sharding import PartitionSpec as P

C = 192
HEADS = 6
FFN = 768
TOK = 144
KEYS = 256
QUAD = 48
REL = 3312
ROWS = 144
CHUNK = ROWS + 16
epsilon = 1e-05
masked = -1000000000.0
f32 = jnp.float32
bf16 = jnp.bfloat16
VMEM = 48 * 1024 * 1024


def constants():
    tok = np.arange(TOK)
    a, r, c = tok // 72, tok // 12 % 6, tok % 12
    turn = np.zeros((TOK, TOK), np.float32)
    turn[tok, (r * 12 + c) * 2 + a] = 1
    quad = np.where(r >= 3, 0, 1) + np.where(c >= 6, 0, 2)
    cut = np.zeros((4 * QUAD, TOK), np.float32)
    cut[quad * QUAD + a * 18 + r % 3 * 6 + c % 6, tok] = 1
    quad = np.where(r < 3, 0, 1) + np.where(c < 6, 0, 2)
    join = np.zeros((TOK, 4 * QUAD), np.float32)
    join[tok, quad * QUAD + (1 - a) * 18 + r % 3 * 6 + c % 6] = 1
    spread = np.zeros((256, 12 * 128), np.float32)
    for ci in range(12):
        for rj in range(6):
            for cj in range(12):
                spread[rj * 23 + ci - cj + 11, ci * 128 + rj * 12 + cj] = 1
    place = np.zeros((TOK, 192), np.float32)
    place[tok, c * 16 + a * 6 + r] = 1
    sort = np.zeros((192, 192), np.float32)
    for ai in range(2):
        for aj in range(2):
            for ri in range(6):
                for h in range(HEADS):
                    sort[(h * 2 + aj) * 16 + ai * 6 + ri, ((ai * 2 + aj) * 6 + ri) * 8 + h] = 1
    made = {"turn": turn, "cut": cut, "join": join, "place": place, "sort": sort}
    made = {name: jnp.asarray(m, f32) for name, m in made.items()}
    made["spread"] = jnp.asarray(spread, bf16)
    return made


def low(ref):
    return ref[...].astype(bf16)


def dot(x, y, dims=((1,), (0,))):
    return lax.dot_general(x, y, (dims, ((), ())), preferred_element_type=f32)


def dot_nt(x, y):
    return dot(x, y, ((1,), (1,)))


def dot_tn(x, y):
    return dot(x, y, ((0,), (0,)))


def norm_parts(values):
    centred = values - jnp.mean(values, axis=-1, keepdims=True)
    rstd = lax.rsqrt(jnp.mean(centred * centred, axis=-1, keepdims=True) + epsilon)
    return centred * rstd, rstd


def norm_fwd(values, gain, shift):
    return (norm_parts(values)[0] * gain + shift).astype(bf16)


def norm_bwd(values, gain, dy):
    hat, rstd = norm_parts(values)
    dhat = dy * gain
    first = jnp.mean(dhat, axis=-1, keepdims=True)
    second = jnp.mean(dhat * hat, axis=-1, keepdims=True)
    return rstd * (dhat - first - hat * second), colsum(dy * hat), colsum(dy)


def colsum(x):
    return jnp.sum(x, axis=0, keepdims=True)


def erf(x):
    return lax.erf(x)


def gelu_parts(z):
    cdf = 0.5 * (1.0 + erf(z * (2.0 ** -0.5)))
    return cdf, z * cdf


def pad_keys(x):
    blank = jnp.zeros((56, x.shape[1]), f32)
    return jnp.concatenate([x[:72], blank, x[72:], blank], axis=0)


def unpad_keys(x):
    return jnp.concatenate([x[:72], x[128:200]], axis=0)


def head_only(x, h):
    lane = lax.broadcasted_iota(jnp.int32, x.shape, 1)
    return jnp.where((lane >= 32 * h) & (lane < 32 * h + 32), x.astype(f32), 0.0).astype(bf16)


def join_rows(refs):
    return jnp.concatenate([ref[...] for ref in refs], axis=0)


def write_pieces(pieces, refs):
    for i, ref in enumerate(refs):
        ref[...] = pieces[i * QUAD : (i + 1) * QUAD].astype(bf16)


def key_mask(valid, band, shift):
    lane = lax.broadcasted_iota(jnp.int32, (1, KEYS), 1)
    column = lane & 127
    total_rows = valid.shape[0]
    last = jnp.where(band == total_rows // 6 - 1, 1, 0)
    allowed = jnp.zeros((1, KEYS), jnp.int32)
    for r in range(6):
        at = band * 6 + r + shift
        at = jnp.where(at >= total_rows, at - total_rows, at)
        hit = (column >= 12 * r) & (column < 12 * r + 12)
        allowed = allowed + jnp.where(hit, valid[at], 0)
    if shift:
        row = lax.broadcasted_iota(jnp.int32, (TOK, KEYS), 0)
        wide = lax.broadcasted_iota(jnp.int32, (TOK, KEYS), 1)
        row_level = jnp.where(row >= 72, 1, 0)
        key_level = wide >> 7
        row_part = jnp.where(row - 72 * row_level >= 36, 1, 0)
        key_part = jnp.where((wide & 127) >= 36, 1, 0)
        apart = (row_level ^ key_level) | ((row_part ^ key_part) & last)
        allowed = jnp.where(apart == 0, jnp.broadcast_to(allowed, (TOK, KEYS)), 0)
        column = wide & 127
    mask = jnp.where(allowed > 0, 0.0, masked)
    return jnp.where(column < 72, mask, 2 * masked)


def make_bias(k, where, types, valid, tables, spread, place, sort, bias_ref, turn_ref, row_ref):
    row_ref[...] = jnp.zeros(row_ref.shape, f32)
    kind = types[k, where[0]]
    for h in range(HEADS):
        row_ref[h : h + 1, :REL] = tables[0, h, pl.ds(kind, 1), :]
    wide_rows = row_ref[...]
    rest = jnp.concatenate([wide_rows[:, 138 * i : 138 * i + 256] for i in range(24)], axis=0)
    total = None
    for _ in range(3):
        part = rest.astype(bf16)
        rest = rest - part.astype(f32)
        wide = dot(dot(sort, part).astype(bf16), spread)
        for g in range(12):
            for ci in range(12):
                turn_ref[ci * 16 : ci * 16 + 16, g * 128 : g * 128 + 128] = wide[
                    g * 16 : g * 16 + 16, ci * 128 : ci * 128 + 128
                ].astype(bf16)
        here = dot(place, turn_ref[...])
        total = here if total is None else total + here
    mask = key_mask(valid, where[0], 3 * k)
    for h in range(HEADS):
        bias_ref[:, h * KEYS : (h + 1) * KEYS] = total[:, h * KEYS : (h + 1) * KEYS] + mask


def table_adjoint(dbias, spread, place, sort, turn_ref):
    rows = dot_tn(place, dbias)
    for g in range(12):
        for ci in range(12):
            turn_ref[g * 16 : g * 16 + 16, ci * 128 : ci * 128 + 128] = rows[
                ci * 16 : ci * 16 + 16, g * 128 : g * 128 + 128
            ].astype(bf16)
    narrow = dot_nt(turn_ref[...], spread).astype(bf16)
    rows = dot_tn(sort, narrow)
    pieces = [rows[8 * i : 8 * i + 8, :138] for i in range(24)]
    return jnp.concatenate(pieces + [jnp.zeros((8, 16), f32)], axis=1)


def put(pack, at, value):
    done = 0
    while done < value.shape[0]:
        chunk, row = divmod(at + done, ROWS)
        size = min(ROWS - row, value.shape[0] - done)
        pack[chunk, row : row + size] = value[done : done + size].astype(bf16)
        done += size


def put_rest(pack, table, small):
    row = lax.broadcasted_iota(jnp.int32, (8, 2 * C), 0)
    for chunk in range(8):
        own = table[:, 384 * chunk : 384 * chunk + 384]
        if chunk < 2:
            left = table[:, 3072 + 128 * chunk : 3200 + 128 * chunk]
            moved = [pltpu.roll(left, 6 - 2 * i, 0) if i < 3 else left for i in range(3)]
            own = jnp.where(row >= 6, jnp.concatenate(moved, axis=1), own)
        short = jnp.where(row == 0, small[chunk], 0.0) if chunk < len(small) else jnp.zeros((8, 2 * C), f32)
        pack[chunk, ROWS : ROWS + 16] = jnp.concatenate([own, short], axis=0).astype(bf16)


def attend_fwd(k, u, inward, inbias, outward, outbias, bias_ref, q_ref, k_ref, v_ref, p_ref, mix_ref):
    weight = inward[0].astype(bf16)
    shift = inbias[k : k + 1]
    keyed = pad_keys(u.astype(f32)).astype(bf16)
    q = (dot(u, weight[:, :C]) + shift[:, :C]).astype(bf16)
    key = (dot(keyed, weight[:, C : 2 * C]) + shift[:, C : 2 * C]).astype(bf16)
    v = (dot(keyed, weight[:, 2 * C :]) + shift[:, 2 * C :]).astype(bf16)
    q_ref[...] = q
    k_ref[...] = key
    v_ref[...] = v
    mix = jnp.zeros((TOK, C), f32)
    for h in range(HEADS):
        scores = dot_nt(head_only(q, h), key) * 32 ** (-0.5) + bias_ref[:, h * KEYS : (h + 1) * KEYS]
        weights = jnp.exp(scores - jnp.max(scores, axis=-1, keepdims=True))
        chances = (weights / jnp.sum(weights, axis=-1, keepdims=True)).astype(bf16)
        p_ref[h] = chances
        mix = mix + dot(chances, head_only(v, h))
    mix = mix.astype(bf16)
    mix_ref[...] = mix
    return (dot(mix, outward[0].astype(bf16)) + outbias[k : k + 1]).astype(bf16)


def attend_bwd(dout, u, inward, outward, spread, place, sort, q_ref, k_ref, v_ref, p_ref, mix_ref, pack, dbias_ref, turn_ref):
    q, key, v, mix = q_ref[...], k_ref[...], v_ref[...], mix_ref[...]
    weight = inward[0].astype(bf16)
    dmix = dot_nt(dout, outward[0].astype(bf16)).astype(bf16)
    dq = jnp.zeros((TOK, C), f32)
    dk = jnp.zeros((KEYS, C), f32)
    dv = jnp.zeros((KEYS, C), f32)
    for h in range(HEADS):
        chances = p_ref[h]
        wide = chances.astype(f32)
        dmix_h = head_only(dmix, h)
        dchances = dot_nt(dmix_h, v)
        dscores = wide * (dchances - jnp.sum(wide * dchances, axis=-1, keepdims=True))
        narrow = dscores.astype(bf16)
        dbias_ref[:, h * KEYS : (h + 1) * KEYS] = narrow
        dv = dv + dot_tn(chances, dmix_h)
        dq = dq + dot(narrow, head_only(key, h))
        dk = dk + dot_tn(narrow, head_only(q, h))
    dq = (dq * 32 ** (-0.5)).astype(bf16)
    dk = (dk * 32 ** (-0.5)).astype(bf16)
    dv = dv.astype(bf16)
    keyed = pad_keys(u.astype(f32)).astype(bf16)
    du = dot_nt(dq, weight[:, :C]) + unpad_keys(
        dot_nt(dk, weight[:, C : 2 * C]) + dot_nt(dv, weight[:, 2 * C :])
    )
    pair = lambda x, y: jnp.concatenate([x, y], axis=1)
    put(pack, 4 * C, pair(dot_tn(u, dq), dot_tn(keyed, dk)))
    put(pack, 5 * C, pair(dot_tn(keyed, dv), dot_tn(mix, dout)))
    small = [
        pair(colsum(dq.astype(f32)), colsum(dk.astype(f32))),
        pair(colsum(dv.astype(f32)), colsum(dout.astype(f32))),
    ]
    return du, table_adjoint(dbias_ref[...], spread, place, sort, turn_ref), small


def mlp_fwd(h, gain, shift, expand, upbias, narrow_t, downbias):
    z = dot(norm_fwd(h, gain, shift), expand) + upbias
    hidden = gelu_parts(z)[1].astype(bf16)
    return (h + dot_nt(hidden, narrow_t) + downbias).astype(bf16)


def mlp_both(h, gain, shift, expand, upbias, narrow_t, downbias, dout, want):
    normed = norm_fwd(h, gain, shift)
    z = dot(normed, expand) + upbias
    cdf, wide = gelu_parts(z)
    hidden = wide.astype(bf16)
    result = None
    if want:
        result = (h + dot_nt(hidden, narrow_t) + downbias).astype(bf16)
    slope = cdf + z * jnp.exp(-0.5 * z * z) * (1.0 / math.sqrt(2.0 * math.pi))
    dz32 = dot(dout, narrow_t) * slope
    dz = dz32.astype(bf16)
    dnormed = dot_nt(dz, expand).astype(bf16).astype(f32)
    dx, dgain, dshift = norm_bwd(h, gain, dnormed)
    dwide = dout.astype(f32)
    dh = (dwide + dx).astype(bf16)
    dexpand = dot_tn(normed, dz)
    dnarrow = dot_tn(dout, hidden)
    dense = [dexpand[:, : 2 * C], dexpand[:, 2 * C :], dnarrow[:, : 2 * C], dnarrow[:, 2 * C :]]
    dup = colsum(dz32)
    small = [
        dup[:, : 2 * C],
        dup[:, 2 * C :],
        jnp.concatenate([colsum(dwide), dgain], axis=1),
        jnp.concatenate([dshift, jnp.zeros((1, C), f32)], axis=1),
    ]
    return result, dh, dense, small


def bias_kernel(where, types, valid, tables, spread, place, sort, bias_ref, turned, rows):
    make_bias(1, where, types, valid, tables, spread[...], low(place), low(sort), bias_ref, turned, rows)


def first_kernel(
    where, types, valid, fields, scales, offsets, inward, inbias, outward, outbias, expand, upbias, narrow, downbias,
    tables, turn, cut, spread, place, sort,
    q, k, v, p, mix, h1, y1, pa, pb, pc, pd, bias, turned, rows,
):
    make_bias(0, where, types, valid, tables, spread[...], low(place), low(sort), bias, turned, rows)
    x = dot(low(turn), fields[...])
    u = norm_fwd(x, scales[0, 0:1], offsets[0, 0:1])
    branch = attend_fwd(0, u, inward, inbias, outward, outbias, bias, q, k, v, p, mix)
    carried = (x + branch.astype(f32)).astype(bf16)
    h1[...] = carried
    out = mlp_fwd(
        carried.astype(f32), scales[0, 1:2], offsets[0, 1:2], expand[0].astype(bf16), upbias[0:1],
        narrow[0].astype(bf16), downbias[0:1],
    )
    y1[...] = out
    normed = norm_fwd(out.astype(f32), scales[1, 0:1], offsets[1, 0:1])
    write_pieces(dot(low(cut), normed), (pa, pb, pc, pd))


def second_kernel(
    qa, qb, qc, qd, inward, inbias, outward, outbias, bias, join,
    u_ref, q, k, v, p, mix, pa, pb, pc, pd,
):
    route = low(join)
    u = dot(route, join_rows((qa, qb, qc, qd))).astype(bf16)
    u_ref[...] = u
    branch = attend_fwd(1, u, inward, inbias, outward, outbias, bias, q, k, v, p, mix)
    write_pieces(dot_tn(route, branch), (pa, pb, pc, pd))


def tail_kernel(
    qa, qb, qc, qd, y1, upstream, scales, offsets, expand, upbias, narrow, downbias, turn, cut,
    result, dh_ref, dense_ref, small_ref, pa, pb, pc, pd,
):
    route = low(cut)
    order = low(turn)
    restored = dot_tn(route, join_rows((qa, qb, qc, qd)))
    h2 = (y1[...].astype(f32) + restored).astype(bf16).astype(f32)
    out, dh, dense, small = mlp_both(
        h2, scales[1, 1:2], offsets[1, 1:2], expand[0].astype(bf16), upbias[1:2],
        narrow[0].astype(bf16), downbias[1:2], dot(order, upstream[...]).astype(bf16), True,
    )
    result[...] = dot_tn(order, out).astype(bf16)
    dh_ref[...] = dh
    for i, part in enumerate(dense):
        dense_ref[i * C : (i + 1) * C] = part.astype(bf16)
    for i, row in enumerate(small):
        small_ref[i : i + 1] = row
    write_pieces(dot(route, dh), (pa, pb, pc, pd))


def second_back_kernel(
    qa, qb, qc, qd, dense, short, u, inward, outward, q, k, v, p, mix, join, spread, place, sort,
    pack, pa, pb, pc, pd, dbias, turned,
):
    route = low(join)
    dout = dot(route, join_rows((qa, qb, qc, qd))).astype(bf16)
    du, table, small = attend_bwd(
        dout, u[...], inward, outward, spread[...], low(place), low(sort), q, k, v, p, mix, pack, dbias, turned
    )
    put(pack, 0, dense[...])
    put_rest(pack, table, [short[i : i + 1] for i in range(4)] + small)
    write_pieces(dot_tn(route, du.astype(bf16)), (pa, pb, pc, pd))


def first_back_kernel(
    qa, qb, qc, qd, fields, dh2, y1, h1, scales, offsets, inward, outward, expand, upbias, narrow, downbias,
    q, k, v, p, mix, turn, cut, spread, place, sort,
    adjoint, pack, dbias, turned,
):
    order = low(turn)
    dn = dot_tn(low(cut), join_rows((qa, qb, qc, qd)))
    dx, dgain, dshift = norm_bwd(y1[...].astype(f32), scales[1, 0:1], dn)
    dy1 = (dh2[...].astype(f32) + dx.astype(bf16).astype(f32)).astype(bf16)
    _, dh1, dense, short = mlp_both(
        h1[...].astype(f32), scales[0, 1:2], offsets[0, 1:2], expand[0].astype(bf16), upbias[0:1],
        narrow[0].astype(bf16), downbias[0:1], dy1, False,
    )
    for i, part in enumerate(dense):
        put(pack, i * C, part)
    x = dot(order, fields[...])
    u = norm_fwd(x, scales[0, 0:1], offsets[0, 0:1])
    du, table, small = attend_bwd(
        dh1, u, inward, outward, spread[...], low(place), low(sort), q, k, v, p, mix, pack, dbias, turned
    )
    dx0, dgain0, dshift0 = norm_bwd(x, scales[0, 0:1], du.astype(bf16).astype(f32))
    adjoint[...] = dot_tn(order, (dh1.astype(f32) + dx0).astype(bf16)).astype(bf16)
    pair = lambda x, y: jnp.concatenate([x, y], axis=1)
    put_rest(pack, table, short + small + [pair(dgain0, dshift0), pair(dgain, dshift)])


def core_kernel(where, first, second, got_first, got_second, *outs):
    def deal(own, got):
        for d, out in enumerate(outs):
            at = (where[3] ^ d) * 2
            out[...] = (own[pl.ds(at, 2)].astype(f32) + got[pl.ds(at, 2)].astype(f32)).astype(bf16)

    @pl.when(where[1] == 0)
    def _():
        deal(first, got_first)

    @pl.when(where[1] != 0)
    def _():
        deal(second, got_second)


def samples_kernel(where, a, b, c, d, keep, send):
    for out, at in ((keep, where[2]), (send, where[2] ^ 1)):
        total = a[at].astype(f32) + b[at].astype(f32) + c[at].astype(f32) + d[at].astype(f32)
        out[...] = total.astype(bf16)


def pair_kernel(a, b, out):
    out[...] = (a[...].astype(f32) + b[...].astype(f32)).astype(bf16)


def band_kernel(a, b, c, d, out):
    four = [ref[...].astype(f32) for ref in (a, b, c, d)]
    total = four[0] + four[1] + four[2] + four[3]
    out[:ROWS] = total[:ROWS].astype(bf16)
    if a.shape[0] == CHUNK:
        aside = jnp.concatenate([total[ROWS + 8 :], jnp.zeros((8, 2 * C), f32)], axis=0)
        out[ROWS:CHUNK] = aside.astype(bf16)
        out[CHUNK:] = jnp.concatenate([m[ROWS : ROWS + 8] for m in four], axis=0).astype(bf16)
    else:
        out[ROWS:CHUNK] = total[ROWS:CHUNK].astype(bf16)
        for i, ref in enumerate((a, b, c, d)):
            out[CHUNK + 32 * i : CHUNK + 32 * i + 32] = ref[CHUNK:]


def final_kernel(
    where, types, own, got,
    scales, offsets, inward, inbias, outward, outbias, expand, upbias, narrow, downbias, tables, dense, *, factor
):
    def routes(k):
        lane = lax.broadcasted_iota(jnp.int32, (1, 128), 1)
        kind = jnp.zeros((1, 128), jnp.int32)
        for e in range(16):
            kind = kind + jnp.where((lane >> 3) == e, types[k, where[0] ^ e], 0)
        row = lax.broadcasted_iota(jnp.int32, (96, 128), 0)
        part = lax.broadcasted_iota(jnp.int32, (96, 128), 1) & 7
        head, match = row >> 4, (row & 15) == kind
        made = [match & (part == head)]
        for i in range(3):
            made.append(match & ((head >> 1) == i) & (part == 6 + (head & 1)))
        return [jnp.where(m, 1.0, 0.0).astype(bf16) for m in made]

    def unpack(k, ref):
        route = routes(k)
        left = None
        small = []
        for chunk in range(8):
            at = (where[3] ^ (chunk // 2), where[2] ^ (chunk % 2))
            dense[chunk * ROWS : (chunk + 1) * ROWS] = ref[at[0], at[1], :ROWS]
            small.append(ref[at[0], at[1], ROWS:CHUNK].astype(f32)[0:1] * factor)
            here = ref[at[0], at[1], CHUNK:]
            rows = dot(route[0], here) * factor
            for h in range(HEADS):
                tables[k, h, :, 384 * chunk : 384 * chunk + 384] = rows[16 * h : 16 * h + 16]
            if chunk < 2:
                left = sum(dot(route[1 + i], here[:, 128 * i : 128 * i + 128]) for i in range(3)) * factor
                start = 3072 + 128 * chunk
                size = min(128, REL - start)
                for h in range(HEADS):
                    tables[k, h, :, start : start + size] = left[16 * h : 16 * h + 16, :size]
        load = lambda i: dense[i * C : (i + 1) * C].astype(f32) * factor
        expand[k, :, : 2 * C] = load(0)
        expand[k, :, 2 * C :] = load(1)
        narrow[k, :, : 2 * C] = load(2)
        narrow[k, :, 2 * C :] = load(3)
        inward[k, :, : 2 * C] = load(4)
        both = load(5)
        inward[k, :, 2 * C :] = both[:, :C]
        outward[k] = both[:, C:]
        upbias[k : k + 1, : 2 * C] = small[0]
        upbias[k : k + 1, 2 * C :] = small[1]
        downbias[k : k + 1] = small[2][:, :C]
        scales[k, 1:2] = small[2][:, C:]
        offsets[k, 1:2] = small[3][:, :C]
        inbias[k : k + 1, : 2 * C] = small[4]
        inbias[k : k + 1, 2 * C :] = small[5][:, :C]
        outbias[k : k + 1] = small[5][:, C:]
        if k == 0:
            for i in range(2):
                scales[i, 0:1] = small[6 + i][:, :C]
                offsets[i, 0:1] = small[6 + i][:, C:]

    @pl.when(where[1] == 0)
    def _():
        unpack(0, own)
        unpack(1, got)

    @pl.when(where[1] != 0)
    def _():
        unpack(0, got)
        unpack(1, own)


def call(kernel, ins, outs, scratch=(), flops=0):
    specs = []
    for array, block in ins:
        dims = array.ndim
        if block == "smem":
            specs.append(pl.BlockSpec(memory_space=pltpu.SMEM))
        elif block is None:
            specs.append(pl.BlockSpec(array.shape, lambda i, dims=dims: (0,) * dims))
        else:
            specs.append(
                pl.BlockSpec((1,) + array.shape[1:], lambda i, dims=dims, block=block: (block,) + (0,) * (dims - 1))
            )
    size = lambda s: math.prod(s.shape) * jnp.dtype(s.dtype).itemsize
    moved = sum(size(o) for o in outs) + sum(size(a) // (1 if b in (None, "smem") else a.shape[0]) for a, b in ins)
    return pl.pallas_call(
        kernel,
        grid=(1,),
        in_specs=specs,
        out_specs=[pl.BlockSpec(o.shape, lambda i, dims=len(o.shape): (0,) * dims) for o in outs],
        out_shape=outs,
        scratch_shapes=list(scratch),
        compiler_params=pltpu.CompilerParams(vmem_limit_bytes=VMEM),
        cost_estimate=pl.CostEstimate(flops=flops, bytes_accessed=moved, transcendentals=0),
    )(*[array for array, _ in ins])


def send_pieces(pieces, step):
    lat, lon = lax.axis_size("lat"), lax.axis_size("lon")
    rows = [(i, (i + step) % lat) for i in range(lat)]
    cols = [(i, (i + step) % lon) for i in range(lon)]
    both = [(i * lon + j, (i + step) % lat * lon + (j + step) % lon) for i in range(lat) for j in range(lon)]
    return (
        pieces[0],
        lax.ppermute(pieces[1], "lat", rows),
        lax.ppermute(pieces[2], "lon", cols),
        lax.ppermute(pieces[3], ("lat", "lon"), both),
    )


def swap(array, axis, distance, only=None):
    devices = range(lax.axis_size(axis))
    return lax.ppermute(array, axis, [(i, i ^ distance) for i in devices if only is None or i % 2 == only])


def body(
    fields, upstream, scales, offsets, inward, inbias, outward, outbias, expand, upbias, narrow, downbias,
    tables, window_type, row_valid,
):
    lon = lax.axis_index("lon")
    where = jnp.stack([lax.axis_index("lat"), lon % 2, lon // 2, lax.axis_index("rep")]).astype(jnp.int32)
    const = constants()
    types = window_type[:, 0, :]
    levels, row_count, col_count = fields.shape[1:4]
    total_rows = row_valid.shape[0]
    x = fields[0].transpose(1, 2, 0, 3).reshape(TOK, C)
    cotangent = upstream[0].transpose(1, 2, 0, 3).reshape(TOK, C)
    narrow = jnp.swapaxes(narrow, 1, 2)
    tables = jnp.swapaxes(tables, 1, 2)
    of = jax.ShapeDtypeStruct
    piece = [of((QUAD, C), bf16)] * 4
    token = of((TOK, C), bf16)
    state = [token, of((KEYS, C), bf16), of((KEYS, C), bf16), of((HEADS, TOK, KEYS), bf16), token]
    pack = of((8, CHUNK, 2 * C), bf16)
    turned = pltpu.VMEM((192, 1536), bf16)
    dbias = pltpu.VMEM((TOK, 1536), bf16)
    rows = pltpu.VMEM((8, 3456), f32)
    whole = lambda *arrays: [(m, None) for m in arrays]
    fixed = lambda *names: [(const[name], None) for name in names]
    scalars = [(where, "smem"), (types, "smem"), (row_valid, "smem")]

    *state0, h1, y1, pa, pb, pc, pd = call(
        first_kernel,
        scalars
        + whole(x, scales, offsets)
        + [(inward, 0)] + whole(inbias) + [(outward, 0)] + whole(outbias)
        + [(expand, 0)] + whole(upbias) + [(narrow, 0)] + whole(downbias)
        + [(tables, 0)]
        + fixed("turn", "cut", "spread", "place", "sort"),
        state + [token, token] + piece,
        (pltpu.VMEM((TOK, 1536), f32), turned, rows),
        10**9,
    )
    pieces = send_pieces((pa, pb, pc, pd), -1)
    (bias1,) = call(
        bias_kernel,
        scalars + [(tables, 1)] + fixed("spread", "place", "sort"),
        [of((TOK, 1536), f32)],
        (turned, rows),
        10**9,
    )
    u1, *rest = call(
        second_kernel,
        whole(*pieces) + [(inward, 1)] + whole(inbias) + [(outward, 1)] + whole(outbias, bias1) + fixed("join"),
        [token] + state + piece,
        (),
        10**9,
    )
    state1, pieces = rest[:5], send_pieces(rest[5:], 1)
    result, dh2, dense1, small1, *pieces = call(
        tail_kernel,
        whole(*pieces, y1, cotangent, scales, offsets)
        + [(expand, 1)] + whole(upbias) + [(narrow, 1)] + whole(downbias)
        + fixed("turn", "cut"),
        [token, token, of((4 * C, 2 * C), bf16), of((8, 2 * C), f32)] + piece,
        (),
        10**9,
    )
    pieces = send_pieces(pieces, -1)
    pack1, *pieces = call(
        second_back_kernel,
        whole(*pieces, dense1, small1, u1) + [(inward, 1), (outward, 1)] + whole(*state1)
        + fixed("join", "spread", "place", "sort"),
        [pack] + piece,
        (dbias, turned),
        10**9,
    )
    pieces = send_pieces(pieces, 1)
    got1 = swap(pack1, "lon", 1, 0)
    adjoint, pack0 = call(
        first_back_kernel,
        whole(*pieces, x, dh2, y1, h1, scales, offsets) + [(inward, 0), (outward, 0), (expand, 0)] + whole(upbias)
        + [(narrow, 0)] + whole(downbias, *state0) + fixed("turn", "cut", "spread", "place", "sort"),
        [token, pack],
        (dbias, turned),
        10**9,
    )
    got0 = swap(pack0, "lon", 1, 1)

    part = of((2, CHUNK, 2 * C), bf16)
    a, b, c, d = call(core_kernel, scalars[:1] + whole(pack0, pack1, got0, got1), [part] * 4)
    b, c, d = (swap(m, "rep", i + 1) for i, m in enumerate((b, c, d)))
    chunk = of((CHUNK, 2 * C), bf16)
    keep, give = call(samples_kernel, scalars[:1] + whole(a, b, c, d), [chunk, chunk])
    (a,) = call(pair_kernel, whole(keep, swap(give, "lon", 2)), [chunk])
    for step, height in ((1, CHUNK + 32), (4, CHUNK + 128)):
        others = [swap(a, "lat", step * i) for i in (1, 2, 3)]
        (a,) = call(band_kernel, whole(a, *others), [of((height, 2 * C), bf16)])
    a = jnp.stack([a, swap(a, "lon", 2)])
    a = jnp.stack([a] + [swap(a, "rep", i) for i in (1, 2, 3)])
    got = swap(a, "lon", 1)

    factor = 1.0 / math.sqrt(lax.axis_size("rep") * levels * total_rows * col_count * lax.axis_size("lon"))

    def finish(*refs):
        final_kernel(*refs, factor=factor)

    outs = [
        (2, 2, C), (2, 2, C), (2, C, 3 * C), (2, 3 * C), (2, C, C), (2, C), (2, C, FFN), (2, FFN), (2, C, FFN),
        (2, C), tables.shape,
    ]
    joined = list(
        call(
            finish,
            scalars[:2] + whole(a, got),
            [of(s, f32) for s in outs],
            (pltpu.VMEM((8 * ROWS, 2 * C), bf16),),
        )
    )
    joined[8] = jnp.swapaxes(joined[8], 1, 2)
    joined[10] = jnp.swapaxes(joined[10], 1, 2)
    back = lambda m: m.reshape(row_count, col_count, levels, C).transpose(2, 0, 1, 3)[None]
    return (back(result), back(adjoint), *joined)


def solution(mesh):
    grid = P("rep", None, "lat", "lon", None)
    return jax.shard_map(
        body, mesh=mesh, in_specs=(grid, grid) + (P(),) * 13, out_specs=(grid, grid) + (P(),) * 11, check_vma=False
    )
```

```python
import math

import jax
import jax.numpy as jnp
import numpy as np
from jax import lax
from jax.experimental import pallas as pl
from jax.experimental.pallas import tpu as pltpu
from jax.sharding import PartitionSpec as P

C = 192
HEADS = 6
FFN = 768
TOK = 144
KEYS = 256
QUAD = 48
REL = 3312
ROWS = 144
CHUNK = ROWS + 16
epsilon = 1e-05
masked = -1000000000.0
f32 = jnp.float32
bf16 = jnp.bfloat16
VMEM = 64 * 1024 * 1024
SMALL = 16 * 1024 * 1024


def constants():
    tok = np.arange(TOK)
    a, r, c = tok // 72, tok // 12 % 6, tok % 12
    turn = np.zeros((TOK, TOK), np.float32)
    turn[tok, (r * 12 + c) * 2 + a] = 1
    quad = np.where(r >= 3, 0, 1) + np.where(c >= 6, 0, 2)
    cut = np.zeros((4 * QUAD, TOK), np.float32)
    cut[quad * QUAD + a * 18 + r % 3 * 6 + c % 6, tok] = 1
    quad = np.where(r < 3, 0, 1) + np.where(c < 6, 0, 2)
    join = np.zeros((TOK, 4 * QUAD), np.float32)
    join[tok, quad * QUAD + (1 - a) * 18 + r % 3 * 6 + c % 6] = 1
    spread = np.zeros((256, 12 * 128), np.float32)
    for ci in range(12):
        for rj in range(6):
            for cj in range(12):
                spread[rj * 23 + ci - cj + 11, ci * 128 + rj * 12 + cj] = 1
    place = np.zeros((TOK, 192), np.float32)
    place[tok, c * 16 + a * 6 + r] = 1
    sort = np.zeros((192, 192), np.float32)
    for ai in range(2):
        for aj in range(2):
            for ri in range(6):
                for h in range(HEADS):
                    sort[(h * 2 + aj) * 16 + ai * 6 + ri, ((ai * 2 + aj) * 6 + ri) * 8 + h] = 1
    made = {"turn": turn, "cut": cut, "join": join, "place": place, "sort": sort}
    made = {name: jnp.asarray(m, f32) for name, m in made.items()}
    made["spread"] = jnp.asarray(spread, bf16)
    return made


def low(ref):
    return ref[...].astype(bf16)


def dot(x, y, dims=((1,), (0,))):
    return lax.dot_general(x, y, (dims, ((), ())), preferred_element_type=f32)


def dot_nt(x, y):
    return dot(x, y, ((1,), (1,)))


def dot_tn(x, y):
    return dot(x, y, ((0,), (0,)))


def norm_parts(values):
    centred = values - jnp.mean(values, axis=-1, keepdims=True)
    rstd = lax.rsqrt(jnp.mean(centred * centred, axis=-1, keepdims=True) + epsilon)
    return centred * rstd, rstd


def norm_fwd(values, gain, shift):
    return (norm_parts(values)[0] * gain + shift).astype(bf16)


def norm_bwd(values, gain, dy):
    hat, rstd = norm_parts(values)
    dhat = dy * gain
    first = jnp.mean(dhat, axis=-1, keepdims=True)
    second = jnp.mean(dhat * hat, axis=-1, keepdims=True)
    return rstd * (dhat - first - hat * second), colsum(dy * hat), colsum(dy)


def colsum(x):
    return jnp.sum(x, axis=0, keepdims=True)


def erf(x):
    return lax.erf(x)


def gelu_parts(z):
    cdf = 0.5 * (1.0 + erf(z * (2.0 ** -0.5)))
    return cdf, z * cdf


def pad_keys(x):
    blank = jnp.zeros((56, x.shape[1]), f32)
    return jnp.concatenate([x[:72], blank, x[72:], blank], axis=0)


def unpad_keys(x):
    return jnp.concatenate([x[:72], x[128:200]], axis=0)


def head_only(x, h):
    lane = lax.broadcasted_iota(jnp.int32, x.shape, 1)
    return jnp.where((lane >= 32 * h) & (lane < 32 * h + 32), x.astype(f32), 0.0).astype(bf16)


def join_rows(refs, part):
    return jnp.concatenate([ref[part * QUAD : (part + 1) * QUAD] for ref in refs], axis=0)


def write_pieces(first, second, refs):
    for i, ref in enumerate(refs):
        ref[:QUAD] = first[i * QUAD : (i + 1) * QUAD].astype(bf16)
        ref[QUAD:] = second[i * QUAD : (i + 1) * QUAD].astype(bf16)


def kind_of(info, k, band):
    return info[4 + 16 * k + band]


def key_mask(info, shift):
    band = info[0]
    lane = lax.broadcasted_iota(jnp.int32, (1, KEYS), 1)
    column = lane & 127
    total_rows = info.shape[0] - 36
    last = jnp.where(band == total_rows // 6 - 1, 1, 0)
    allowed = jnp.zeros((1, KEYS), jnp.int32)
    for r in range(6):
        at = band * 6 + r + shift
        at = jnp.where(at >= total_rows, at - total_rows, at)
        hit = (column >= 12 * r) & (column < 12 * r + 12)
        allowed = allowed + jnp.where(hit, info[36 + at], 0)
    if shift:
        row = lax.broadcasted_iota(jnp.int32, (TOK, KEYS), 0)
        wide = lax.broadcasted_iota(jnp.int32, (TOK, KEYS), 1)
        row_level = jnp.where(row >= 72, 1, 0)
        key_level = wide >> 7
        row_part = jnp.where(row - 72 * row_level >= 36, 1, 0)
        key_part = jnp.where((wide & 127) >= 36, 1, 0)
        apart = (row_level ^ key_level) | ((row_part ^ key_part) & last)
        allowed = jnp.where(apart == 0, jnp.broadcast_to(allowed, (TOK, KEYS)), 0)
        column = wide & 127
    mask = jnp.where(allowed > 0, 0.0, masked)
    return jnp.where(column < 72, mask, 2 * masked)


def make_bias(k, info, tables, spread, place, sort, bias_ref, turn_ref, row_ref):
    row_ref[...] = jnp.zeros(row_ref.shape, f32)
    kind = kind_of(info, k, info[0])
    for h in range(HEADS):
        row_ref[h : h + 1, :REL] = tables[0, h, pl.ds(kind, 1), :]
    wide_rows = row_ref[...]
    rest = jnp.concatenate([wide_rows[:, 138 * i : 138 * i + 256] for i in range(24)], axis=0)
    total = None
    for _ in range(3):
        part = rest.astype(bf16)
        rest = rest - part.astype(f32)
        wide = dot(dot(sort, part).astype(bf16), spread)
        for g in range(12):
            for ci in range(12):
                turn_ref[ci * 16 : ci * 16 + 16, g * 128 : g * 128 + 128] = wide[
                    g * 16 : g * 16 + 16, ci * 128 : ci * 128 + 128
                ].astype(bf16)
        here = dot(place, turn_ref[...])
        total = here if total is None else total + here
    mask = key_mask(info, 3 * k)
    for h in range(HEADS):
        bias_ref[:, h * KEYS : (h + 1) * KEYS] = total[:, h * KEYS : (h + 1) * KEYS] + mask


def table_adjoint(dbias, spread, place, sort, turn_ref):
    rows = dot_tn(place, dbias)
    for g in range(12):
        for ci in range(12):
            turn_ref[g * 16 : g * 16 + 16, ci * 128 : ci * 128 + 128] = rows[
                ci * 16 : ci * 16 + 16, g * 128 : g * 128 + 128
            ].astype(bf16)
    narrow = dot_nt(turn_ref[...], spread).astype(bf16)
    rows = dot_tn(sort, narrow)
    pieces = [rows[8 * i : 8 * i + 8, :138] for i in range(24)]
    return jnp.concatenate(pieces + [jnp.zeros((8, 16), f32)], axis=1)


def put(pack, at, value):
    done = 0
    while done < value.shape[0]:
        chunk, row = divmod(at + done, ROWS)
        size = min(ROWS - row, value.shape[0] - done)
        pack[chunk, row : row + size] = value[done : done + size].astype(bf16)
        done += size


def put_rest(pack, table, small):
    row = lax.broadcasted_iota(jnp.int32, (8, 2 * C), 0)
    for chunk in range(8):
        own = table[:, 384 * chunk : 384 * chunk + 384]
        if chunk < 2:
            left = table[:, 3072 + 128 * chunk : 3200 + 128 * chunk]
            moved = [pltpu.roll(left, 6 - 2 * i, 0) if i < 3 else left for i in range(3)]
            own = jnp.where(row >= 6, jnp.concatenate(moved, axis=1), own)
        short = jnp.where(row == 0, small[chunk], 0.0) if chunk < len(small) else jnp.zeros((8, 2 * C), f32)
        pack[chunk, ROWS : ROWS + 16] = jnp.concatenate([own, short], axis=0).astype(bf16)


def attend_fwd(k, u, inward, inbias, outward, outbias, bias_ref, q_ref, k_ref, v_ref, p_ref, mix_ref):
    weight = inward[0].astype(bf16)
    shift = inbias[k : k + 1]
    keyed = pad_keys(u.astype(f32)).astype(bf16)
    q = (dot(u, weight[:, :C]) + shift[:, :C]).astype(bf16)
    key = (dot(keyed, weight[:, C : 2 * C]) + shift[:, C : 2 * C]).astype(bf16)
    v = (dot(keyed, weight[:, 2 * C :]) + shift[:, 2 * C :]).astype(bf16)
    q_ref[...] = q
    k_ref[...] = key
    v_ref[...] = v
    mix = jnp.zeros((TOK, C), f32)
    for h in range(HEADS):
        scores = dot_nt(head_only(q, h), key) * 32 ** (-0.5) + bias_ref[:, h * KEYS : (h + 1) * KEYS]
        weights = jnp.exp(scores - jnp.max(scores, axis=-1, keepdims=True))
        chances = (weights / jnp.sum(weights, axis=-1, keepdims=True)).astype(bf16)
        p_ref[h] = chances
        mix = mix + dot(chances, head_only(v, h))
    mix = mix.astype(bf16)
    mix_ref[...] = mix
    return (dot(mix, outward[0].astype(bf16)) + outbias[k : k + 1]).astype(bf16)


def attend_bwd(dout, u, inward, outward, spread, place, sort, q_ref, k_ref, v_ref, p_ref, mix_ref, pack, dbias_ref, turn_ref):
    q, key, v, mix = q_ref[...], k_ref[...], v_ref[...], mix_ref[...]
    weight = inward[0].astype(bf16)
    dmix = dot_nt(dout, outward[0].astype(bf16)).astype(bf16)
    dq = jnp.zeros((TOK, C), f32)
    dk = jnp.zeros((KEYS, C), f32)
    dv = jnp.zeros((KEYS, C), f32)
    for h in range(HEADS):
        chances = p_ref[h]
        wide = chances.astype(f32)
        dmix_h = head_only(dmix, h)
        dchances = dot_nt(dmix_h, v)
        dscores = wide * (dchances - jnp.sum(wide * dchances, axis=-1, keepdims=True))
        narrow = dscores.astype(bf16)
        dbias_ref[:, h * KEYS : (h + 1) * KEYS] = narrow
        dv = dv + dot_tn(chances, dmix_h)
        dq = dq + dot(narrow, head_only(key, h))
        dk = dk + dot_tn(narrow, head_only(q, h))
    dq = (dq * 32 ** (-0.5)).astype(bf16)
    dk = (dk * 32 ** (-0.5)).astype(bf16)
    dv = dv.astype(bf16)
    keyed = pad_keys(u.astype(f32)).astype(bf16)
    du = dot_nt(dq, weight[:, :C]) + unpad_keys(
        dot_nt(dk, weight[:, C : 2 * C]) + dot_nt(dv, weight[:, 2 * C :])
    )
    pair = lambda x, y: jnp.concatenate([x, y], axis=1)
    put(pack, 4 * C, pair(dot_tn(u, dq), dot_tn(keyed, dk)))
    put(pack, 5 * C, pair(dot_tn(keyed, dv), dot_tn(mix, dout)))
    small = [
        pair(colsum(dq.astype(f32)), colsum(dk.astype(f32))),
        pair(colsum(dv.astype(f32)), colsum(dout.astype(f32))),
    ]
    return du, table_adjoint(dbias_ref[...], spread, place, sort, turn_ref), small


def mlp_fwd(h, gain, shift, expand, upbias, narrow_t, downbias):
    z = dot(norm_fwd(h, gain, shift), expand) + upbias
    hidden = gelu_parts(z)[1].astype(bf16)
    return (h + dot_nt(hidden, narrow_t) + downbias).astype(bf16)


def mlp_both(h, gain, shift, expand, upbias, narrow_t, downbias, dout, want):
    normed = norm_fwd(h, gain, shift)
    z = dot(normed, expand) + upbias
    cdf, wide = gelu_parts(z)
    hidden = wide.astype(bf16)
    result = None
    if want:
        result = (h + dot_nt(hidden, narrow_t) + downbias).astype(bf16)
    slope = cdf + z * jnp.exp(-0.5 * z * z) * (1.0 / math.sqrt(2.0 * math.pi))
    dz32 = dot(dout, narrow_t) * slope
    dz = dz32.astype(bf16)
    dnormed = dot_nt(dz, expand).astype(bf16).astype(f32)
    dx, dgain, dshift = norm_bwd(h, gain, dnormed)
    dwide = dout.astype(f32)
    dh = (dwide + dx).astype(bf16)
    dexpand = dot_tn(normed, dz)
    dnarrow = dot_tn(dout, hidden)
    dense = [dexpand[:, : 2 * C], dexpand[:, 2 * C :], dnarrow[:, : 2 * C], dnarrow[:, 2 * C :]]
    dup = colsum(dz32)
    small = [
        dup[:, : 2 * C],
        dup[:, 2 * C :],
        jnp.concatenate([colsum(dwide), dgain], axis=1),
        jnp.concatenate([dshift, jnp.zeros((1, C), f32)], axis=1),
    ]
    return result, dh, dense, small


def bias_kernel(info, tables, spread, place, sort, bias_ref, turned, rows):
    make_bias(1, info, tables, spread[...], low(place), low(sort), bias_ref, turned, rows)


def first_kernel(
    info, fields, upstream, scales, offsets, inward, inbias, outward, outbias, expand, upbias, narrow, downbias,
    tables, turn, cut, spread, place, sort,
    q, k, v, p, mix, h1, pa, pb, pc, pd, bias, turned, rows,
):
    make_bias(0, info, tables, spread[...], low(place), low(sort), bias, turned, rows)
    order, route = low(turn), low(cut)
    x = dot(order, fields[...])
    u = norm_fwd(x, scales[0, 0:1], offsets[0, 0:1])
    branch = attend_fwd(0, u, inward, inbias, outward, outbias, bias, q, k, v, p, mix)
    carried = (x + branch.astype(f32)).astype(bf16)
    h1[...] = carried
    out = mlp_fwd(
        carried.astype(f32), scales[0, 1:2], offsets[0, 1:2], expand[0].astype(bf16), upbias[0:1],
        narrow[0].astype(bf16), downbias[0:1],
    )
    cotangent = dot(order, upstream[...]).astype(bf16)
    write_pieces(dot(route, out), dot(route, cotangent), (pa, pb, pc, pd))


def second_kernel(
    qa, qb, qc, qd, scales, offsets, inward, inbias, outward, outbias, expand, upbias, narrow, downbias,
    bias, join, spread, place, sort,
    pack, pa, pb, pc, pd, q, k, v, p, mix, dbias, turned,
):
    route = low(join)
    pieces = (qa, qb, qc, qd)
    y1 = dot(route, join_rows(pieces, 0))
    cotangent = dot(route, join_rows(pieces, 1)).astype(bf16)
    u = norm_fwd(y1, scales[1, 0:1], offsets[1, 0:1])
    branch = attend_fwd(1, u, inward, inbias, outward, outbias, bias, q, k, v, p, mix)
    h2 = (y1 + branch.astype(f32)).astype(bf16).astype(f32)
    out, dh, dense, short = mlp_both(
        h2, scales[1, 1:2], offsets[1, 1:2], expand[0].astype(bf16), upbias[1:2],
        narrow[0].astype(bf16), downbias[1:2], cotangent, True,
    )
    for i, part in enumerate(dense):
        put(pack, i * C, part)
    du, table, small = attend_bwd(
        dh, u, inward, outward, spread[...], low(place), low(sort), q, k, v, p, mix, pack, dbias, turned
    )
    dx, dgain, dshift = norm_bwd(y1, scales[1, 0:1], du.astype(bf16).astype(f32))
    dy1 = (dh.astype(f32) + dx.astype(bf16).astype(f32)).astype(bf16)
    put_rest(pack, table, short + small + [jnp.concatenate([dgain, dshift], axis=1)])
    write_pieces(dot_tn(route, dy1), dot_tn(route, out), (pa, pb, pc, pd))


def first_back_kernel(
    qa, qb, qc, qd, fields, h1, scales, offsets, inward, outward, expand, upbias, narrow, downbias,
    q, k, v, p, mix, turn, cut, spread, place, sort,
    result, adjoint, pack, dbias, turned,
):
    order, route = low(turn), low(cut)
    pieces = (qa, qb, qc, qd)
    result[...] = dot_tn(order, dot_tn(route, join_rows(pieces, 1)).astype(bf16)).astype(bf16)
    dy1 = dot_tn(route, join_rows(pieces, 0)).astype(bf16)
    _, dh1, dense, short = mlp_both(
        h1[...].astype(f32), scales[0, 1:2], offsets[0, 1:2], expand[0].astype(bf16), upbias[0:1],
        narrow[0].astype(bf16), downbias[0:1], dy1, False,
    )
    for i, part in enumerate(dense):
        put(pack, i * C, part)
    x = dot(order, fields[...])
    u = norm_fwd(x, scales[0, 0:1], offsets[0, 0:1])
    du, table, small = attend_bwd(
        dh1, u, inward, outward, spread[...], low(place), low(sort), q, k, v, p, mix, pack, dbias, turned
    )
    dx0, dgain0, dshift0 = norm_bwd(x, scales[0, 0:1], du.astype(bf16).astype(f32))
    adjoint[...] = dot_tn(order, (dh1.astype(f32) + dx0).astype(bf16)).astype(bf16)
    put_rest(pack, table, short + small + [jnp.concatenate([dgain0, dshift0], axis=1)])


def core_kernel(info, first, second, got_first, got_second, a, b, c, d, own, got, sems):
    for core, sources in ((0, (first, got_first)), (1, (second, got_second))):

        @pl.when(info[1] == core)
        def _(sources=sources):
            copies = [pltpu.make_async_copy(m, n, sems.at[i]) for i, (m, n) in enumerate(zip(sources, (own, got)))]
            for copy in copies:
                copy.start()
            for copy in copies:
                copy.wait()

    for n, out in enumerate((a, b, c, d)):
        at = (info[3] ^ n) * 2
        out[...] = (own[pl.ds(at, 2)].astype(f32) + got[pl.ds(at, 2)].astype(f32)).astype(bf16)


def samples_kernel(info, a, b, c, d, keep, send):
    for out, at in ((keep, info[2]), (send, info[2] ^ 1)):
        total = a[at].astype(f32) + b[at].astype(f32) + c[at].astype(f32) + d[at].astype(f32)
        out[...] = total.astype(bf16)


def pair_kernel(a, b, out):
    out[...] = (a[...].astype(f32) + b[...].astype(f32)).astype(bf16)


def band_kernel(a, b, c, d, out):
    four = [ref[...].astype(f32) for ref in (a, b, c, d)]
    total = four[0] + four[1] + four[2] + four[3]
    out[:ROWS] = total[:ROWS].astype(bf16)
    if a.shape[0] == CHUNK:
        aside = jnp.concatenate([total[ROWS + 8 :], jnp.zeros((8, 2 * C), f32)], axis=0)
        out[ROWS:CHUNK] = aside.astype(bf16)
        out[CHUNK:] = jnp.concatenate([m[ROWS : ROWS + 8] for m in four], axis=0).astype(bf16)
    else:
        out[ROWS:CHUNK] = total[ROWS:CHUNK].astype(bf16)
        for i, ref in enumerate((a, b, c, d)):
            out[CHUNK + 32 * i : CHUNK + 32 * i + 32] = ref[CHUNK:]


def final_kernel(
    info, own, got,
    scales, offsets, inward, inbias, outward, outbias, expand, upbias, narrow, downbias, tables, dense, *, factor
):
    def routes(k):
        lane = lax.broadcasted_iota(jnp.int32, (1, 128), 1)
        kind = jnp.zeros((1, 128), jnp.int32)
        for e in range(16):
            kind = kind + jnp.where((lane >> 3) == e, kind_of(info, k, info[0] ^ e), 0)
        row = lax.broadcasted_iota(jnp.int32, (96, 128), 0)
        part = lax.broadcasted_iota(jnp.int32, (96, 128), 1) & 7
        head, match = row >> 4, (row & 15) == kind
        made = [match & (part == head)]
        for i in range(3):
            made.append(match & ((head >> 1) == i) & (part == 6 + (head & 1)))
        return [jnp.where(m, 1.0, 0.0).astype(bf16) for m in made]

    def unpack(k, ref):
        route = routes(k)
        left = None
        small = []
        for chunk in range(8):
            at = (info[3] ^ (chunk // 2), info[2] ^ (chunk % 2))
            dense[chunk * ROWS : (chunk + 1) * ROWS] = ref[at[0], at[1], :ROWS]
            small.append(ref[at[0], at[1], ROWS:CHUNK].astype(f32)[0:1] * factor)
            here = ref[at[0], at[1], CHUNK:]
            rows = dot(route[0], here) * factor
            for h in range(HEADS):
                tables[k, h, :, 384 * chunk : 384 * chunk + 384] = rows[16 * h : 16 * h + 16]
            if chunk < 2:
                left = sum(dot(route[1 + i], here[:, 128 * i : 128 * i + 128]) for i in range(3)) * factor
                start = 3072 + 128 * chunk
                size = min(128, REL - start)
                for h in range(HEADS):
                    tables[k, h, :, start : start + size] = left[16 * h : 16 * h + 16, :size]
        load = lambda i: dense[i * C : (i + 1) * C].astype(f32) * factor
        expand[k, :, : 2 * C] = load(0)
        expand[k, :, 2 * C :] = load(1)
        narrow[k, :, : 2 * C] = load(2)
        narrow[k, :, 2 * C :] = load(3)
        inward[k, :, : 2 * C] = load(4)
        both = load(5)
        inward[k, :, 2 * C :] = both[:, :C]
        outward[k] = both[:, C:]
        upbias[k : k + 1, : 2 * C] = small[0]
        upbias[k : k + 1, 2 * C :] = small[1]
        downbias[k : k + 1] = small[2][:, :C]
        scales[k, 1:2] = small[2][:, C:]
        offsets[k, 1:2] = small[3][:, :C]
        inbias[k : k + 1, : 2 * C] = small[4]
        inbias[k : k + 1, 2 * C :] = small[5][:, :C]
        outbias[k : k + 1] = small[5][:, C:]
        scales[k, 0:1] = small[6][:, :C]
        offsets[k, 0:1] = small[6][:, C:]

    @pl.when(info[1] == 0)
    def _():
        unpack(0, own)
        unpack(1, got)

    @pl.when(info[1] != 0)
    def _():
        unpack(0, got)
        unpack(1, own)


def call(kernel, ins, outs, scratch=(), far_outs=0, limit=VMEM):
    specs, fetched, slots = [], [], []
    for array, block, far in ins:
        dims = array.ndim
        shape = array.shape if block in (None, "smem", "raw") else (1,) + array.shape[1:]
        if block == "smem":
            specs.append(pl.BlockSpec(memory_space=pltpu.SMEM))
        elif block == "raw":
            specs.append(pl.BlockSpec(memory_space=pltpu.HBM))
        elif far:
            specs.append(pl.BlockSpec(memory_space=pltpu.HBM))
            fetched.append((len(specs) - 1, block))
            slots.append(pltpu.VMEM(shape, array.dtype))
        else:
            specs.append(pl.BlockSpec(array.shape, lambda i, dims=dims: (0,) * dims))
    out_specs = []
    for i, o in enumerate(outs):
        if i < far_outs:
            out_specs.append(pl.BlockSpec(memory_space=pltpu.HBM))
            slots.append(pltpu.VMEM(o.shape, o.dtype))
        else:
            out_specs.append(pl.BlockSpec(o.shape, lambda i, dims=len(o.shape): (0,) * dims))

    def wrapped(*refs):
        in_refs, refs = list(refs[: len(ins)]), refs[len(ins) :]
        out_refs, refs = list(refs[: len(outs)]), refs[len(outs) :]
        own, refs = refs[: len(scratch)], refs[len(scratch) :]
        copies = []
        for n, (at, block) in enumerate(fetched):
            source = in_refs[at] if block is None else in_refs[at].at[block : block + 1]
            copies.append(pltpu.make_async_copy(source, refs[n], refs[-1].at[n]))
            in_refs[at] = refs[n]
        for copy in copies:
            copy.start()
        for copy in copies:
            copy.wait()
        targets = out_refs[:far_outs]
        out_refs[:far_outs] = refs[len(fetched) : len(fetched) + far_outs]
        kernel(*in_refs, *out_refs, *own)
        copies = [
            pltpu.make_async_copy(out_refs[n], targets[n], refs[-1].at[len(fetched) + n]) for n in range(far_outs)
        ]
        for copy in copies:
            copy.start()
        for copy in copies:
            copy.wait()

    size = lambda s: math.prod(s.shape) * jnp.dtype(s.dtype).itemsize
    moved = sum(size(o) for o in outs) + sum(size(a) for a, b, _ in ins)
    if slots:
        slots.append(pltpu.SemaphoreType.DMA((len(slots),)))
    return pl.pallas_call(
        wrapped,
        grid=(1,),
        in_specs=specs,
        out_specs=out_specs,
        out_shape=outs,
        scratch_shapes=list(scratch) + slots,
        compiler_params=pltpu.CompilerParams(vmem_limit_bytes=limit),
        cost_estimate=pl.CostEstimate(flops=10**9, bytes_accessed=moved, transcendentals=0),
    )(*[array for array, _, _ in ins])


def send_pieces(pieces, step):
    lat, lon = lax.axis_size("lat"), lax.axis_size("lon")
    rows = [(i, (i + step) % lat) for i in range(lat)]
    cols = [(i, (i + step) % lon) for i in range(lon)]
    both = [(i * lon + j, (i + step) % lat * lon + (j + step) % lon) for i in range(lat) for j in range(lon)]
    return (
        pieces[0],
        lax.ppermute(pieces[1], "lat", rows),
        lax.ppermute(pieces[2], "lon", cols),
        lax.ppermute(pieces[3], ("lat", "lon"), both),
    )


def swap(array, axis, distance, only=None):
    devices = range(lax.axis_size(axis))
    return lax.ppermute(array, axis, [(i, i ^ distance) for i in devices if only is None or i % 2 == only])


def body(
    fields, upstream, scales, offsets, inward, inbias, outward, outbias, expand, upbias, narrow, downbias,
    tables, window_type, row_valid,
):
    lon = lax.axis_index("lon")
    place = jnp.stack([lax.axis_index("lat"), lon % 2, lon // 2, lax.axis_index("rep")]).astype(jnp.int32)
    info = jnp.concatenate([place, window_type[0, 0], window_type[1, 0], row_valid])
    const = constants()
    levels, row_count, col_count = fields.shape[1:4]
    total_rows = row_valid.shape[0]
    x = fields[0].transpose(1, 2, 0, 3).reshape(TOK, C)
    cotangent = upstream[0].transpose(1, 2, 0, 3).reshape(TOK, C)
    narrow = jnp.swapaxes(narrow, 1, 2)
    tables = jnp.swapaxes(tables, 1, 2)
    of = jax.ShapeDtypeStruct
    piece = [of((2 * QUAD, C), bf16)] * 4
    token = of((TOK, C), bf16)
    state = [token, of((KEYS, C), bf16), of((KEYS, C), bf16), of((HEADS, TOK, KEYS), bf16), token]
    pack = of((8, CHUNK, 2 * C), bf16)
    turned = pltpu.VMEM((192, 1536), bf16)
    dbias = pltpu.VMEM((TOK, 1536), bf16)
    rows = pltpu.VMEM((8, 3456), f32)
    near = lambda *arrays: [(m, None, False) for m in arrays]
    far = lambda *arrays: [(m, None, True) for m in arrays]
    block = lambda k, *arrays: [(m, k, True) for m in arrays]
    raw = lambda *arrays: [(m, "raw", True) for m in arrays]
    fixed = lambda *names: far(*[const[name] for name in names])
    scalars = [(info, "smem", False)]

    def weights(k):
        return (
            far(scales, offsets) + block(k, inward) + far(inbias) + block(k, outward) + far(outbias)
            + block(k, expand) + far(upbias) + block(k, narrow) + far(downbias)
        )

    *state0, h1, pa, pb, pc, pd = call(
        first_kernel,
        scalars + far(x, cotangent) + weights(0) + block(0, tables) + fixed("turn", "cut", "spread", "place", "sort"),
        state + [token] + piece,
        (pltpu.VMEM((TOK, 1536), f32), turned, rows),
        6,
    )
    pieces = send_pieces((pa, pb, pc, pd), -1)
    (bias1,) = call(
        bias_kernel,
        scalars + block(1, tables) + fixed("spread", "place", "sort"),
        [of((TOK, 1536), f32)],
        (turned, rows),
    )
    pack1, *pieces = call(
        second_kernel,
        far(*pieces) + weights(1) + far(bias1) + fixed("join", "spread", "place", "sort"),
        [pack] + piece,
        [pltpu.VMEM(m.shape, m.dtype) for m in state] + [dbias, turned],
    )
    pieces = send_pieces(pieces, 1)
    got1 = swap(pack1, "lon", 1, 0)
    result, adjoint, pack0 = call(
        first_back_kernel,
        far(*pieces, x, h1, scales, offsets) + block(0, inward, outward, expand) + far(upbias)
        + block(0, narrow) + far(downbias, *state0) + fixed("turn", "cut", "spread", "place", "sort"),
        [token, token, pack],
        (dbias, turned),
    )
    got0 = swap(pack0, "lon", 1, 1)

    part = of((2, CHUNK, 2 * C), bf16)
    a, b, c, d = call(
        core_kernel,
        scalars + raw(pack0, pack1, got0, got1),
        [part] * 4,
        [pltpu.VMEM(pack.shape, bf16)] * 2 + [pltpu.SemaphoreType.DMA((2,))],
    )
    b, c, d = (swap(m, "rep", i + 1) for i, m in enumerate((b, c, d)))
    chunk = of((CHUNK, 2 * C), bf16)
    keep, give = call(samples_kernel, scalars + near(a, b, c, d), [chunk, chunk], limit=SMALL)
    (a,) = call(pair_kernel, near(keep, swap(give, "lon", 2)), [chunk], limit=SMALL)
    for step, height in ((1, CHUNK + 32), (4, CHUNK + 128)):
        others = [swap(a, "lat", step * i) for i in (1, 2, 3)]
        (a,) = call(band_kernel, near(a, *others), [of((height, 2 * C), bf16)], limit=SMALL)
    a = jnp.stack([a, swap(a, "lon", 2)])
    a = jnp.stack([a] + [swap(a, "rep", i) for i in (1, 2, 3)])
    got = swap(a, "lon", 1)

    factor = 1.0 / math.sqrt(lax.axis_size("rep") * levels * total_rows * col_count * lax.axis_size("lon"))

    def finish(*refs):
        final_kernel(*refs, factor=factor)

    outs = [
        (2, 2, C), (2, 2, C), (2, C, 3 * C), (2, 3 * C), (2, C, C), (2, C), (2, C, FFN), (2, FFN), (2, C, FFN),
        (2, C), tables.shape,
    ]
    joined = list(
        call(
            finish,
            scalars + near(a, got),
            [of(s, f32) for s in outs],
            (pltpu.VMEM((8 * ROWS, 2 * C), bf16),),
            limit=2 * SMALL,
        )
    )
    joined[8] = jnp.swapaxes(joined[8], 1, 2)
    joined[10] = jnp.swapaxes(joined[10], 1, 2)
    back = lambda m: m.reshape(row_count, col_count, levels, C).transpose(2, 0, 1, 3)[None]
    return (back(result), back(adjoint), *joined)


def solution(mesh):
    grid = P("rep", None, "lat", "lon", None)
    return jax.shard_map(
        body, mesh=mesh, in_specs=(grid, grid) + (P(),) * 13, out_specs=(grid, grid) + (P(),) * 11, check_vma=False
    )
```

```python
import functools
import math

import jax
import jax.numpy as jnp
import numpy as np
from jax import lax
from jax.experimental import pallas as pl
from jax.experimental.pallas import tpu as pltpu
from jax.sharding import PartitionSpec as P

C = 192
HEADS = 6
FFN = 768
TOK = 144
KEYS = 256
QUAD = 48
REL = 3312
ROWS = 144
CHUNK = ROWS + 16
epsilon = 1e-05
masked = -1000000000.0
f32 = jnp.float32
bf16 = jnp.bfloat16
VMEM = 64 * 1024 * 1024
SMALL = 16 * 1024 * 1024


def constants():
    tok = np.arange(TOK)
    a, r, c = tok // 72, tok // 12 % 6, tok % 12
    turn = np.zeros((TOK, TOK), np.float32)
    turn[tok, (r * 12 + c) * 2 + a] = 1
    quad = np.where(r >= 3, 0, 1) + np.where(c >= 6, 0, 2)
    cut = np.zeros((4 * QUAD, TOK), np.float32)
    cut[quad * QUAD + a * 18 + r % 3 * 6 + c % 6, tok] = 1
    quad = np.where(r < 3, 0, 1) + np.where(c < 6, 0, 2)
    join = np.zeros((TOK, 4 * QUAD), np.float32)
    join[tok, quad * QUAD + (1 - a) * 18 + r % 3 * 6 + c % 6] = 1
    spread = np.zeros((256, 12 * 128), np.float32)
    for ci in range(12):
        for rj in range(6):
            for cj in range(12):
                spread[rj * 23 + ci - cj + 11, ci * 128 + rj * 12 + cj] = 1
    place = np.zeros((TOK, 192), np.float32)
    place[tok, c * 16 + a * 6 + r] = 1
    sort = np.zeros((192, 192), np.float32)
    for ai in range(2):
        for aj in range(2):
            for ri in range(6):
                for h in range(HEADS):
                    sort[(h * 2 + aj) * 16 + ai * 6 + ri, ((ai * 2 + aj) * 6 + ri) * 8 + h] = 1
    made = {"turn": turn, "cut": cut, "join": join, "place": place, "sort": sort}
    made = {name: jnp.asarray(m, f32) for name, m in made.items()}
    made["spread"] = jnp.asarray(spread, bf16)
    return made


def low(ref):
    return ref[...].astype(bf16)


def dot(x, y, dims=((1,), (0,))):
    return lax.dot_general(x, y, (dims, ((), ())), preferred_element_type=f32)


def dot_nt(x, y):
    return dot(x, y, ((1,), (1,)))


def dot_tn(x, y):
    return dot(x, y, ((0,), (0,)))


def norm_parts(values):
    centred = values - jnp.mean(values, axis=-1, keepdims=True)
    rstd = lax.rsqrt(jnp.mean(centred * centred, axis=-1, keepdims=True) + epsilon)
    return centred * rstd, rstd


def norm_fwd(values, gain, shift):
    return (norm_parts(values)[0] * gain + shift).astype(bf16)


def norm_bwd(values, gain, dy):
    hat, rstd = norm_parts(values)
    dhat = dy * gain
    first = jnp.mean(dhat, axis=-1, keepdims=True)
    second = jnp.mean(dhat * hat, axis=-1, keepdims=True)
    return rstd * (dhat - first - hat * second), colsum(dy * hat), colsum(dy)


def colsum(x):
    return jnp.sum(x, axis=0, keepdims=True)


def erf(x):
    return lax.erf(x)


def gelu_parts(z):
    cdf = 0.5 * (1.0 + erf(z * (2.0 ** -0.5)))
    return cdf, z * cdf


def pad_keys(x):
    blank = jnp.zeros((56, x.shape[1]), f32)
    return jnp.concatenate([x[:72], blank, x[72:], blank], axis=0)


def unpad_keys(x):
    return jnp.concatenate([x[:72], x[128:200]], axis=0)


def head_only(x, h):
    lane = lax.broadcasted_iota(jnp.int32, x.shape, 1)
    return jnp.where((lane >= 32 * h) & (lane < 32 * h + 32), x.astype(f32), 0.0).astype(bf16)


def join_rows(refs, part):
    return jnp.concatenate([ref[part * QUAD : (part + 1) * QUAD] for ref in refs], axis=0)


def write_pieces(first, second, refs):
    for i, ref in enumerate(refs):
        ref[:QUAD] = first[i * QUAD : (i + 1) * QUAD].astype(bf16)
        ref[QUAD:] = second[i * QUAD : (i + 1) * QUAD].astype(bf16)


def place_of():
    lon = lax.axis_index("lon")
    return lax.axis_index("lat"), lon & 1, lon >> 1, lax.axis_index("rep")


def key_mask(valid, band, shift):
    lane = lax.broadcasted_iota(jnp.int32, (1, KEYS), 1)
    column = lane & 127
    total_rows = valid.shape[0]
    last = jnp.where(band == total_rows // 6 - 1, 1, 0)
    allowed = jnp.zeros((1, KEYS), jnp.int32)
    for r in range(6):
        at = band * 6 + r + shift
        at = jnp.where(at >= total_rows, at - total_rows, at)
        hit = (column >= 12 * r) & (column < 12 * r + 12)
        allowed = allowed + jnp.where(hit, valid[at], 0)
    if shift:
        row = lax.broadcasted_iota(jnp.int32, (TOK, KEYS), 0)
        wide = lax.broadcasted_iota(jnp.int32, (TOK, KEYS), 1)
        row_level = jnp.where(row >= 72, 1, 0)
        key_level = wide >> 7
        row_part = jnp.where(row - 72 * row_level >= 36, 1, 0)
        key_part = jnp.where((wide & 127) >= 36, 1, 0)
        apart = (row_level ^ key_level) | ((row_part ^ key_part) & last)
        allowed = jnp.where(apart == 0, jnp.broadcast_to(allowed, (TOK, KEYS)), 0)
        column = wide & 127
    mask = jnp.where(allowed > 0, 0.0, masked)
    return jnp.where(column < 72, mask, 2 * masked)


def make_bias(k, types, valid, tables, spread, place, sort, bias_ref, turn_ref, row_ref):
    row_ref[...] = jnp.zeros(row_ref.shape, f32)
    band = place_of()[0]
    kind = types[k, 0, band]
    for h in range(HEADS):
        row_ref[h : h + 1, :REL] = tables[0, h, pl.ds(kind, 1), :]
    wide_rows = row_ref[...]
    rest = jnp.concatenate([wide_rows[:, 138 * i : 138 * i + 256] for i in range(24)], axis=0)
    total = None
    for _ in range(3):
        part = rest.astype(bf16)
        rest = rest - part.astype(f32)
        wide = dot(dot(sort, part).astype(bf16), spread)
        for g in range(12):
            for ci in range(12):
                turn_ref[ci * 16 : ci * 16 + 16, g * 128 : g * 128 + 128] = wide[
                    g * 16 : g * 16 + 16, ci * 128 : ci * 128 + 128
                ].astype(bf16)
        here = dot(place, turn_ref[...])
        total = here if total is None else total + here
    mask = key_mask(valid, band, 3 * k)
    for h in range(HEADS):
        bias_ref[:, h * KEYS : (h + 1) * KEYS] = total[:, h * KEYS : (h + 1) * KEYS] + mask


def table_adjoint(dbias, spread, place, sort, turn_ref):
    rows = dot_tn(place, dbias)
    for g in range(12):
        for ci in range(12):
            turn_ref[g * 16 : g * 16 + 16, ci * 128 : ci * 128 + 128] = rows[
                ci * 16 : ci * 16 + 16, g * 128 : g * 128 + 128
            ].astype(bf16)
    narrow = dot_nt(turn_ref[...], spread).astype(bf16)
    rows = dot_tn(sort, narrow)
    pieces = [rows[8 * i : 8 * i + 8, :138] for i in range(24)]
    return jnp.concatenate(pieces + [jnp.zeros((8, 16), f32)], axis=1)


def put(pack, at, value):
    done = 0
    while done < value.shape[0]:
        chunk, row = divmod(at + done, ROWS)
        size = min(ROWS - row, value.shape[0] - done)
        pack[chunk, row : row + size] = value[done : done + size].astype(bf16)
        done += size


def put_rest(pack, table, small):
    row = lax.broadcasted_iota(jnp.int32, (8, 2 * C), 0)
    for chunk in range(8):
        own = table[:, 384 * chunk : 384 * chunk + 384]
        if chunk < 2:
            left = table[:, 3072 + 128 * chunk : 3200 + 128 * chunk]
            moved = [pltpu.roll(left, 6 - 2 * i, 0) if i < 3 else left for i in range(3)]
            own = jnp.where(row >= 6, jnp.concatenate(moved, axis=1), own)
        short = jnp.where(row == 0, small[chunk], 0.0) if chunk < len(small) else jnp.zeros((8, 2 * C), f32)
        pack[chunk, ROWS : ROWS + 16] = jnp.concatenate([own, short], axis=0).astype(bf16)


def attend_fwd(k, u, inward, inbias, outward, outbias, bias_ref, q_ref, k_ref, v_ref, p_ref, mix_ref):
    weight = inward[0].astype(bf16)
    shift = inbias[k : k + 1]
    keyed = pad_keys(u.astype(f32)).astype(bf16)
    q = (dot(u, weight[:, :C]) + shift[:, :C]).astype(bf16)
    key = (dot(keyed, weight[:, C : 2 * C]) + shift[:, C : 2 * C]).astype(bf16)
    v = (dot(keyed, weight[:, 2 * C :]) + shift[:, 2 * C :]).astype(bf16)
    q_ref[...] = q
    k_ref[...] = key
    v_ref[...] = v
    mix = jnp.zeros((TOK, C), f32)
    for h in range(HEADS):
        scores = dot_nt(head_only(q, h), key) * 32 ** (-0.5) + bias_ref[:, h * KEYS : (h + 1) * KEYS]
        weights = jnp.exp(scores - jnp.max(scores, axis=-1, keepdims=True))
        chances = (weights / jnp.sum(weights, axis=-1, keepdims=True)).astype(bf16)
        p_ref[h] = chances
        mix = mix + dot(chances, head_only(v, h))
    mix = mix.astype(bf16)
    mix_ref[...] = mix
    return (dot(mix, outward[0].astype(bf16)) + outbias[k : k + 1]).astype(bf16)


def attend_bwd(dout, u, inward, outward, spread, place, sort, q_ref, k_ref, v_ref, p_ref, mix_ref, pack, dbias_ref, turn_ref):
    q, key, v, mix = q_ref[...], k_ref[...], v_ref[...], mix_ref[...]
    weight = inward[0].astype(bf16)
    dmix = dot_nt(dout, outward[0].astype(bf16)).astype(bf16)
    dq = jnp.zeros((TOK, C), f32)
    dk = jnp.zeros((KEYS, C), f32)
    dv = jnp.zeros((KEYS, C), f32)
    for h in range(HEADS):
        chances = p_ref[h]
        wide = chances.astype(f32)
        dmix_h = head_only(dmix, h)
        dchances = dot_nt(dmix_h, v)
        dscores = wide * (dchances - jnp.sum(wide * dchances, axis=-1, keepdims=True))
        narrow = dscores.astype(bf16)
        dbias_ref[:, h * KEYS : (h + 1) * KEYS] = narrow
        dv = dv + dot_tn(chances, dmix_h)
        dq = dq + dot(narrow, head_only(key, h))
        dk = dk + dot_tn(narrow, head_only(q, h))
    dq = (dq * 32 ** (-0.5)).astype(bf16)
    dk = (dk * 32 ** (-0.5)).astype(bf16)
    dv = dv.astype(bf16)
    keyed = pad_keys(u.astype(f32)).astype(bf16)
    du = dot_nt(dq, weight[:, :C]) + unpad_keys(
        dot_nt(dk, weight[:, C : 2 * C]) + dot_nt(dv, weight[:, 2 * C :])
    )
    pair = lambda x, y: jnp.concatenate([x, y], axis=1)
    put(pack, 4 * C, pair(dot_tn(u, dq), dot_tn(keyed, dk)))
    put(pack, 5 * C, pair(dot_tn(keyed, dv), dot_tn(mix, dout)))
    small = [
        pair(colsum(dq.astype(f32)), colsum(dk.astype(f32))),
        pair(colsum(dv.astype(f32)), colsum(dout.astype(f32))),
    ]
    return du, table_adjoint(dbias_ref[...], spread, place, sort, turn_ref), small


def mlp_fwd(h, gain, shift, expand, upbias, narrow_t, downbias):
    z = dot(norm_fwd(h, gain, shift), expand) + upbias
    hidden = gelu_parts(z)[1].astype(bf16)
    return (h + dot_nt(hidden, narrow_t) + downbias).astype(bf16)


def mlp_both(h, gain, shift, expand, upbias, narrow_t, downbias, dout, want):
    normed = norm_fwd(h, gain, shift)
    z = dot(normed, expand) + upbias
    cdf, wide = gelu_parts(z)
    hidden = wide.astype(bf16)
    result = None
    if want:
        result = (h + dot_nt(hidden, narrow_t) + downbias).astype(bf16)
    slope = cdf + z * jnp.exp(-0.5 * z * z) * (1.0 / math.sqrt(2.0 * math.pi))
    dz32 = dot(dout, narrow_t) * slope
    dz = dz32.astype(bf16)
    dnormed = dot_nt(dz, expand).astype(bf16).astype(f32)
    dx, dgain, dshift = norm_bwd(h, gain, dnormed)
    dwide = dout.astype(f32)
    dh = (dwide + dx).astype(bf16)
    dexpand = dot_tn(normed, dz)
    dnarrow = dot_tn(dout, hidden)
    dense = [dexpand[:, : 2 * C], dexpand[:, 2 * C :], dnarrow[:, : 2 * C], dnarrow[:, 2 * C :]]
    dup = colsum(dz32)
    small = [
        dup[:, : 2 * C],
        dup[:, 2 * C :],
        jnp.concatenate([colsum(dwide), dgain], axis=1),
        jnp.concatenate([dshift, jnp.zeros((1, C), f32)], axis=1),
    ]
    return result, dh, dense, small


def bias_kernel(types, valid, tables, spread, place, sort, bias_ref, turned, rows):
    make_bias(1, types, valid, tables, spread[...], low(place), low(sort), bias_ref, turned, rows)


def first_kernel(
    types, valid, fields, upstream, scales, offsets, inward, inbias, outward, outbias, expand, upbias, narrow, downbias,
    tables, turn, cut, spread, place, sort,
    q, k, v, p, mix, h1, pa, pb, pc, pd, bias, turned, rows,
):
    make_bias(0, types, valid, tables, spread[...], low(place), low(sort), bias, turned, rows)
    order, route = low(turn), low(cut)
    x = dot(order, fields[...])
    u = norm_fwd(x, scales[0, 0:1], offsets[0, 0:1])
    branch = attend_fwd(0, u, inward, inbias, outward, outbias, bias, q, k, v, p, mix)
    carried = (x + branch.astype(f32)).astype(bf16)
    h1[...] = carried
    out = mlp_fwd(
        carried.astype(f32), scales[0, 1:2], offsets[0, 1:2], expand[0].astype(bf16), upbias[0:1],
        narrow[0].astype(bf16), downbias[0:1],
    )
    cotangent = dot(order, upstream[...]).astype(bf16)
    write_pieces(dot(route, out), dot(route, cotangent), (pa, pb, pc, pd))


def second_kernel(
    qa, qb, qc, qd, scales, offsets, inward, inbias, outward, outbias, expand, upbias, narrow, downbias,
    bias, join, spread, place, sort,
    pack, pa, pb, pc, pd, q, k, v, p, mix, dbias, turned,
):
    route = low(join)
    pieces = (qa, qb, qc, qd)
    y1 = dot(route, join_rows(pieces, 0))
    cotangent = dot(route, join_rows(pieces, 1)).astype(bf16)
    u = norm_fwd(y1, scales[1, 0:1], offsets[1, 0:1])
    branch = attend_fwd(1, u, inward, inbias, outward, outbias, bias, q, k, v, p, mix)
    h2 = (y1 + branch.astype(f32)).astype(bf16).astype(f32)
    out, dh, dense, short = mlp_both(
        h2, scales[1, 1:2], offsets[1, 1:2], expand[0].astype(bf16), upbias[1:2],
        narrow[0].astype(bf16), downbias[1:2], cotangent, True,
    )
    for i, part in enumerate(dense):
        put(pack, i * C, part)
    du, table, small = attend_bwd(
        dh, u, inward, outward, spread[...], low(place), low(sort), q, k, v, p, mix, pack, dbias, turned
    )
    dx, dgain, dshift = norm_bwd(y1, scales[1, 0:1], du.astype(bf16).astype(f32))
    dy1 = (dh.astype(f32) + dx.astype(bf16).astype(f32)).astype(bf16)
    put_rest(pack, table, short + small + [jnp.concatenate([dgain, dshift], axis=1)])
    write_pieces(dot_tn(route, dy1), dot_tn(route, out), (pa, pb, pc, pd))


def first_back_kernel(
    qa, qb, qc, qd, fields, h1, scales, offsets, inward, outward, expand, upbias, narrow, downbias,
    q, k, v, p, mix, turn, cut, spread, place, sort,
    result, adjoint, pack, dbias, turned,
):
    order, route = low(turn), low(cut)
    pieces = (qa, qb, qc, qd)
    result[...] = dot_tn(order, dot_tn(route, join_rows(pieces, 1)).astype(bf16)).astype(bf16)
    dy1 = dot_tn(route, join_rows(pieces, 0)).astype(bf16)
    _, dh1, dense, short = mlp_both(
        h1[...].astype(f32), scales[0, 1:2], offsets[0, 1:2], expand[0].astype(bf16), upbias[0:1],
        narrow[0].astype(bf16), downbias[0:1], dy1, False,
    )
    for i, part in enumerate(dense):
        put(pack, i * C, part)
    x = dot(order, fields[...])
    u = norm_fwd(x, scales[0, 0:1], offsets[0, 0:1])
    du, table, small = attend_bwd(
        dh1, u, inward, outward, spread[...], low(place), low(sort), q, k, v, p, mix, pack, dbias, turned
    )
    dx0, dgain0, dshift0 = norm_bwd(x, scales[0, 0:1], du.astype(bf16).astype(f32))
    adjoint[...] = dot_tn(order, (dh1.astype(f32) + dx0).astype(bf16)).astype(bf16)
    put_rest(pack, table, short + small + [jnp.concatenate([dgain0, dshift0], axis=1)])


def core_kernel(first, second, got_first, got_second, *refs):
    outs, (own, got, made, sems) = refs[:8], refs[8:]
    _, core, side, rep = place_of()
    part = lambda n: pl.ds((rep ^ (n // 2)) * 2 + (side ^ (n % 2)), 1)
    order = (4, 5, 2, 3, 6, 7, 1, 0)
    for k, (mine, theirs) in enumerate(((first, got_first), (second, got_second))):

        @pl.when(core == k)
        def _(mine=mine, theirs=theirs):
            for n in order:
                pltpu.make_async_copy(mine.at[part(n)], own.at[n], sems.at[n]).start()
                pltpu.make_async_copy(theirs.at[part(n)], got.at[n], sems.at[8 + n]).start()

    sent = []
    for n in order:
        pltpu.make_async_copy(first.at[part(n)], own.at[n], sems.at[n]).wait()
        pltpu.make_async_copy(got_first.at[part(n)], got.at[n], sems.at[8 + n]).wait()
        made[n] = (own[n].astype(f32) + got[n].astype(f32)).astype(bf16)
        sent.append(pltpu.make_async_copy(made.at[n], outs[n], sems.at[16 + n]))
        sent[-1].start()
    for copy in sent:
        copy.wait()


def add_kernel(*refs):
    total = refs[0][0].astype(f32)
    for ref in refs[1:-1]:
        total = total + ref[0].astype(f32)
    refs[-1][...] = total.astype(bf16)


def band_kernel(a, b, c, d, out):
    four = [ref[...].astype(f32) for ref in (a, b, c, d)]
    total = four[0] + four[1] + four[2] + four[3]
    out[:ROWS] = total[:ROWS].astype(bf16)
    if a.shape[0] == CHUNK:
        aside = jnp.concatenate([total[ROWS + 8 :], jnp.zeros((8, 2 * C), f32)], axis=0)
        out[ROWS:CHUNK] = aside.astype(bf16)
        out[CHUNK:] = jnp.concatenate([m[ROWS : ROWS + 8] for m in four], axis=0).astype(bf16)
    else:
        out[ROWS:CHUNK] = total[ROWS:CHUNK].astype(bf16)
        for i, ref in enumerate((a, b, c, d)):
            out[CHUNK + 32 * i : CHUNK + 32 * i + 32] = ref[CHUNK:]


def final_kernel(factor, types, own, got, *refs):
    big, short = refs[:5], refs[5:11]
    inward, outward, expand, narrow, tables, dense, sems = refs[11:]
    scales, offsets, inbias, outbias, upbias, downbias = short
    band, core, side, rep = place_of()
    lane = lax.broadcasted_iota(jnp.int32, (1, 128), 1)
    row = lax.broadcasted_iota(jnp.int32, (96, 128), 0)
    part = lax.broadcasted_iota(jnp.int32, (96, 128), 1) & 7
    head = row >> 4

    def unpack(k, ref):
        kind = jnp.zeros((1, 128), jnp.int32)
        for e in range(16):
            kind = kind + jnp.where((lane >> 3) == e, types[k, 0, band ^ e], 0)
        match = (row & 15) == kind
        made = [match & (part == head)]
        for i in range(3):
            made.append(match & ((head >> 1) == i) & (part == 6 + (head & 1)))
        route = [jnp.where(m, 1.0, 0.0).astype(bf16) for m in made]
        small = []
        for chunk in range(8):
            y, x = rep ^ (chunk // 2), side ^ (chunk % 2)
            dense[chunk * ROWS : (chunk + 1) * ROWS] = ref[y, x, :ROWS]
            small.append(ref[y, x, ROWS:CHUNK].astype(f32)[0:1] * factor)
            here = ref[y, x, CHUNK:]
            rows = dot(route[0], here) * factor
            for h in range(HEADS):
                tables[k, h, :, 384 * chunk : 384 * chunk + 384] = rows[16 * h : 16 * h + 16]
            if chunk < 2:
                left = sum(dot(route[1 + i], here[:, 128 * i : 128 * i + 128]) for i in range(3)) * factor
                start = 3072 + 128 * chunk
                size = min(128, REL - start)
                for h in range(HEADS):
                    tables[k, h, :, start : start + size] = left[16 * h : 16 * h + 16, :size]
        load = lambda i: dense[i * C : (i + 1) * C].astype(f32) * factor
        expand[k, :, : 2 * C] = load(0)
        expand[k, :, 2 * C :] = load(1)
        narrow[k, :, : 2 * C] = load(2)
        narrow[k, :, 2 * C :] = load(3)
        inward[k, :, : 2 * C] = load(4)
        both = load(5)
        inward[k, :, 2 * C :] = both[:, :C]
        outward[k] = both[:, C:]
        upbias[k : k + 1, : 2 * C] = small[0]
        upbias[k : k + 1, 2 * C :] = small[1]
        downbias[k : k + 1] = small[2][:, :C]
        scales[k, 1:2] = small[2][:, C:]
        offsets[k, 1:2] = small[3][:, :C]
        inbias[k : k + 1, : 2 * C] = small[4]
        inbias[k : k + 1, 2 * C :] = small[5][:, :C]
        outbias[k : k + 1] = small[5][:, C:]
        scales[k, 0:1] = small[6][:, :C]
        offsets[k, 0:1] = small[6][:, C:]

    sent = []
    for k in range(2):
        for source, wanted in ((own, core == k), (got, core != k)):

            @pl.when(wanted)
            def _(k=k, source=source):
                unpack(k, source)

        for n, array in enumerate((inward, outward, expand, narrow, tables)):
            sent.append(pltpu.make_async_copy(array.at[k], big[n].at[k], sems.at[5 * k + n]))
            sent[-1].start()
    for copy in sent:
        copy.wait()


def call(kernel, ins, outs, scratch=(), far_outs=0, raw_outs=0, aliases={}, limit=VMEM):
    specs, fetched, slots = [], [], []
    for array, block, far in ins:
        dims = array.ndim
        shape = array.shape if block in (None, "smem", "raw") else (1,) + array.shape[1:]
        if block == "smem":
            specs.append(pl.BlockSpec(memory_space=pltpu.SMEM))
        elif block == "raw":
            specs.append(pl.BlockSpec(memory_space=pltpu.HBM))
        elif far:
            specs.append(pl.BlockSpec(memory_space=pltpu.HBM))
            fetched.append((len(specs) - 1, block))
            slots.append(pltpu.VMEM(shape, array.dtype))
        else:
            specs.append(pl.BlockSpec(array.shape, lambda i, dims=dims: (0,) * dims))
    out_specs = []
    for i, o in enumerate(outs):
        if i < raw_outs:
            out_specs.append(pl.BlockSpec(memory_space=pltpu.HBM))
        elif i < far_outs:
            out_specs.append(pl.BlockSpec(memory_space=pltpu.HBM))
            slots.append(pltpu.VMEM(o.shape, o.dtype))
        else:
            out_specs.append(pl.BlockSpec(o.shape, lambda i, dims=len(o.shape): (0,) * dims))

    def wrapped(*refs):
        in_refs, refs = list(refs[: len(ins)]), refs[len(ins) :]
        out_refs, refs = list(refs[: len(outs)]), refs[len(outs) :]
        own, refs = refs[: len(scratch)], refs[len(scratch) :]
        copies = []
        for n, (at, block) in enumerate(fetched):
            source = in_refs[at] if block is None else in_refs[at].at[block : block + 1]
            copies.append(pltpu.make_async_copy(source, refs[n], refs[-1].at[n]))
            in_refs[at] = refs[n]
        for copy in copies:
            copy.start()
        for copy in copies:
            copy.wait()
        targets = out_refs[:far_outs]
        out_refs[:far_outs] = refs[len(fetched) : len(fetched) + far_outs]
        kernel(*in_refs, *out_refs, *own)
        copies = [
            pltpu.make_async_copy(out_refs[n], targets[n], refs[-1].at[len(fetched) + n]) for n in range(far_outs)
        ]
        for copy in copies:
            copy.start()
        for copy in copies:
            copy.wait()

    size = lambda s: math.prod(s.shape) * jnp.dtype(s.dtype).itemsize
    moved = sum(size(o) for o in outs) + sum(size(a) for a, b, _ in ins)
    if slots:
        slots.append(pltpu.SemaphoreType.DMA((len(slots),)))
    return pl.pallas_call(
        wrapped,
        grid=(1,),
        in_specs=specs,
        out_specs=out_specs,
        out_shape=outs,
        scratch_shapes=list(scratch) + slots,
        input_output_aliases=aliases,
        compiler_params=pltpu.CompilerParams(vmem_limit_bytes=limit),
        cost_estimate=pl.CostEstimate(flops=10**9, bytes_accessed=moved, transcendentals=0),
    )(*[array for array, _, _ in ins])


def send_pieces(pieces, step):
    lat, lon = lax.axis_size("lat"), lax.axis_size("lon")
    rows = [(i, (i + step) % lat) for i in range(lat)]
    cols = [(i, (i + step) % lon) for i in range(lon)]
    both = [(i * lon + j, (i + step) % lat * lon + (j + step) % lon) for i in range(lat) for j in range(lon)]
    return (
        pieces[0],
        lax.ppermute(pieces[1], "lat", rows),
        lax.ppermute(pieces[2], "lon", cols),
        lax.ppermute(pieces[3], ("lat", "lon"), both),
    )


def swap(array, axis, distance):
    return lax.ppermute(array, axis, [(i, i ^ distance) for i in range(lax.axis_size(axis))])


def trade(array, over_rep, over_side):
    if not over_rep and not over_side:
        return array
    lon, rep = lax.axis_size("lon"), lax.axis_size("rep")
    pairs = [
        (i * rep + j, (i ^ (2 * over_side)) * rep + (j ^ over_rep)) for i in range(lon) for j in range(rep)
    ]
    return lax.ppermute(array, ("lon", "rep"), pairs)


def body(
    fields, upstream, scales, offsets, inward, inbias, outward, outbias, expand, upbias, narrow, downbias,
    tables, window_type, row_valid,
):
    const = constants()
    levels, row_count, col_count = fields.shape[1:4]
    total_rows = row_valid.shape[0]
    x = fields[0].transpose(1, 2, 0, 3).reshape(TOK, C)
    cotangent = upstream[0].transpose(1, 2, 0, 3).reshape(TOK, C)
    narrow = jnp.swapaxes(narrow, 1, 2)
    tables = jnp.swapaxes(tables, 1, 2)
    of = jax.ShapeDtypeStruct
    piece = [of((2 * QUAD, C), bf16)] * 4
    token = of((TOK, C), bf16)
    state = [token, of((KEYS, C), bf16), of((KEYS, C), bf16), of((HEADS, TOK, KEYS), bf16), token]
    pack = of((8, CHUNK, 2 * C), bf16)
    turned = pltpu.VMEM((192, 1536), bf16)
    dbias = pltpu.VMEM((TOK, 1536), bf16)
    rows = pltpu.VMEM((8, 3456), f32)
    near = lambda *arrays: [(m, None, False) for m in arrays]
    far = lambda *arrays: [(m, None, True) for m in arrays]
    block = lambda k, *arrays: [(m, k, True) for m in arrays]
    raw = lambda *arrays: [(m, "raw", True) for m in arrays]
    fixed = lambda *names: far(*[const[name] for name in names])
    scalars = [(window_type, "smem", False), (row_valid, "smem", False)]

    def weights(k):
        return (
            far(scales, offsets) + block(k, inward) + far(inbias) + block(k, outward) + far(outbias)
            + block(k, expand) + far(upbias) + block(k, narrow) + far(downbias)
        )

    *state0, h1, pa, pb, pc, pd = call(
        first_kernel,
        scalars + far(x, cotangent) + weights(0) + block(0, tables) + fixed("turn", "cut", "spread", "place", "sort"),
        state + [token] + piece,
        (pltpu.VMEM((TOK, 1536), f32), turned, rows),
        6,
    )
    pieces = send_pieces((pa, pb, pc, pd), -1)
    (bias1,) = call(
        bias_kernel,
        scalars + block(1, tables) + fixed("spread", "place", "sort"),
        [of((TOK, 1536), f32)],
        (turned, rows),
    )
    pack1, *pieces = call(
        second_kernel,
        far(*pieces) + weights(1) + far(bias1) + fixed("join", "spread", "place", "sort"),
        [pack] + piece,
        [pltpu.VMEM(m.shape, m.dtype) for m in state] + [dbias, turned],
    )
    pieces = send_pieces(pieces, 1)
    got1 = swap(pack1, "lon", 1)
    result, adjoint, pack0 = call(
        first_back_kernel,
        far(*pieces, x, h1, scales, offsets) + block(0, inward, outward, expand) + far(upbias)
        + block(0, narrow) + far(downbias, *state0) + fixed("turn", "cut", "spread", "place", "sort"),
        [token, token, pack],
        (dbias, turned),
    )
    got0 = swap(pack0, "lon", 1)

    part = of((1, CHUNK, 2 * C), bf16)
    dealt = call(
        core_kernel,
        raw(pack0, pack1, got0, got1),
        [part] * 8,
        [pltpu.VMEM((8,) + part.shape, bf16)] * 3 + [pltpu.SemaphoreType.DMA((24,))],
        raw_outs=8,
    )
    dealt = [trade(m, n // 2, n % 2) for n, m in enumerate(dealt)]
    (a,) = call(add_kernel, near(*dealt), [of((CHUNK, 2 * C), bf16)], limit=SMALL)
    for step, height in ((1, CHUNK + 32), (4, CHUNK + 128)):
        others = [swap(a, "lat", step * i) for i in (1, 2, 3)]
        (a,) = call(band_kernel, near(a, *others), [of((height, 2 * C), bf16)], limit=SMALL)
    a = jnp.stack([trade(a, n // 2, n % 2) for n in range(8)]).reshape((4, 2) + a.shape)
    got = swap(a, "lon", 1)

    factor = 1.0 / math.sqrt(lax.axis_size("rep") * levels * total_rows * col_count * lax.axis_size("lon"))

    wide = [(2, C, 3 * C), (2, C, C), (2, C, FFN), (2, C, FFN), tables.shape]
    short = [(2, 2, C), (2, 2, C), (2, 3 * C), (2, C), (2, FFN), (2, C)]
    joined = call(
        functools.partial(final_kernel, factor),
        scalars[:1] + near(a, got),
        [of(m, f32) for m in wide + short],
        [pltpu.VMEM(m, f32) for m in wide]
        + [pltpu.VMEM((8 * ROWS, 2 * C), bf16), pltpu.SemaphoreType.DMA((10,))],
        raw_outs=5,
        limit=2 * SMALL,
    )
    inward_out, outward_out, expand_out, narrow_out, tables_out = joined[:5]
    scales_out, offsets_out, inbias_out, outbias_out, upbias_out, downbias_out = joined[5:]
    back = lambda m: m.reshape(row_count, col_count, levels, C).transpose(2, 0, 1, 3)[None]
    return (
        back(result), back(adjoint), scales_out, offsets_out, inward_out, inbias_out, outward_out, outbias_out,
        expand_out, upbias_out, jnp.swapaxes(narrow_out, 1, 2), downbias_out, jnp.swapaxes(tables_out, 1, 2),
    )


def solution(mesh):
    grid = P("rep", None, "lat", "lon", None)
    return jax.shard_map(
        body, mesh=mesh, in_specs=(grid, grid) + (P(),) * 13, out_specs=(grid, grid) + (P(),) * 11, check_vma=False
    )
```

```python
import functools
import math

import jax
import jax.numpy as jnp
import numpy as np
from jax import lax
from jax.experimental import pallas as pl
from jax.experimental.pallas import tpu as pltpu
from jax.sharding import PartitionSpec as P

C = 192
HEADS = 6
FFN = 768
TOK = 144
KEYS = 256
QUAD = 48
REL = 3312
ROWS = 144
CHUNK = ROWS + 16
epsilon = 1e-05
masked = -1000000000.0
f32 = jnp.float32
bf16 = jnp.bfloat16
VMEM = 64 * 1024 * 1024
SMALL = 16 * 1024 * 1024


def constants():
    tok = np.arange(TOK)
    a, r, c = tok // 72, tok // 12 % 6, tok % 12
    turn = np.zeros((TOK, TOK), np.float32)
    turn[tok, (r * 12 + c) * 2 + a] = 1
    quad = np.where(r >= 3, 0, 1) + np.where(c >= 6, 0, 2)
    cut = np.zeros((4 * QUAD, TOK), np.float32)
    cut[quad * QUAD + a * 18 + r % 3 * 6 + c % 6, tok] = 1
    quad = np.where(r < 3, 0, 1) + np.where(c < 6, 0, 2)
    join = np.zeros((TOK, 4 * QUAD), np.float32)
    join[tok, quad * QUAD + (1 - a) * 18 + r % 3 * 6 + c % 6] = 1
    spread = np.zeros((256, 12 * 128), np.float32)
    for ci in range(12):
        for rj in range(6):
            for cj in range(12):
                spread[rj * 23 + ci - cj + 11, ci * 128 + rj * 12 + cj] = 1
    place = np.zeros((TOK, 192), np.float32)
    place[tok, c * 16 + a * 6 + r] = 1
    sort = np.zeros((192, 192), np.float32)
    for ai in range(2):
        for aj in range(2):
            for ri in range(6):
                for h in range(HEADS):
                    sort[(h * 2 + aj) * 16 + ai * 6 + ri, ((ai * 2 + aj) * 6 + ri) * 8 + h] = 1
    made = {"turn": turn, "cut": cut, "join": join, "place": place, "sort": sort}
    made = {name: jnp.asarray(m, f32) for name, m in made.items()}
    made["spread"] = jnp.asarray(spread, bf16)
    return made


def low(ref):
    return ref[...].astype(bf16)


def dot(x, y, dims=((1,), (0,))):
    return lax.dot_general(x, y, (dims, ((), ())), preferred_element_type=f32)


def dot_nt(x, y):
    return dot(x, y, ((1,), (1,)))


def dot_tn(x, y):
    return dot(x, y, ((0,), (0,)))


def norm_parts(values):
    centred = values - jnp.mean(values, axis=-1, keepdims=True)
    rstd = lax.rsqrt(jnp.mean(centred * centred, axis=-1, keepdims=True) + epsilon)
    return centred * rstd, rstd


def norm_fwd(values, gain, shift):
    return (norm_parts(values)[0] * gain + shift).astype(bf16)


def norm_bwd(values, gain, dy):
    hat, rstd = norm_parts(values)
    dhat = dy * gain
    first = jnp.mean(dhat, axis=-1, keepdims=True)
    second = jnp.mean(dhat * hat, axis=-1, keepdims=True)
    return rstd * (dhat - first - hat * second), colsum(dy * hat), colsum(dy)


def colsum(x):
    return jnp.sum(x, axis=0, keepdims=True)


def erf(x):
    return lax.erf(x)


def gelu_parts(z):
    cdf = 0.5 * (1.0 + erf(z * (2.0 ** -0.5)))
    return cdf, z * cdf


def pad_keys(x):
    blank = jnp.zeros((56, x.shape[1]), f32)
    return jnp.concatenate([x[:72], blank, x[72:], blank], axis=0)


def unpad_keys(x):
    return jnp.concatenate([x[:72], x[128:200]], axis=0)


def head_only(x, h):
    lane = lax.broadcasted_iota(jnp.int32, x.shape, 1)
    return jnp.where((lane >= 32 * h) & (lane < 32 * h + 32), x.astype(f32), 0.0).astype(bf16)


def join_rows(refs, part):
    return jnp.concatenate([ref[part * QUAD : (part + 1) * QUAD] for ref in refs], axis=0)


def write_pieces(first, second, refs):
    for i, ref in enumerate(refs):
        ref[:QUAD] = first[i * QUAD : (i + 1) * QUAD].astype(bf16)
        ref[QUAD:] = second[i * QUAD : (i + 1) * QUAD].astype(bf16)


def place_of():
    lon = lax.axis_index("lon")
    return lax.axis_index("lat"), lon & 1, lon >> 1, lax.axis_index("rep")


def key_mask(valid, band, shift):
    lane = lax.broadcasted_iota(jnp.int32, (1, KEYS), 1)
    column = lane & 127
    total_rows = valid.shape[0]
    last = jnp.where(band == total_rows // 6 - 1, 1, 0)
    allowed = jnp.zeros((1, KEYS), jnp.int32)
    for r in range(6):
        at = band * 6 + r + shift
        at = jnp.where(at >= total_rows, at - total_rows, at)
        hit = (column >= 12 * r) & (column < 12 * r + 12)
        allowed = allowed + jnp.where(hit, valid[at], 0)
    if shift:
        row = lax.broadcasted_iota(jnp.int32, (TOK, KEYS), 0)
        wide = lax.broadcasted_iota(jnp.int32, (TOK, KEYS), 1)
        row_level = jnp.where(row >= 72, 1, 0)
        key_level = wide >> 7
        row_part = jnp.where(row - 72 * row_level >= 36, 1, 0)
        key_part = jnp.where((wide & 127) >= 36, 1, 0)
        apart = (row_level ^ key_level) | ((row_part ^ key_part) & last)
        allowed = jnp.where(apart == 0, jnp.broadcast_to(allowed, (TOK, KEYS)), 0)
        column = wide & 127
    mask = jnp.where(allowed > 0, 0.0, masked)
    return jnp.where(column < 72, mask, 2 * masked)


def make_bias(k, types, valid, tables, spread, place, sort, bias_ref, turn_ref, row_ref):
    row_ref[...] = jnp.zeros(row_ref.shape, f32)
    band = place_of()[0]
    kind = types[k, 0, band]
    for h in range(HEADS):
        row_ref[h : h + 1, :REL] = tables[0, h, pl.ds(kind, 1), :]
    wide_rows = row_ref[...]
    rest = jnp.concatenate([wide_rows[:, 138 * i : 138 * i + 256] for i in range(24)], axis=0)
    total = None
    for _ in range(3):
        part = rest.astype(bf16)
        rest = rest - part.astype(f32)
        wide = dot(dot(sort, part).astype(bf16), spread)
        for g in range(12):
            for ci in range(12):
                turn_ref[ci * 16 : ci * 16 + 16, g * 128 : g * 128 + 128] = wide[
                    g * 16 : g * 16 + 16, ci * 128 : ci * 128 + 128
                ].astype(bf16)
        here = dot(place, turn_ref[...])
        total = here if total is None else total + here
    mask = key_mask(valid, band, 3 * k)
    for h in range(HEADS):
        bias_ref[:, h * KEYS : (h + 1) * KEYS] = total[:, h * KEYS : (h + 1) * KEYS] + mask


def table_adjoint(dbias, spread, place, sort, turn_ref):
    rows = dot_tn(place, dbias)
    for g in range(12):
        for ci in range(12):
            turn_ref[g * 16 : g * 16 + 16, ci * 128 : ci * 128 + 128] = rows[
                ci * 16 : ci * 16 + 16, g * 128 : g * 128 + 128
            ].astype(bf16)
    narrow = dot_nt(turn_ref[...], spread).astype(bf16)
    rows = dot_tn(sort, narrow)
    pieces = [rows[8 * i : 8 * i + 8, :138] for i in range(24)]
    return jnp.concatenate(pieces + [jnp.zeros((8, 16), f32)], axis=1)


def put(pack, at, value):
    done = 0
    while done < value.shape[0]:
        chunk, row = divmod(at + done, ROWS)
        size = min(ROWS - row, value.shape[0] - done)
        pack[chunk, row : row + size] = value[done : done + size].astype(bf16)
        done += size


def put_rest(pack, table, small):
    row = lax.broadcasted_iota(jnp.int32, (8, 2 * C), 0)
    for chunk in range(8):
        own = table[:, 384 * chunk : 384 * chunk + 384]
        if chunk < 2:
            left = table[:, 3072 + 128 * chunk : 3200 + 128 * chunk]
            moved = [pltpu.roll(left, 6 - 2 * i, 0) if i < 3 else left for i in range(3)]
            own = jnp.where(row >= 6, jnp.concatenate(moved, axis=1), own)
        short = jnp.where(row == 0, small[chunk], 0.0) if chunk < len(small) else jnp.zeros((8, 2 * C), f32)
        pack[chunk, ROWS : ROWS + 16] = jnp.concatenate([own, short], axis=0).astype(bf16)


def attend_fwd(k, u, inward, inbias, outward, outbias, bias_ref, q_ref, k_ref, v_ref, p_ref, mix_ref):
    weight = inward[0].astype(bf16)
    shift = inbias[k : k + 1]
    keyed = pad_keys(u.astype(f32)).astype(bf16)
    q = (dot(u, weight[:, :C]) + shift[:, :C]).astype(bf16)
    key = (dot(keyed, weight[:, C : 2 * C]) + shift[:, C : 2 * C]).astype(bf16)
    v = (dot(keyed, weight[:, 2 * C :]) + shift[:, 2 * C :]).astype(bf16)
    q_ref[...] = q
    k_ref[...] = key
    v_ref[...] = v
    mix = jnp.zeros((TOK, C), f32)
    for h in range(HEADS):
        scores = dot_nt(head_only(q, h), key) * 32 ** (-0.5) + bias_ref[:, h * KEYS : (h + 1) * KEYS]
        weights = jnp.exp(scores - jnp.max(scores, axis=-1, keepdims=True))
        chances = (weights / jnp.sum(weights, axis=-1, keepdims=True)).astype(bf16)
        p_ref[h] = chances
        mix = mix + dot(chances, head_only(v, h))
    mix = mix.astype(bf16)
    mix_ref[...] = mix
    return (dot(mix, outward[0].astype(bf16)) + outbias[k : k + 1]).astype(bf16)


def attend_bwd(dout, u, inward, outward, spread, place, sort, q_ref, k_ref, v_ref, p_ref, mix_ref, pack, dbias_ref, turn_ref):
    q, key, v, mix = q_ref[...], k_ref[...], v_ref[...], mix_ref[...]
    weight = inward[0].astype(bf16)
    dmix = dot_nt(dout, outward[0].astype(bf16)).astype(bf16)
    dq = jnp.zeros((TOK, C), f32)
    dk = jnp.zeros((KEYS, C), f32)
    dv = jnp.zeros((KEYS, C), f32)
    for h in range(HEADS):
        chances = p_ref[h]
        wide = chances.astype(f32)
        dmix_h = head_only(dmix, h)
        dchances = dot_nt(dmix_h, v)
        dscores = wide * (dchances - jnp.sum(wide * dchances, axis=-1, keepdims=True))
        narrow = dscores.astype(bf16)
        dbias_ref[:, h * KEYS : (h + 1) * KEYS] = narrow
        dv = dv + dot_tn(chances, dmix_h)
        dq = dq + dot(narrow, head_only(key, h))
        dk = dk + dot_tn(narrow, head_only(q, h))
    dq = (dq * 32 ** (-0.5)).astype(bf16)
    dk = (dk * 32 ** (-0.5)).astype(bf16)
    dv = dv.astype(bf16)
    keyed = pad_keys(u.astype(f32)).astype(bf16)
    du = dot_nt(dq, weight[:, :C]) + unpad_keys(
        dot_nt(dk, weight[:, C : 2 * C]) + dot_nt(dv, weight[:, 2 * C :])
    )
    pair = lambda x, y: jnp.concatenate([x, y], axis=1)
    put(pack, 4 * C, pair(dot_tn(u, dq), dot_tn(keyed, dk)))
    put(pack, 5 * C, pair(dot_tn(keyed, dv), dot_tn(mix, dout)))
    small = [
        pair(colsum(dq.astype(f32)), colsum(dk.astype(f32))),
        pair(colsum(dv.astype(f32)), colsum(dout.astype(f32))),
    ]
    return du, table_adjoint(dbias_ref[...], spread, place, sort, turn_ref), small


def mlp_fwd(h, gain, shift, expand, upbias, narrow_t, downbias):
    z = dot(norm_fwd(h, gain, shift), expand) + upbias
    hidden = gelu_parts(z)[1].astype(bf16)
    return (h + dot_nt(hidden, narrow_t) + downbias).astype(bf16)


def mlp_both(h, gain, shift, expand, upbias, narrow_t, downbias, dout, want):
    normed = norm_fwd(h, gain, shift)
    z = dot(normed, expand) + upbias
    cdf, wide = gelu_parts(z)
    hidden = wide.astype(bf16)
    result = None
    if want:
        result = (h + dot_nt(hidden, narrow_t) + downbias).astype(bf16)
    slope = cdf + z * jnp.exp(-0.5 * z * z) * (1.0 / math.sqrt(2.0 * math.pi))
    dz32 = dot(dout, narrow_t) * slope
    dz = dz32.astype(bf16)
    dnormed = dot_nt(dz, expand).astype(bf16).astype(f32)
    dx, dgain, dshift = norm_bwd(h, gain, dnormed)
    dwide = dout.astype(f32)
    dh = (dwide + dx).astype(bf16)
    dexpand = dot_tn(normed, dz)
    dnarrow = dot_tn(dout, hidden)
    dense = [dexpand[:, : 2 * C], dexpand[:, 2 * C :], dnarrow[:, : 2 * C], dnarrow[:, 2 * C :]]
    dup = colsum(dz32)
    small = [
        dup[:, : 2 * C],
        dup[:, 2 * C :],
        jnp.concatenate([colsum(dwide), dgain], axis=1),
        jnp.concatenate([dshift, jnp.zeros((1, C), f32)], axis=1),
    ]
    return result, dh, dense, small


def bias_kernel(types, valid, tables, spread, place, sort, bias_ref, turned, rows):
    make_bias(1, types, valid, tables, spread[...], low(place), low(sort), bias_ref, turned, rows)


def first_kernel(
    types, valid, fields, upstream, scales, offsets, inward, inbias, outward, outbias, expand, upbias, narrow, downbias,
    tables, turn, cut, spread, place, sort,
    q, k, v, p, mix, h1, pa, pb, pc, pd, bias, turned, rows,
):
    make_bias(0, types, valid, tables, spread[...], low(place), low(sort), bias, turned, rows)
    order, route = low(turn), low(cut)
    x = dot(order, fields[...])
    u = norm_fwd(x, scales[0, 0:1], offsets[0, 0:1])
    branch = attend_fwd(0, u, inward, inbias, outward, outbias, bias, q, k, v, p, mix)
    carried = (x + branch.astype(f32)).astype(bf16)
    h1[...] = carried
    out = mlp_fwd(
        carried.astype(f32), scales[0, 1:2], offsets[0, 1:2], expand[0].astype(bf16), upbias[0:1],
        narrow[0].astype(bf16), downbias[0:1],
    )
    cotangent = dot(order, upstream[...]).astype(bf16)
    write_pieces(dot(route, out), dot(route, cotangent), (pa, pb, pc, pd))


def second_kernel(
    qa, qb, qc, qd, scales, offsets, inward, inbias, outward, outbias, expand, upbias, narrow, downbias,
    bias, join, spread, place, sort,
    pack, pa, pb, pc, pd, q, k, v, p, mix, dbias, turned,
):
    route = low(join)
    pieces = (qa, qb, qc, qd)
    y1 = dot(route, join_rows(pieces, 0))
    cotangent = dot(route, join_rows(pieces, 1)).astype(bf16)
    u = norm_fwd(y1, scales[1, 0:1], offsets[1, 0:1])
    branch = attend_fwd(1, u, inward, inbias, outward, outbias, bias, q, k, v, p, mix)
    h2 = (y1 + branch.astype(f32)).astype(bf16).astype(f32)
    out, dh, dense, short = mlp_both(
        h2, scales[1, 1:2], offsets[1, 1:2], expand[0].astype(bf16), upbias[1:2],
        narrow[0].astype(bf16), downbias[1:2], cotangent, True,
    )
    for i, part in enumerate(dense):
        put(pack, i * C, part)
    du, table, small = attend_bwd(
        dh, u, inward, outward, spread[...], low(place), low(sort), q, k, v, p, mix, pack, dbias, turned
    )
    dx, dgain, dshift = norm_bwd(y1, scales[1, 0:1], du.astype(bf16).astype(f32))
    dy1 = (dh.astype(f32) + dx.astype(bf16).astype(f32)).astype(bf16)
    put_rest(pack, table, short + small + [jnp.concatenate([dgain, dshift], axis=1)])
    write_pieces(dot_tn(route, dy1), dot_tn(route, out), (pa, pb, pc, pd))


def first_back_kernel(
    qa, qb, qc, qd, fields, h1, scales, offsets, inward, outward, expand, upbias, narrow, downbias,
    q, k, v, p, mix, turn, cut, spread, place, sort,
    result, adjoint, pack, dbias, turned,
):
    order, route = low(turn), low(cut)
    pieces = (qa, qb, qc, qd)
    result[...] = dot_tn(order, dot_tn(route, join_rows(pieces, 1)).astype(bf16)).astype(bf16)
    dy1 = dot_tn(route, join_rows(pieces, 0)).astype(bf16)
    _, dh1, dense, short = mlp_both(
        h1[...].astype(f32), scales[0, 1:2], offsets[0, 1:2], expand[0].astype(bf16), upbias[0:1],
        narrow[0].astype(bf16), downbias[0:1], dy1, False,
    )
    for i, part in enumerate(dense):
        put(pack, i * C, part)
    x = dot(order, fields[...])
    u = norm_fwd(x, scales[0, 0:1], offsets[0, 0:1])
    du, table, small = attend_bwd(
        dh1, u, inward, outward, spread[...], low(place), low(sort), q, k, v, p, mix, pack, dbias, turned
    )
    dx0, dgain0, dshift0 = norm_bwd(x, scales[0, 0:1], du.astype(bf16).astype(f32))
    adjoint[...] = dot_tn(order, (dh1.astype(f32) + dx0).astype(bf16)).astype(bf16)
    put_rest(pack, table, short + small + [jnp.concatenate([dgain0, dshift0], axis=1)])


def core_kernel(first, second, got_first, got_second, *refs):
    outs, (own, got, made, sems) = refs[:8], refs[8:]
    _, core, side, rep = place_of()
    part = lambda n: pl.ds((rep ^ (n // 2)) * 2 + (side ^ (n % 2)), 1)
    order = (5, 3, 7, 1, 4, 2, 6, 0)
    for k, (mine, theirs) in enumerate(((first, got_first), (second, got_second))):

        @pl.when(core == k)
        def _(mine=mine, theirs=theirs):
            for n in order:
                pltpu.make_async_copy(mine.at[part(n)], own.at[n], sems.at[n]).start()
                pltpu.make_async_copy(theirs.at[part(n)], got.at[n], sems.at[8 + n]).start()

    sent = []
    for n in order:
        pltpu.make_async_copy(first.at[part(n)], own.at[n], sems.at[n]).wait()
        pltpu.make_async_copy(got_first.at[part(n)], got.at[n], sems.at[8 + n]).wait()
        made[n] = (own[n].astype(f32) + got[n].astype(f32)).astype(bf16)
        sent.append(pltpu.make_async_copy(made.at[n], outs[n], sems.at[16 + n]))
        sent[-1].start()
    for copy in sent:
        copy.wait()


def add_kernel(*refs):
    total = refs[0][...].astype(f32)
    for ref in refs[1:-1]:
        total = total + ref[...].astype(f32)
    refs[-1][...] = total.astype(bf16)


def band_kernel(a, b, c, d, out):
    four = [ref[...].astype(f32) for ref in (a, b, c, d)]
    total = four[0] + four[1] + four[2] + four[3]
    out[:ROWS] = total[:ROWS].astype(bf16)
    if a.shape[0] == CHUNK:
        aside = jnp.concatenate([total[ROWS + 8 :], jnp.zeros((8, 2 * C), f32)], axis=0)
        out[ROWS:CHUNK] = aside.astype(bf16)
        out[CHUNK:] = jnp.concatenate([m[ROWS : ROWS + 8] for m in four], axis=0).astype(bf16)
    else:
        out[ROWS:CHUNK] = total[ROWS:CHUNK].astype(bf16)
        for i, ref in enumerate((a, b, c, d)):
            out[CHUNK + 32 * i : CHUNK + 32 * i + 32] = ref[CHUNK:]


def final_kernel(factor, types, own, got, *refs):
    big, short = refs[:5], refs[5:11]
    inward, outward, expand, narrow, tables, dense, sems = refs[11:]
    scales, offsets, inbias, outbias, upbias, downbias = short
    band, core, side, rep = place_of()
    lane = lax.broadcasted_iota(jnp.int32, (1, 128), 1)
    row = lax.broadcasted_iota(jnp.int32, (96, 128), 0)
    part = lax.broadcasted_iota(jnp.int32, (96, 128), 1) & 7
    head = row >> 4

    def unpack(k, ref):
        kind = jnp.zeros((1, 128), jnp.int32)
        for e in range(16):
            kind = kind + jnp.where((lane >> 3) == e, types[k, 0, band ^ e], 0)
        match = (row & 15) == kind
        made = [match & (part == head)]
        for i in range(3):
            made.append(match & ((head >> 1) == i) & (part == 6 + (head & 1)))
        route = [jnp.where(m, 1.0, 0.0).astype(bf16) for m in made]
        small = []
        for chunk in range(8):
            y, x = rep ^ (chunk // 2), side ^ (chunk % 2)
            dense[chunk * ROWS : (chunk + 1) * ROWS] = ref[y, x, :ROWS]
            small.append(ref[y, x, ROWS:CHUNK].astype(f32)[0:1] * factor)
            here = ref[y, x, CHUNK:]
            rows = dot(route[0], here) * factor
            for h in range(HEADS):
                tables[k, h, :, 384 * chunk : 384 * chunk + 384] = rows[16 * h : 16 * h + 16]
            if chunk < 2:
                left = sum(dot(route[1 + i], here[:, 128 * i : 128 * i + 128]) for i in range(3)) * factor
                start = 3072 + 128 * chunk
                size = min(128, REL - start)
                for h in range(HEADS):
                    tables[k, h, :, start : start + size] = left[16 * h : 16 * h + 16, :size]
        load = lambda i: dense[i * C : (i + 1) * C].astype(f32) * factor
        expand[k, :, : 2 * C] = load(0)
        expand[k, :, 2 * C :] = load(1)
        narrow[k, :, : 2 * C] = load(2)
        narrow[k, :, 2 * C :] = load(3)
        inward[k, :, : 2 * C] = load(4)
        both = load(5)
        inward[k, :, 2 * C :] = both[:, :C]
        outward[k] = both[:, C:]
        upbias[k : k + 1, : 2 * C] = small[0]
        upbias[k : k + 1, 2 * C :] = small[1]
        downbias[k : k + 1] = small[2][:, :C]
        scales[k, 1:2] = small[2][:, C:]
        offsets[k, 1:2] = small[3][:, :C]
        inbias[k : k + 1, : 2 * C] = small[4]
        inbias[k : k + 1, 2 * C :] = small[5][:, :C]
        outbias[k : k + 1] = small[5][:, C:]
        scales[k, 0:1] = small[6][:, :C]
        offsets[k, 0:1] = small[6][:, C:]

    sent = []
    for k in range(2):
        for source, wanted in ((own, core == k), (got, core != k)):

            @pl.when(wanted)
            def _(k=k, source=source):
                unpack(k, source)

        for n, array in enumerate((inward, outward, expand, narrow, tables)):
            sent.append(pltpu.make_async_copy(array.at[k], big[n].at[k], sems.at[5 * k + n]))
            sent[-1].start()
    for copy in sent:
        copy.wait()


def call(kernel, ins, outs, scratch=(), far_outs=0, raw_outs=0, aliases={}, limit=VMEM):
    specs, fetched, slots = [], [], []
    for array, block, far in ins:
        dims = array.ndim
        shape = array.shape if block in (None, "smem", "raw") else (1,) + array.shape[1:]
        if block == "smem":
            specs.append(pl.BlockSpec(memory_space=pltpu.SMEM))
        elif block == "raw":
            specs.append(pl.BlockSpec(memory_space=pltpu.HBM))
        elif far:
            specs.append(pl.BlockSpec(memory_space=pltpu.HBM))
            fetched.append((len(specs) - 1, block))
            slots.append(pltpu.VMEM(shape, array.dtype))
        else:
            specs.append(pl.BlockSpec(array.shape, lambda i, dims=dims: (0,) * dims))
    out_specs = []
    for i, o in enumerate(outs):
        if i < raw_outs:
            out_specs.append(pl.BlockSpec(memory_space=pltpu.HBM))
        elif i < far_outs:
            out_specs.append(pl.BlockSpec(memory_space=pltpu.HBM))
            slots.append(pltpu.VMEM(o.shape, o.dtype))
        else:
            out_specs.append(pl.BlockSpec(o.shape, lambda i, dims=len(o.shape): (0,) * dims))

    def wrapped(*refs):
        in_refs, refs = list(refs[: len(ins)]), refs[len(ins) :]
        out_refs, refs = list(refs[: len(outs)]), refs[len(outs) :]
        own, refs = refs[: len(scratch)], refs[len(scratch) :]
        copies = []
        for n, (at, block) in enumerate(fetched):
            source = in_refs[at] if block is None else in_refs[at].at[block : block + 1]
            copies.append(pltpu.make_async_copy(source, refs[n], refs[-1].at[n]))
            in_refs[at] = refs[n]
        for copy in copies:
            copy.start()
        for copy in copies:
            copy.wait()
        targets = out_refs[:far_outs]
        out_refs[:far_outs] = refs[len(fetched) : len(fetched) + far_outs]
        kernel(*in_refs, *out_refs, *own)
        copies = [
            pltpu.make_async_copy(out_refs[n], targets[n], refs[-1].at[len(fetched) + n]) for n in range(far_outs)
        ]
        for copy in copies:
            copy.start()
        for copy in copies:
            copy.wait()

    size = lambda s: math.prod(s.shape) * jnp.dtype(s.dtype).itemsize
    moved = sum(size(o) for o in outs) + sum(size(a) for a, b, _ in ins)
    if slots:
        slots.append(pltpu.SemaphoreType.DMA((len(slots),)))
    return pl.pallas_call(
        wrapped,
        grid=(1,),
        in_specs=specs,
        out_specs=out_specs,
        out_shape=outs,
        scratch_shapes=list(scratch) + slots,
        input_output_aliases=aliases,
        compiler_params=pltpu.CompilerParams(vmem_limit_bytes=limit),
        cost_estimate=pl.CostEstimate(flops=10**9, bytes_accessed=moved, transcendentals=0),
    )(*[array for array, _, _ in ins])


def send_pieces(pieces, step):
    lat, lon = lax.axis_size("lat"), lax.axis_size("lon")
    rows = [(i, (i + step) % lat) for i in range(lat)]
    cols = [(i, (i + step) % lon) for i in range(lon)]
    both = [(i * lon + j, (i + step) % lat * lon + (j + step) % lon) for i in range(lat) for j in range(lon)]
    return (
        pieces[0],
        lax.ppermute(pieces[1], "lat", rows),
        lax.ppermute(pieces[2], "lon", cols),
        lax.ppermute(pieces[3], ("lat", "lon"), both),
    )


def swap(array, axis, distance):
    return lax.ppermute(array, axis, [(i, i ^ distance) for i in range(lax.axis_size(axis))])


def body(
    fields, upstream, scales, offsets, inward, inbias, outward, outbias, expand, upbias, narrow, downbias,
    tables, window_type, row_valid,
):
    const = constants()
    levels, row_count, col_count = fields.shape[1:4]
    total_rows = row_valid.shape[0]
    x = fields[0].transpose(1, 2, 0, 3).reshape(TOK, C)
    cotangent = upstream[0].transpose(1, 2, 0, 3).reshape(TOK, C)
    narrow = jnp.swapaxes(narrow, 1, 2)
    tables = jnp.swapaxes(tables, 1, 2)
    of = jax.ShapeDtypeStruct
    piece = [of((2 * QUAD, C), bf16)] * 4
    token = of((TOK, C), bf16)
    state = [token, of((KEYS, C), bf16), of((KEYS, C), bf16), of((HEADS, TOK, KEYS), bf16), token]
    pack = of((8, CHUNK, 2 * C), bf16)
    turned = pltpu.VMEM((192, 1536), bf16)
    dbias = pltpu.VMEM((TOK, 1536), bf16)
    rows = pltpu.VMEM((8, 3456), f32)
    near = lambda *arrays: [(m, None, False) for m in arrays]
    far = lambda *arrays: [(m, None, True) for m in arrays]
    block = lambda k, *arrays: [(m, k, True) for m in arrays]
    raw = lambda *arrays: [(m, "raw", True) for m in arrays]
    fixed = lambda *names: far(*[const[name] for name in names])
    scalars = [(window_type, "smem", False), (row_valid, "smem", False)]

    def weights(k):
        return (
            far(scales, offsets) + block(k, inward) + far(inbias) + block(k, outward) + far(outbias)
            + block(k, expand) + far(upbias) + block(k, narrow) + far(downbias)
        )

    *state0, h1, pa, pb, pc, pd = call(
        first_kernel,
        scalars + far(x, cotangent) + weights(0) + block(0, tables) + fixed("turn", "cut", "spread", "place", "sort"),
        state + [token] + piece,
        (pltpu.VMEM((TOK, 1536), f32), turned, rows),
        6,
    )
    pieces = send_pieces((pa, pb, pc, pd), -1)
    (bias1,) = call(
        bias_kernel,
        scalars + block(1, tables) + fixed("spread", "place", "sort"),
        [of((TOK, 1536), f32)],
        (turned, rows),
    )
    pack1, *pieces = call(
        second_kernel,
        far(*pieces) + weights(1) + far(bias1) + fixed("join", "spread", "place", "sort"),
        [pack] + piece,
        [pltpu.VMEM(m.shape, m.dtype) for m in state] + [dbias, turned],
    )
    pieces = send_pieces(pieces, 1)
    got1 = swap(pack1, "lon", 1)
    result, adjoint, pack0 = call(
        first_back_kernel,
        far(*pieces, x, h1, scales, offsets) + block(0, inward, outward, expand) + far(upbias)
        + block(0, narrow) + far(downbias, *state0) + fixed("turn", "cut", "spread", "place", "sort"),
        [token, token, pack],
        (dbias, turned),
    )
    got0 = swap(pack0, "lon", 1)

    part = of((1, CHUNK, 2 * C), bf16)
    dealt = call(
        core_kernel,
        raw(pack0, pack1, got0, got1),
        [part] * 8,
        [pltpu.VMEM((8,) + part.shape, bf16)] * 3 + [pltpu.SemaphoreType.DMA((24,))],
        raw_outs=8,
    )
    over = lambda parts: [parts[0]] + [swap(parts[d], "rep", d) for d in (1, 2, 3)]
    give = call(add_kernel, near(*over(dealt[1::2])), [part], limit=SMALL)[0]
    a = call(add_kernel, near(*over(dealt[0::2]), swap(give, "lon", 2)), [part], limit=SMALL)[0][0]
    for step, height in ((1, CHUNK + 32), (4, CHUNK + 128)):
        others = [swap(a, "lat", step * i) for i in (1, 2, 3)]
        (a,) = call(band_kernel, near(a, *others), [of((height, 2 * C), bf16)], limit=SMALL)
    beside = swap(a, "lon", 2)
    a = jnp.stack([m for pair in zip(over([a] * 4), over([beside] * 4)) for m in pair]).reshape((4, 2) + a.shape)
    got = swap(a, "lon", 1)

    factor = 1.0 / math.sqrt(lax.axis_size("rep") * levels * total_rows * col_count * lax.axis_size("lon"))

    wide = [(2, C, 3 * C), (2, C, C), (2, C, FFN), (2, C, FFN), tables.shape]
    short = [(2, 2, C), (2, 2, C), (2, 3 * C), (2, C), (2, FFN), (2, C)]
    joined = call(
        functools.partial(final_kernel, factor),
        scalars[:1] + near(a, got),
        [of(m, f32) for m in wide + short],
        [pltpu.VMEM(m, f32) for m in wide]
        + [pltpu.VMEM((8 * ROWS, 2 * C), bf16), pltpu.SemaphoreType.DMA((10,))],
        raw_outs=5,
        limit=2 * SMALL,
    )
    inward_out, outward_out, expand_out, narrow_out, tables_out = joined[:5]
    scales_out, offsets_out, inbias_out, outbias_out, upbias_out, downbias_out = joined[5:]
    back = lambda m: m.reshape(row_count, col_count, levels, C).transpose(2, 0, 1, 3)[None]
    return (
        back(result), back(adjoint), scales_out, offsets_out, inward_out, inbias_out, outward_out, outbias_out,
        expand_out, upbias_out, jnp.swapaxes(narrow_out, 1, 2), downbias_out, jnp.swapaxes(tables_out, 1, 2),
    )


def solution(mesh):
    grid = P("rep", None, "lat", "lon", None)
    return jax.shard_map(
        body, mesh=mesh, in_specs=(grid, grid) + (P(),) * 13, out_specs=(grid, grid) + (P(),) * 11, check_vma=False
    )
```

```python
import functools
import math

import jax
import jax.numpy as jnp
import numpy as np
from jax import lax
from jax.experimental import pallas as pl
from jax.experimental.pallas import tpu as pltpu
from jax.sharding import PartitionSpec as P

C = 192
HEADS = 6
FFN = 768
TOK = 144
KEYS = 256
QUAD = 48
REL = 3312
ROWS = 144
CHUNK = ROWS + 16
HALF = 64
epsilon = 1e-05
masked = -1000000000.0
f32 = jnp.float32
bf16 = jnp.bfloat16
VMEM = 64 * 1024 * 1024
SMALL = 16 * 1024 * 1024


def constants():
    tok = np.arange(TOK)
    a, r, c = tok // 72, tok // 12 % 6, tok % 12
    turn = np.zeros((TOK, TOK), np.float32)
    turn[tok, (r * 12 + c) * 2 + a] = 1
    quad = np.where(r >= 3, 0, 1) + np.where(c >= 6, 0, 2)
    cut = np.zeros((4 * QUAD, TOK), np.float32)
    cut[quad * QUAD + a * 18 + r % 3 * 6 + c % 6, tok] = 1
    quad = np.where(r < 3, 0, 1) + np.where(c < 6, 0, 2)
    join = np.zeros((TOK, 4 * QUAD), np.float32)
    join[tok, quad * QUAD + (1 - a) * 18 + r % 3 * 6 + c % 6] = 1
    spread = np.zeros((256, 12 * 128), np.float32)
    for ci in range(12):
        for rj in range(6):
            for cj in range(12):
                spread[rj * 23 + ci - cj + 11, ci * 128 + rj * 12 + cj] = 1
    place = np.zeros((TOK, 192), np.float32)
    place[tok, c * 16 + a * 6 + r] = 1
    sort = np.zeros((192, 192), np.float32)
    for ai in range(2):
        for aj in range(2):
            for ri in range(6):
                for h in range(HEADS):
                    sort[(h * 2 + aj) * 16 + ai * 6 + ri, ((ai * 2 + aj) * 6 + ri) * 8 + h] = 1
    made = {"turn": turn, "cut": cut, "join": join, "place": place, "sort": sort}
    made = {name: jnp.asarray(m, f32) for name, m in made.items()}
    made["spread"] = jnp.asarray(spread, bf16)
    return made


def low(ref):
    return ref[...].astype(bf16)


def dot(x, y, dims=((1,), (0,))):
    return lax.dot_general(x, y, (dims, ((), ())), preferred_element_type=f32)


def dot_nt(x, y):
    return dot(x, y, ((1,), (1,)))


def dot_tn(x, y):
    return dot(x, y, ((0,), (0,)))


def norm_parts(values):
    centred = values - jnp.mean(values, axis=-1, keepdims=True)
    rstd = lax.rsqrt(jnp.mean(centred * centred, axis=-1, keepdims=True) + epsilon)
    return centred * rstd, rstd


def norm_fwd(values, gain, shift):
    return (norm_parts(values)[0] * gain + shift).astype(bf16)


def norm_bwd(values, gain, dy):
    hat, rstd = norm_parts(values)
    dhat = dy * gain
    first = jnp.mean(dhat, axis=-1, keepdims=True)
    second = jnp.mean(dhat * hat, axis=-1, keepdims=True)
    return rstd * (dhat - first - hat * second), colsum(dy * hat), colsum(dy)


def colsum(x):
    return jnp.sum(x, axis=0, keepdims=True)


def erf(x):
    return lax.erf(x)


def gelu_parts(z):
    cdf = 0.5 * (1.0 + erf(z * (2.0 ** -0.5)))
    return cdf, z * cdf


def pad_keys(x):
    blank = jnp.zeros((56, x.shape[1]), f32)
    return jnp.concatenate([x[:72], blank, x[72:], blank], axis=0)


def unpad_keys(x):
    return jnp.concatenate([x[:72], x[128:200]], axis=0)


def head_only(x, h):
    lane = lax.broadcasted_iota(jnp.int32, x.shape, 1)
    return jnp.where((lane >= 32 * h) & (lane < 32 * h + 32), x.astype(f32), 0.0).astype(bf16)


def join_rows(refs, part):
    return jnp.concatenate([ref[part * QUAD : (part + 1) * QUAD] for ref in refs], axis=0)


def write_pieces(first, second, refs):
    for i, ref in enumerate(refs):
        ref[:QUAD] = first[i * QUAD : (i + 1) * QUAD].astype(bf16)
        ref[QUAD:] = second[i * QUAD : (i + 1) * QUAD].astype(bf16)


def place_of():
    lon = lax.axis_index("lon")
    return lax.axis_index("lat"), lon & 1, lon >> 1, lax.axis_index("rep")


def key_mask(valid, band, shift):
    lane = lax.broadcasted_iota(jnp.int32, (1, KEYS), 1)
    column = lane & 127
    total_rows = valid.shape[0]
    last = jnp.where(band == total_rows // 6 - 1, 1, 0)
    allowed = jnp.zeros((1, KEYS), jnp.int32)
    for r in range(6):
        at = band * 6 + r + shift
        at = jnp.where(at >= total_rows, at - total_rows, at)
        hit = (column >= 12 * r) & (column < 12 * r + 12)
        allowed = allowed + jnp.where(hit, valid[at], 0)
    if shift:
        row = lax.broadcasted_iota(jnp.int32, (TOK, KEYS), 0)
        wide = lax.broadcasted_iota(jnp.int32, (TOK, KEYS), 1)
        row_level = jnp.where(row >= 72, 1, 0)
        key_level = wide >> 7
        row_part = jnp.where(row - 72 * row_level >= 36, 1, 0)
        key_part = jnp.where((wide & 127) >= 36, 1, 0)
        apart = (row_level ^ key_level) | ((row_part ^ key_part) & last)
        allowed = jnp.where(apart == 0, jnp.broadcast_to(allowed, (TOK, KEYS)), 0)
        column = wide & 127
    mask = jnp.where(allowed > 0, 0.0, masked)
    return jnp.where(column < 72, mask, 2 * masked)


def make_bias(k, types, valid, tables, spread, place, sort, bias_ref, turn_ref, row_ref):
    row_ref[...] = jnp.zeros(row_ref.shape, f32)
    band = place_of()[0]
    kind = types[k, 0, band]
    for h in range(HEADS):
        row_ref[h : h + 1, :REL] = tables[0, h, pl.ds(kind, 1), :]
    wide_rows = row_ref[...]
    rest = jnp.concatenate([wide_rows[:, 138 * i : 138 * i + 256] for i in range(24)], axis=0)
    total = None
    for _ in range(3):
        part = rest.astype(bf16)
        rest = rest - part.astype(f32)
        wide = dot(dot(sort, part).astype(bf16), spread)
        for g in range(12):
            for ci in range(12):
                turn_ref[ci * 16 : ci * 16 + 16, g * 128 : g * 128 + 128] = wide[
                    g * 16 : g * 16 + 16, ci * 128 : ci * 128 + 128
                ].astype(bf16)
        here = dot(place, turn_ref[...])
        total = here if total is None else total + here
    mask = key_mask(valid, band, 3 * k)
    for h in range(HEADS):
        bias_ref[:, h * KEYS : (h + 1) * KEYS] = total[:, h * KEYS : (h + 1) * KEYS] + mask


def table_adjoint(dbias, spread, place, sort, turn_ref):
    rows = dot_tn(place, dbias)
    for g in range(12):
        for ci in range(12):
            turn_ref[g * 16 : g * 16 + 16, ci * 128 : ci * 128 + 128] = rows[
                ci * 16 : ci * 16 + 16, g * 128 : g * 128 + 128
            ].astype(bf16)
    narrow = dot_nt(turn_ref[...], spread).astype(bf16)
    rows = dot_tn(sort, narrow)
    pieces = [rows[8 * i : 8 * i + 8, :138] for i in range(24)]
    return jnp.concatenate(pieces + [jnp.zeros((8, 16), f32)], axis=1)


def put(pack, at, value):
    done = 0
    while done < value.shape[0]:
        chunk, row = divmod(at + done, ROWS)
        size = min(ROWS - row, value.shape[0] - done)
        pack[chunk, row : row + size] = value[done : done + size].astype(bf16)
        done += size


def put_rest(pack, table, small):
    row = lax.broadcasted_iota(jnp.int32, (8, 2 * C), 0)
    for chunk in range(8):
        own = table[:, 384 * chunk : 384 * chunk + 384]
        if chunk < 2:
            left = table[:, 3072 + 128 * chunk : 3200 + 128 * chunk]
            moved = [pltpu.roll(left, 6 - 2 * i, 0) if i < 3 else left for i in range(3)]
            own = jnp.where(row >= 6, jnp.concatenate(moved, axis=1), own)
        short = jnp.where(row == 0, small[chunk], 0.0) if chunk < len(small) else jnp.zeros((8, 2 * C), f32)
        pack[chunk, ROWS : ROWS + 16] = jnp.concatenate([own, short], axis=0).astype(bf16)


def attend_fwd(k, u, inward, inbias, outward, outbias, bias_ref, q_ref, k_ref, v_ref, p_ref, mix_ref):
    weight = inward[0].astype(bf16)
    shift = inbias[k : k + 1]
    keyed = pad_keys(u.astype(f32)).astype(bf16)
    q = (dot(u, weight[:, :C]) + shift[:, :C]).astype(bf16)
    key = (dot(keyed, weight[:, C : 2 * C]) + shift[:, C : 2 * C]).astype(bf16)
    v = (dot(keyed, weight[:, 2 * C :]) + shift[:, 2 * C :]).astype(bf16)
    q_ref[...] = q
    k_ref[...] = key
    v_ref[...] = v
    mix = jnp.zeros((TOK, C), f32)
    for h in range(HEADS):
        scores = dot_nt(head_only(q, h), key) * 32 ** (-0.5) + bias_ref[:, h * KEYS : (h + 1) * KEYS]
        weights = jnp.exp(scores - jnp.max(scores, axis=-1, keepdims=True))
        chances = (weights / jnp.sum(weights, axis=-1, keepdims=True)).astype(bf16)
        p_ref[h] = chances
        mix = mix + dot(chances, head_only(v, h))
    mix = mix.astype(bf16)
    mix_ref[...] = mix
    return (dot(mix, outward[0].astype(bf16)) + outbias[k : k + 1]).astype(bf16)


def attend_bwd(dout, u, inward, outward, spread, place, sort, q_ref, k_ref, v_ref, p_ref, mix_ref, pack, dbias_ref, turn_ref):
    q, key, v, mix = q_ref[...], k_ref[...], v_ref[...], mix_ref[...]
    weight = inward[0].astype(bf16)
    dmix = dot_nt(dout, outward[0].astype(bf16)).astype(bf16)
    dq = jnp.zeros((TOK, C), f32)
    dk = jnp.zeros((KEYS, C), f32)
    dv = jnp.zeros((KEYS, C), f32)
    for h in range(HEADS):
        chances = p_ref[h]
        wide = chances.astype(f32)
        dmix_h = head_only(dmix, h)
        dchances = dot_nt(dmix_h, v)
        dscores = wide * (dchances - jnp.sum(wide * dchances, axis=-1, keepdims=True))
        narrow = dscores.astype(bf16)
        dbias_ref[:, h * KEYS : (h + 1) * KEYS] = narrow
        dv = dv + dot_tn(chances, dmix_h)
        dq = dq + dot(narrow, head_only(key, h))
        dk = dk + dot_tn(narrow, head_only(q, h))
    dq = (dq * 32 ** (-0.5)).astype(bf16)
    dk = (dk * 32 ** (-0.5)).astype(bf16)
    dv = dv.astype(bf16)
    keyed = pad_keys(u.astype(f32)).astype(bf16)
    du = dot_nt(dq, weight[:, :C]) + unpad_keys(
        dot_nt(dk, weight[:, C : 2 * C]) + dot_nt(dv, weight[:, 2 * C :])
    )
    pair = lambda x, y: jnp.concatenate([x, y], axis=1)
    put(pack, 4 * C, pair(dot_tn(u, dq), dot_tn(keyed, dk)))
    put(pack, 5 * C, pair(dot_tn(keyed, dv), dot_tn(mix, dout)))
    small = [
        pair(colsum(dq.astype(f32)), colsum(dk.astype(f32))),
        pair(colsum(dv.astype(f32)), colsum(dout.astype(f32))),
    ]
    return du, table_adjoint(dbias_ref[...], spread, place, sort, turn_ref), small


def mlp_fwd(h, gain, shift, expand, upbias, narrow_t, downbias):
    z = dot(norm_fwd(h, gain, shift), expand) + upbias
    hidden = gelu_parts(z)[1].astype(bf16)
    return (h + dot_nt(hidden, narrow_t) + downbias).astype(bf16)


def mlp_both(h, gain, shift, expand, upbias, narrow_t, downbias, dout, want):
    normed = norm_fwd(h, gain, shift)
    z = dot(normed, expand) + upbias
    cdf, wide = gelu_parts(z)
    hidden = wide.astype(bf16)
    result = None
    if want:
        result = (h + dot_nt(hidden, narrow_t) + downbias).astype(bf16)
    slope = cdf + z * jnp.exp(-0.5 * z * z) * (1.0 / math.sqrt(2.0 * math.pi))
    dz32 = dot(dout, narrow_t) * slope
    dz = dz32.astype(bf16)
    dnormed = dot_nt(dz, expand).astype(bf16).astype(f32)
    dx, dgain, dshift = norm_bwd(h, gain, dnormed)
    dwide = dout.astype(f32)
    dh = (dwide + dx).astype(bf16)
    dexpand = dot_tn(normed, dz)
    dnarrow = dot_tn(dout, hidden)
    dense = [dexpand[:, : 2 * C], dexpand[:, 2 * C :], dnarrow[:, : 2 * C], dnarrow[:, 2 * C :]]
    dup = colsum(dz32)
    small = [
        dup[:, : 2 * C],
        dup[:, 2 * C :],
        jnp.concatenate([colsum(dwide), dgain], axis=1),
        jnp.concatenate([dshift, jnp.zeros((1, C), f32)], axis=1),
    ]
    return result, dh, dense, small


def bias_kernel(types, valid, tables, spread, place, sort, bias_ref, turned, rows):
    make_bias(1, types, valid, tables, spread[...], low(place), low(sort), bias_ref, turned, rows)


def first_kernel(
    types, valid, fields, upstream, scales, offsets, inward, inbias, outward, outbias, expand, upbias, narrow, downbias,
    tables, turn, cut, spread, place, sort,
    q, k, v, p, mix, h1, pa, pb, pc, pd, bias, turned, rows,
):
    make_bias(0, types, valid, tables, spread[...], low(place), low(sort), bias, turned, rows)
    order, route = low(turn), low(cut)
    x = dot(order, fields[...])
    u = norm_fwd(x, scales[0, 0:1], offsets[0, 0:1])
    branch = attend_fwd(0, u, inward, inbias, outward, outbias, bias, q, k, v, p, mix)
    carried = (x + branch.astype(f32)).astype(bf16)
    h1[...] = carried
    out = mlp_fwd(
        carried.astype(f32), scales[0, 1:2], offsets[0, 1:2], expand[0].astype(bf16), upbias[0:1],
        narrow[0].astype(bf16), downbias[0:1],
    )
    cotangent = dot(order, upstream[...]).astype(bf16)
    write_pieces(dot(route, out), dot(route, cotangent), (pa, pb, pc, pd))


def second_kernel(
    qa, qb, qc, qd, scales, offsets, inward, inbias, outward, outbias, expand, upbias, narrow, downbias,
    bias, join, spread, place, sort,
    pack, pa, pb, pc, pd, q, k, v, p, mix, dbias, turned,
):
    route = low(join)
    pieces = (qa, qb, qc, qd)
    y1 = dot(route, join_rows(pieces, 0))
    cotangent = dot(route, join_rows(pieces, 1)).astype(bf16)
    u = norm_fwd(y1, scales[1, 0:1], offsets[1, 0:1])
    branch = attend_fwd(1, u, inward, inbias, outward, outbias, bias, q, k, v, p, mix)
    h2 = (y1 + branch.astype(f32)).astype(bf16).astype(f32)
    out, dh, dense, short = mlp_both(
        h2, scales[1, 1:2], offsets[1, 1:2], expand[0].astype(bf16), upbias[1:2],
        narrow[0].astype(bf16), downbias[1:2], cotangent, True,
    )
    for i, part in enumerate(dense):
        put(pack, i * C, part)
    du, table, small = attend_bwd(
        dh, u, inward, outward, spread[...], low(place), low(sort), q, k, v, p, mix, pack, dbias, turned
    )
    dx, dgain, dshift = norm_bwd(y1, scales[1, 0:1], du.astype(bf16).astype(f32))
    dy1 = (dh.astype(f32) + dx.astype(bf16).astype(f32)).astype(bf16)
    put_rest(pack, table, short + small + [jnp.concatenate([dgain, dshift], axis=1)])
    write_pieces(dot_tn(route, dy1), dot_tn(route, out), (pa, pb, pc, pd))


def first_back_kernel(
    qa, qb, qc, qd, fields, h1, scales, offsets, inward, outward, expand, upbias, narrow, downbias,
    q, k, v, p, mix, turn, cut, spread, place, sort,
    result, adjoint, pack, dbias, turned,
):
    order, route = low(turn), low(cut)
    pieces = (qa, qb, qc, qd)
    result[...] = dot_tn(order, dot_tn(route, join_rows(pieces, 1)).astype(bf16)).astype(bf16)
    dy1 = dot_tn(route, join_rows(pieces, 0)).astype(bf16)
    _, dh1, dense, short = mlp_both(
        h1[...].astype(f32), scales[0, 1:2], offsets[0, 1:2], expand[0].astype(bf16), upbias[0:1],
        narrow[0].astype(bf16), downbias[0:1], dy1, False,
    )
    for i, part in enumerate(dense):
        put(pack, i * C, part)
    x = dot(order, fields[...])
    u = norm_fwd(x, scales[0, 0:1], offsets[0, 0:1])
    du, table, small = attend_bwd(
        dh1, u, inward, outward, spread[...], low(place), low(sort), q, k, v, p, mix, pack, dbias, turned
    )
    dx0, dgain0, dshift0 = norm_bwd(x, scales[0, 0:1], du.astype(bf16).astype(f32))
    adjoint[...] = dot_tn(order, (dh1.astype(f32) + dx0).astype(bf16)).astype(bf16)
    put_rest(pack, table, short + small + [jnp.concatenate([dgain0, dshift0], axis=1)])


def core_kernel(first, second, got_first, got_second, *refs):
    outs, (own, got, made, sems) = refs[:8], refs[8:]
    _, core, side, rep = place_of()
    part = lambda n: pl.ds((rep ^ (n // 2)) * 2 + (side ^ (n % 2)), 1)
    order = (5, 3, 7, 1, 4, 2, 6, 0)
    for k, (mine, theirs) in enumerate(((first, got_first), (second, got_second))):

        @pl.when(core == k)
        def _(mine=mine, theirs=theirs):
            for n in order:
                pltpu.make_async_copy(mine.at[part(n)], own.at[n], sems.at[n]).start()
                pltpu.make_async_copy(theirs.at[part(n)], got.at[n], sems.at[8 + n]).start()

    sent = []
    for n in order:
        pltpu.make_async_copy(first.at[part(n)], own.at[n], sems.at[n]).wait()
        pltpu.make_async_copy(got_first.at[part(n)], got.at[n], sems.at[8 + n]).wait()
        made[n] = (own[n].astype(f32) + got[n].astype(f32)).astype(bf16)
        sent.append(pltpu.make_async_copy(made.at[n], outs[n], sems.at[16 + n]))
        sent[-1].start()
    for copy in sent:
        copy.wait()


def add_kernel(*refs):
    total = refs[0][...].astype(f32)
    for ref in refs[1:-1]:
        total = total + ref[...].astype(f32)
    refs[-1][...] = total.astype(bf16)


def add(refs):
    total = refs[0][...].astype(f32)
    for ref in refs[1:]:
        total = total + ref[...].astype(f32)
    return total


def split_kernel(*refs):
    total = add(refs[:-2])[0]
    a, b = refs[-2:]
    a[:HALF] = total[:HALF].astype(bf16)
    a[HALF:] = total[ROWS:].astype(bf16)
    b[...] = total[HALF:ROWS].astype(bf16)


def near_bands_kernel(*refs):
    total = add(refs[:4])
    a, b = refs[8:]
    a[:HALF] = total[:HALF].astype(bf16)
    aside = jnp.concatenate([total[HALF + 8 :], jnp.zeros((8, 2 * C), f32)], axis=0)
    a[HALF : HALF + 16] = aside.astype(bf16)
    rows = [ref[HALF : HALF + 16].astype(f32)[:8] for ref in refs[:4]]
    a[HALF + 16 :] = jnp.concatenate(rows, axis=0).astype(bf16)
    b[...] = add(refs[4:8]).astype(bf16)


def far_bands_kernel(*refs):
    out = refs[8]
    total = refs[0][: HALF + 16].astype(f32)
    for ref in refs[1:4]:
        total = total + ref[: HALF + 16].astype(f32)
    out[:HALF] = total[:HALF].astype(bf16)
    out[HALF:ROWS] = add(refs[4:8]).astype(bf16)
    out[ROWS:CHUNK] = total[HALF:].astype(bf16)
    for i, ref in enumerate(refs[:4]):
        out[CHUNK + 32 * i : CHUNK + 32 * i + 32] = ref[HALF + 16 :]


def final_kernel(factor, types, own_near, own_far, got_near, got_far, *refs):
    own, got = (own_near, own_far), (got_near, got_far)
    big, short = refs[:5], refs[5:11]
    inward, outward, expand, narrow, tables, dense, sems = refs[11:]
    scales, offsets, inbias, outbias, upbias, downbias = short
    band, core, side, rep = place_of()
    lane = lax.broadcasted_iota(jnp.int32, (1, 128), 1)
    row = lax.broadcasted_iota(jnp.int32, (96, 128), 0)
    part = lax.broadcasted_iota(jnp.int32, (96, 128), 1) & 7
    head = row >> 4

    def unpack(k, sides, s):
        kind = jnp.zeros((1, 128), jnp.int32)
        for e in range(16):
            kind = kind + jnp.where((lane >> 3) == e, types[k, 0, band ^ e], 0)
        match = (row & 15) == kind
        made = [match & (part == head)]
        for i in range(3):
            made.append(match & ((head >> 1) == i) & (part == 6 + (head & 1)))
        route = [jnp.where(m, 1.0, 0.0).astype(bf16) for m in made]
        small = []
        for chunk in range(8):
            y, ref = rep ^ (chunk // 2), sides[s ^ (chunk % 2)]
            dense[chunk * ROWS : (chunk + 1) * ROWS] = ref[y, :ROWS]
            small.append(ref[y, ROWS:CHUNK].astype(f32)[0:1] * factor)
            here = ref[y, CHUNK:]
            rows = dot(route[0], here) * factor
            for h in range(HEADS):
                tables[k, h, :, 384 * chunk : 384 * chunk + 384] = rows[16 * h : 16 * h + 16]
            if chunk < 2:
                left = sum(dot(route[1 + i], here[:, 128 * i : 128 * i + 128]) for i in range(3)) * factor
                start = 3072 + 128 * chunk
                size = min(128, REL - start)
                for h in range(HEADS):
                    tables[k, h, :, start : start + size] = left[16 * h : 16 * h + 16, :size]
        load = lambda i: dense[i * C : (i + 1) * C].astype(f32) * factor
        expand[k, :, : 2 * C] = load(0)
        expand[k, :, 2 * C :] = load(1)
        narrow[k, :, : 2 * C] = load(2)
        narrow[k, :, 2 * C :] = load(3)
        inward[k, :, : 2 * C] = load(4)
        both = load(5)
        inward[k, :, 2 * C :] = both[:, :C]
        outward[k] = both[:, C:]
        upbias[k : k + 1, : 2 * C] = small[0]
        upbias[k : k + 1, 2 * C :] = small[1]
        downbias[k : k + 1] = small[2][:, :C]
        scales[k, 1:2] = small[2][:, C:]
        offsets[k, 1:2] = small[3][:, :C]
        inbias[k : k + 1, : 2 * C] = small[4]
        inbias[k : k + 1, 2 * C :] = small[5][:, :C]
        outbias[k : k + 1] = small[5][:, C:]
        scales[k, 0:1] = small[6][:, :C]
        offsets[k, 0:1] = small[6][:, C:]

    sent = []
    for k in range(2):
        for source, wanted in ((own, core == k), (got, core != k)):

            for s in range(2):

                @pl.when(wanted & (side == s))
                def _(k=k, source=source, s=s):
                    unpack(k, source, s)

        for n, array in enumerate((inward, outward, expand, narrow, tables)):
            sent.append(pltpu.make_async_copy(array.at[k], big[n].at[k], sems.at[5 * k + n]))
            sent[-1].start()
    for copy in sent:
        copy.wait()


def call(kernel, ins, outs, scratch=(), far_outs=0, raw_outs=0, aliases={}, limit=VMEM):
    specs, fetched, slots = [], [], []
    for array, block, far in ins:
        dims = array.ndim
        shape = array.shape if block in (None, "smem", "raw") else (1,) + array.shape[1:]
        if block == "smem":
            specs.append(pl.BlockSpec(memory_space=pltpu.SMEM))
        elif block == "raw":
            specs.append(pl.BlockSpec(memory_space=pltpu.HBM))
        elif far:
            specs.append(pl.BlockSpec(memory_space=pltpu.HBM))
            fetched.append((len(specs) - 1, block))
            slots.append(pltpu.VMEM(shape, array.dtype))
        else:
            specs.append(pl.BlockSpec(array.shape, lambda i, dims=dims: (0,) * dims))
    out_specs = []
    for i, o in enumerate(outs):
        if i < raw_outs:
            out_specs.append(pl.BlockSpec(memory_space=pltpu.HBM))
        elif i < far_outs:
            out_specs.append(pl.BlockSpec(memory_space=pltpu.HBM))
            slots.append(pltpu.VMEM(o.shape, o.dtype))
        else:
            out_specs.append(pl.BlockSpec(o.shape, lambda i, dims=len(o.shape): (0,) * dims))

    def wrapped(*refs):
        in_refs, refs = list(refs[: len(ins)]), refs[len(ins) :]
        out_refs, refs = list(refs[: len(outs)]), refs[len(outs) :]
        own, refs = refs[: len(scratch)], refs[len(scratch) :]
        copies = []
        for n, (at, block) in enumerate(fetched):
            source = in_refs[at] if block is None else in_refs[at].at[block : block + 1]
            copies.append(pltpu.make_async_copy(source, refs[n], refs[-1].at[n]))
            in_refs[at] = refs[n]
        for copy in copies:
            copy.start()
        for copy in copies:
            copy.wait()
        targets = out_refs[:far_outs]
        out_refs[:far_outs] = refs[len(fetched) : len(fetched) + far_outs]
        kernel(*in_refs, *out_refs, *own)
        copies = [
            pltpu.make_async_copy(out_refs[n], targets[n], refs[-1].at[len(fetched) + n]) for n in range(far_outs)
        ]
        for copy in copies:
            copy.start()
        for copy in copies:
            copy.wait()

    size = lambda s: math.prod(s.shape) * jnp.dtype(s.dtype).itemsize
    moved = sum(size(o) for o in outs) + sum(size(a) for a, b, _ in ins)
    if slots:
        slots.append(pltpu.SemaphoreType.DMA((len(slots),)))
    return pl.pallas_call(
        wrapped,
        grid=(1,),
        in_specs=specs,
        out_specs=out_specs,
        out_shape=outs,
        scratch_shapes=list(scratch) + slots,
        input_output_aliases=aliases,
        compiler_params=pltpu.CompilerParams(vmem_limit_bytes=limit),
        cost_estimate=pl.CostEstimate(flops=10**9, bytes_accessed=moved, transcendentals=0),
    )(*[array for array, _, _ in ins])


def send_pieces(pieces, step):
    lat, lon = lax.axis_size("lat"), lax.axis_size("lon")
    rows = [(i, (i + step) % lat) for i in range(lat)]
    cols = [(i, (i + step) % lon) for i in range(lon)]
    both = [(i * lon + j, (i + step) % lat * lon + (j + step) % lon) for i in range(lat) for j in range(lon)]
    return (
        pieces[0],
        lax.ppermute(pieces[1], "lat", rows),
        lax.ppermute(pieces[2], "lon", cols),
        lax.ppermute(pieces[3], ("lat", "lon"), both),
    )


def swap(array, axis, distance):
    return lax.ppermute(array, axis, [(i, i ^ distance) for i in range(lax.axis_size(axis))])


def body(
    fields, upstream, scales, offsets, inward, inbias, outward, outbias, expand, upbias, narrow, downbias,
    tables, window_type, row_valid,
):
    const = constants()
    levels, row_count, col_count = fields.shape[1:4]
    total_rows = row_valid.shape[0]
    x = fields[0].transpose(1, 2, 0, 3).reshape(TOK, C)
    cotangent = upstream[0].transpose(1, 2, 0, 3).reshape(TOK, C)
    narrow = jnp.swapaxes(narrow, 1, 2)
    tables = jnp.swapaxes(tables, 1, 2)
    of = jax.ShapeDtypeStruct
    piece = [of((2 * QUAD, C), bf16)] * 4
    token = of((TOK, C), bf16)
    state = [token, of((KEYS, C), bf16), of((KEYS, C), bf16), of((HEADS, TOK, KEYS), bf16), token]
    pack = of((8, CHUNK, 2 * C), bf16)
    turned = pltpu.VMEM((192, 1536), bf16)
    dbias = pltpu.VMEM((TOK, 1536), bf16)
    rows = pltpu.VMEM((8, 3456), f32)
    near = lambda *arrays: [(m, None, False) for m in arrays]
    far = lambda *arrays: [(m, None, True) for m in arrays]
    block = lambda k, *arrays: [(m, k, True) for m in arrays]
    raw = lambda *arrays: [(m, "raw", True) for m in arrays]
    fixed = lambda *names: far(*[const[name] for name in names])
    scalars = [(window_type, "smem", False), (row_valid, "smem", False)]

    def weights(k):
        return (
            far(scales, offsets) + block(k, inward) + far(inbias) + block(k, outward) + far(outbias)
            + block(k, expand) + far(upbias) + block(k, narrow) + far(downbias)
        )

    *state0, h1, pa, pb, pc, pd = call(
        first_kernel,
        scalars + far(x, cotangent) + weights(0) + block(0, tables) + fixed("turn", "cut", "spread", "place", "sort"),
        state + [token] + piece,
        (pltpu.VMEM((TOK, 1536), f32), turned, rows),
        6,
    )
    pieces = send_pieces((pa, pb, pc, pd), -1)
    (bias1,) = call(
        bias_kernel,
        scalars + block(1, tables) + fixed("spread", "place", "sort"),
        [of((TOK, 1536), f32)],
        (turned, rows),
    )
    pack1, *pieces = call(
        second_kernel,
        far(*pieces) + weights(1) + far(bias1) + fixed("join", "spread", "place", "sort"),
        [pack] + piece,
        [pltpu.VMEM(m.shape, m.dtype) for m in state] + [dbias, turned],
    )
    pieces = send_pieces(pieces, 1)
    got1 = swap(pack1, "lon", 1)
    result, adjoint, pack0 = call(
        first_back_kernel,
        far(*pieces, x, h1, scales, offsets) + block(0, inward, outward, expand) + far(upbias)
        + block(0, narrow) + far(downbias, *state0) + fixed("turn", "cut", "spread", "place", "sort"),
        [token, token, pack],
        (dbias, turned),
    )
    got0 = swap(pack0, "lon", 1)

    part = of((1, CHUNK, 2 * C), bf16)
    dealt = call(
        core_kernel,
        raw(pack0, pack1, got0, got1),
        [part] * 8,
        [pltpu.VMEM((8,) + part.shape, bf16)] * 3 + [pltpu.SemaphoreType.DMA((24,))],
        raw_outs=8,
    )
    over = lambda parts: [parts[0]] + [swap(parts[d], "rep", d) for d in (1, 2, 3)]
    give = call(add_kernel, near(*over(dealt[1::2])), [part], limit=SMALL)[0]
    first = of((HALF + 16, 2 * C), bf16)
    a, b = call(split_kernel, near(*over(dealt[0::2]), swap(give, "lon", 2)), [first, first], limit=SMALL)
    bands = lambda m, step: [m] + [swap(m, "lat", step * i) for i in (1, 2, 3)]
    a, b = call(
        near_bands_kernel,
        near(*bands(a, 1), *bands(b, 4)),
        [of((HALF + 48, 2 * C), bf16), first],
        limit=SMALL,
    )
    (a,) = call(
        far_bands_kernel, near(*bands(a, 4), *bands(b, 1)), [of((CHUNK + 128, 2 * C), bf16)], limit=SMALL
    )
    beside = swap(a, "lon", 2)
    own = [jnp.stack(over([m] * 4)) for m in (a, beside)]
    got = [swap(m, "lon", 1) for m in own]

    factor = 1.0 / math.sqrt(lax.axis_size("rep") * levels * total_rows * col_count * lax.axis_size("lon"))

    wide = [(2, C, 3 * C), (2, C, C), (2, C, FFN), (2, C, FFN), tables.shape]
    short = [(2, 2, C), (2, 2, C), (2, 3 * C), (2, C), (2, FFN), (2, C)]
    joined = call(
        functools.partial(final_kernel, factor),
        scalars[:1] + near(*own, *got),
        [of(m, f32) for m in wide + short],
        [pltpu.VMEM(m, f32) for m in wide]
        + [pltpu.VMEM((8 * ROWS, 2 * C), bf16), pltpu.SemaphoreType.DMA((10,))],
        raw_outs=5,
        limit=2 * SMALL,
    )
    inward_out, outward_out, expand_out, narrow_out, tables_out = joined[:5]
    scales_out, offsets_out, inbias_out, outbias_out, upbias_out, downbias_out = joined[5:]
    back = lambda m: m.reshape(row_count, col_count, levels, C).transpose(2, 0, 1, 3)[None]
    return (
        back(result), back(adjoint), scales_out, offsets_out, inward_out, inbias_out, outward_out, outbias_out,
        expand_out, upbias_out, jnp.swapaxes(narrow_out, 1, 2), downbias_out, jnp.swapaxes(tables_out, 1, 2),
    )


def solution(mesh):
    grid = P("rep", None, "lat", "lon", None)
    return jax.shard_map(
        body, mesh=mesh, in_specs=(grid, grid) + (P(),) * 13, out_specs=(grid, grid) + (P(),) * 11, check_vma=False
    )
```

```python
import functools
import math

import jax
import jax.numpy as jnp
import numpy as np
from jax import lax
from jax.experimental import pallas as pl
from jax.experimental.pallas import tpu as pltpu
from jax.sharding import PartitionSpec as P

C = 192
HEADS = 6
FFN = 768
TOK = 144
KEYS = 256
QUAD = 48
REL = 3312
ROWS = 144
CHUNK = ROWS + 16
epsilon = 1e-05
masked = -1000000000.0
f32 = jnp.float32
bf16 = jnp.bfloat16
VMEM = 64 * 1024 * 1024
SMALL = 16 * 1024 * 1024


def constants():
    tok = np.arange(TOK)
    a, r, c = tok // 72, tok // 12 % 6, tok % 12
    turn = np.zeros((TOK, TOK), np.float32)
    turn[tok, (r * 12 + c) * 2 + a] = 1
    quad = np.where(r >= 3, 0, 1) + np.where(c >= 6, 0, 2)
    cut = np.zeros((4 * QUAD, TOK), np.float32)
    cut[quad * QUAD + a * 18 + r % 3 * 6 + c % 6, tok] = 1
    quad = np.where(r < 3, 0, 1) + np.where(c < 6, 0, 2)
    join = np.zeros((TOK, 4 * QUAD), np.float32)
    join[tok, quad * QUAD + (1 - a) * 18 + r % 3 * 6 + c % 6] = 1
    spread = np.zeros((256, 12 * 128), np.float32)
    for ci in range(12):
        for rj in range(6):
            for cj in range(12):
                spread[rj * 23 + ci - cj + 11, ci * 128 + rj * 12 + cj] = 1
    place = np.zeros((TOK, 192), np.float32)
    place[tok, c * 16 + a * 6 + r] = 1
    sort = np.zeros((192, 192), np.float32)
    for ai in range(2):
        for aj in range(2):
            for ri in range(6):
                for h in range(HEADS):
                    sort[(h * 2 + aj) * 16 + ai * 6 + ri, ((ai * 2 + aj) * 6 + ri) * 8 + h] = 1
    made = {"turn": turn, "cut": cut, "join": join, "place": place, "sort": sort}
    made = {name: jnp.asarray(m, f32) for name, m in made.items()}
    made["spread"] = jnp.asarray(spread, bf16)
    return made


def low(ref):
    return ref[...].astype(bf16)


def dot(x, y, dims=((1,), (0,))):
    return lax.dot_general(x, y, (dims, ((), ())), preferred_element_type=f32)


def dot_nt(x, y):
    return dot(x, y, ((1,), (1,)))


def dot_tn(x, y):
    return dot(x, y, ((0,), (0,)))


def norm_parts(values):
    centred = values - jnp.mean(values, axis=-1, keepdims=True)
    rstd = lax.rsqrt(jnp.mean(centred * centred, axis=-1, keepdims=True) + epsilon)
    return centred * rstd, rstd


def norm_fwd(values, gain, shift):
    return (norm_parts(values)[0] * gain + shift).astype(bf16)


def norm_bwd(values, gain, dy):
    hat, rstd = norm_parts(values)
    dhat = dy * gain
    first = jnp.mean(dhat, axis=-1, keepdims=True)
    second = jnp.mean(dhat * hat, axis=-1, keepdims=True)
    return rstd * (dhat - first - hat * second), colsum(dy * hat), colsum(dy)


def colsum(x):
    return jnp.sum(x, axis=0, keepdims=True)


def erf(x):
    return lax.erf(x)


def gelu_parts(z):
    cdf = 0.5 * (1.0 + erf(z * (2.0 ** -0.5)))
    return cdf, z * cdf


def pad_keys(x):
    blank = jnp.zeros((56, x.shape[1]), f32)
    return jnp.concatenate([x[:72], blank, x[72:], blank], axis=0)


def unpad_keys(x):
    return jnp.concatenate([x[:72], x[128:200]], axis=0)


def head_only(x, h):
    lane = lax.broadcasted_iota(jnp.int32, x.shape, 1)
    return jnp.where((lane >= 32 * h) & (lane < 32 * h + 32), x.astype(f32), 0.0).astype(bf16)


def join_rows(refs, part):
    return jnp.concatenate([ref[part * QUAD : (part + 1) * QUAD] for ref in refs], axis=0)


def write_pieces(first, second, refs):
    for i, ref in enumerate(refs):
        ref[:QUAD] = first[i * QUAD : (i + 1) * QUAD].astype(bf16)
        ref[QUAD:] = second[i * QUAD : (i + 1) * QUAD].astype(bf16)


def place_of():
    lon = lax.axis_index("lon")
    return lax.axis_index("lat"), lon & 1, lon >> 1, lax.axis_index("rep")


def key_mask(valid, band, shift):
    lane = lax.broadcasted_iota(jnp.int32, (1, KEYS), 1)
    column = lane & 127
    total_rows = valid.shape[0]
    last = jnp.where(band == total_rows // 6 - 1, 1, 0)
    allowed = jnp.zeros((1, KEYS), jnp.int32)
    for r in range(6):
        at = band * 6 + r + shift
        at = jnp.where(at >= total_rows, at - total_rows, at)
        hit = (column >= 12 * r) & (column < 12 * r + 12)
        allowed = allowed + jnp.where(hit, valid[at], 0)
    if shift:
        row = lax.broadcasted_iota(jnp.int32, (TOK, KEYS), 0)
        wide = lax.broadcasted_iota(jnp.int32, (TOK, KEYS), 1)
        row_level = jnp.where(row >= 72, 1, 0)
        key_level = wide >> 7
        row_part = jnp.where(row - 72 * row_level >= 36, 1, 0)
        key_part = jnp.where((wide & 127) >= 36, 1, 0)
        apart = (row_level ^ key_level) | ((row_part ^ key_part) & last)
        allowed = jnp.where(apart == 0, jnp.broadcast_to(allowed, (TOK, KEYS)), 0)
        column = wide & 127
    mask = jnp.where(allowed > 0, 0.0, masked)
    return jnp.where(column < 72, mask, 2 * masked)


def make_bias(k, types, valid, tables, spread, place, sort, bias_ref, turn_ref, row_ref):
    row_ref[...] = jnp.zeros(row_ref.shape, f32)
    band = place_of()[0]
    kind = types[k, 0, band]
    for h in range(HEADS):
        row_ref[h : h + 1, :REL] = tables[0, h, pl.ds(kind, 1), :]
    wide_rows = row_ref[...]
    rest = jnp.concatenate([wide_rows[:, 138 * i : 138 * i + 256] for i in range(24)], axis=0)
    total = None
    for _ in range(3):
        part = rest.astype(bf16)
        rest = rest - part.astype(f32)
        wide = dot(dot(sort, part).astype(bf16), spread)
        for g in range(12):
            for ci in range(12):
                turn_ref[ci * 16 : ci * 16 + 16, g * 128 : g * 128 + 128] = wide[
                    g * 16 : g * 16 + 16, ci * 128 : ci * 128 + 128
                ].astype(bf16)
        here = dot(place, turn_ref[...])
        total = here if total is None else total + here
    mask = key_mask(valid, band, 3 * k)
    for h in range(HEADS):
        bias_ref[:, h * KEYS : (h + 1) * KEYS] = total[:, h * KEYS : (h + 1) * KEYS] + mask


def table_adjoint(dbias, spread, place, sort, turn_ref):
    rows = dot_tn(place, dbias)
    for g in range(12):
        for ci in range(12):
            turn_ref[g * 16 : g * 16 + 16, ci * 128 : ci * 128 + 128] = rows[
                ci * 16 : ci * 16 + 16, g * 128 : g * 128 + 128
            ].astype(bf16)
    narrow = dot_nt(turn_ref[...], spread).astype(bf16)
    rows = dot_tn(sort, narrow)
    pieces = [rows[8 * i : 8 * i + 8, :138] for i in range(24)]
    return jnp.concatenate(pieces + [jnp.zeros((8, 16), f32)], axis=1)


def put(pack, at, value):
    done = 0
    while done < value.shape[0]:
        chunk, row = divmod(at + done, ROWS)
        size = min(ROWS - row, value.shape[0] - done)
        pack[chunk, row : row + size] = value[done : done + size].astype(bf16)
        done += size


def put_rest(pack, table, small):
    row = lax.broadcasted_iota(jnp.int32, (8, 2 * C), 0)
    for chunk in range(8):
        own = table[:, 384 * chunk : 384 * chunk + 384]
        if chunk < 2:
            left = table[:, 3072 + 128 * chunk : 3200 + 128 * chunk]
            moved = [pltpu.roll(left, 6 - 2 * i, 0) if i < 3 else left for i in range(3)]
            own = jnp.where(row >= 6, jnp.concatenate(moved, axis=1), own)
        short = jnp.where(row == 0, small[chunk], 0.0) if chunk < len(small) else jnp.zeros((8, 2 * C), f32)
        pack[chunk, ROWS : ROWS + 16] = jnp.concatenate([own, short], axis=0).astype(bf16)


def attend_fwd(k, u, inward, inbias, outward, outbias, bias_ref, q_ref, k_ref, v_ref, p_ref, mix_ref):
    weight = inward[0].astype(bf16)
    shift = inbias[k : k + 1]
    keyed = pad_keys(u.astype(f32)).astype(bf16)
    q = (dot(u, weight[:, :C]) + shift[:, :C]).astype(bf16)
    key = (dot(keyed, weight[:, C : 2 * C]) + shift[:, C : 2 * C]).astype(bf16)
    v = (dot(keyed, weight[:, 2 * C :]) + shift[:, 2 * C :]).astype(bf16)
    q_ref[...] = q
    k_ref[...] = key
    v_ref[...] = v
    mix = jnp.zeros((TOK, C), f32)
    for h in range(HEADS):
        scores = dot_nt(head_only(q, h), key) * 32 ** (-0.5) + bias_ref[:, h * KEYS : (h + 1) * KEYS]
        weights = jnp.exp(scores - jnp.max(scores, axis=-1, keepdims=True))
        chances = (weights / jnp.sum(weights, axis=-1, keepdims=True)).astype(bf16)
        p_ref[h] = chances
        mix = mix + dot(chances, head_only(v, h))
    mix = mix.astype(bf16)
    mix_ref[...] = mix
    return (dot(mix, outward[0].astype(bf16)) + outbias[k : k + 1]).astype(bf16)


def attend_bwd(dout, u, inward, outward, spread, place, sort, q_ref, k_ref, v_ref, p_ref, mix_ref, pack, dbias_ref, turn_ref):
    q, key, v, mix = q_ref[...], k_ref[...], v_ref[...], mix_ref[...]
    weight = inward[0].astype(bf16)
    dmix = dot_nt(dout, outward[0].astype(bf16)).astype(bf16)
    dq = jnp.zeros((TOK, C), f32)
    dk = jnp.zeros((KEYS, C), f32)
    dv = jnp.zeros((KEYS, C), f32)
    for h in range(HEADS):
        chances = p_ref[h]
        wide = chances.astype(f32)
        dmix_h = head_only(dmix, h)
        dchances = dot_nt(dmix_h, v)
        dscores = wide * (dchances - jnp.sum(wide * dchances, axis=-1, keepdims=True))
        narrow = dscores.astype(bf16)
        dbias_ref[:, h * KEYS : (h + 1) * KEYS] = narrow
        dv = dv + dot_tn(chances, dmix_h)
        dq = dq + dot(narrow, head_only(key, h))
        dk = dk + dot_tn(narrow, head_only(q, h))
    dq = (dq * 32 ** (-0.5)).astype(bf16)
    dk = (dk * 32 ** (-0.5)).astype(bf16)
    dv = dv.astype(bf16)
    keyed = pad_keys(u.astype(f32)).astype(bf16)
    du = dot_nt(dq, weight[:, :C]) + unpad_keys(
        dot_nt(dk, weight[:, C : 2 * C]) + dot_nt(dv, weight[:, 2 * C :])
    )
    pair = lambda x, y: jnp.concatenate([x, y], axis=1)
    put(pack, 4 * C, pair(dot_tn(u, dq), dot_tn(keyed, dk)))
    put(pack, 5 * C, pair(dot_tn(keyed, dv), dot_tn(mix, dout)))
    small = [
        pair(colsum(dq.astype(f32)), colsum(dk.astype(f32))),
        pair(colsum(dv.astype(f32)), colsum(dout.astype(f32))),
    ]
    return du, table_adjoint(dbias_ref[...], spread, place, sort, turn_ref), small


def mlp_fwd(h, gain, shift, expand, upbias, narrow_t, downbias):
    z = dot(norm_fwd(h, gain, shift), expand) + upbias
    hidden = gelu_parts(z)[1].astype(bf16)
    return (h + dot_nt(hidden, narrow_t) + downbias).astype(bf16)


def mlp_both(h, gain, shift, expand, upbias, narrow_t, downbias, dout, want):
    normed = norm_fwd(h, gain, shift)
    z = dot(normed, expand) + upbias
    cdf, wide = gelu_parts(z)
    hidden = wide.astype(bf16)
    result = None
    if want:
        result = (h + dot_nt(hidden, narrow_t) + downbias).astype(bf16)
    slope = cdf + z * jnp.exp(-0.5 * z * z) * (1.0 / math.sqrt(2.0 * math.pi))
    dz32 = dot(dout, narrow_t) * slope
    dz = dz32.astype(bf16)
    dnormed = dot_nt(dz, expand).astype(bf16).astype(f32)
    dx, dgain, dshift = norm_bwd(h, gain, dnormed)
    dwide = dout.astype(f32)
    dh = (dwide + dx).astype(bf16)
    dexpand = dot_tn(normed, dz)
    dnarrow = dot_tn(dout, hidden)
    dense = [dexpand[:, : 2 * C], dexpand[:, 2 * C :], dnarrow[:, : 2 * C], dnarrow[:, 2 * C :]]
    dup = colsum(dz32)
    small = [
        dup[:, : 2 * C],
        dup[:, 2 * C :],
        jnp.concatenate([colsum(dwide), dgain], axis=1),
        jnp.concatenate([dshift, jnp.zeros((1, C), f32)], axis=1),
    ]
    return result, dh, dense, small


def bias_kernel(types, valid, tables, spread, place, sort, bias_ref, turned, rows):
    make_bias(1, types, valid, tables, spread[...], low(place), low(sort), bias_ref, turned, rows)


def first_kernel(
    types, valid, fields, upstream, scales, offsets, inward, inbias, outward, outbias, expand, upbias, narrow, downbias,
    tables, turn, cut, spread, place, sort,
    q, k, v, p, mix, h1, pa, pb, pc, pd, bias, turned, rows,
):
    make_bias(0, types, valid, tables, spread[...], low(place), low(sort), bias, turned, rows)
    order, route = low(turn), low(cut)
    x = dot(order, fields[...])
    u = norm_fwd(x, scales[0, 0:1], offsets[0, 0:1])
    branch = attend_fwd(0, u, inward, inbias, outward, outbias, bias, q, k, v, p, mix)
    carried = (x + branch.astype(f32)).astype(bf16)
    h1[...] = carried
    out = mlp_fwd(
        carried.astype(f32), scales[0, 1:2], offsets[0, 1:2], expand[0].astype(bf16), upbias[0:1],
        narrow[0].astype(bf16), downbias[0:1],
    )
    cotangent = dot(order, upstream[...]).astype(bf16)
    write_pieces(dot(route, out), dot(route, cotangent), (pa, pb, pc, pd))


def second_kernel(
    qa, qb, qc, qd, scales, offsets, inward, inbias, outward, outbias, expand, upbias, narrow, downbias,
    bias, join, spread, place, sort,
    pack, pa, pb, pc, pd, q, k, v, p, mix, dbias, turned,
):
    route = low(join)
    pieces = (qa, qb, qc, qd)
    y1 = dot(route, join_rows(pieces, 0))
    cotangent = dot(route, join_rows(pieces, 1)).astype(bf16)
    u = norm_fwd(y1, scales[1, 0:1], offsets[1, 0:1])
    branch = attend_fwd(1, u, inward, inbias, outward, outbias, bias, q, k, v, p, mix)
    h2 = (y1 + branch.astype(f32)).astype(bf16).astype(f32)
    out, dh, dense, short = mlp_both(
        h2, scales[1, 1:2], offsets[1, 1:2], expand[0].astype(bf16), upbias[1:2],
        narrow[0].astype(bf16), downbias[1:2], cotangent, True,
    )
    for i, part in enumerate(dense):
        put(pack, i * C, part)
    du, table, small = attend_bwd(
        dh, u, inward, outward, spread[...], low(place), low(sort), q, k, v, p, mix, pack, dbias, turned
    )
    dx, dgain, dshift = norm_bwd(y1, scales[1, 0:1], du.astype(bf16).astype(f32))
    dy1 = (dh.astype(f32) + dx.astype(bf16).astype(f32)).astype(bf16)
    put_rest(pack, table, short + small + [jnp.concatenate([dgain, dshift], axis=1)])
    write_pieces(dot_tn(route, dy1), dot_tn(route, out), (pa, pb, pc, pd))


def first_back_kernel(
    qa, qb, qc, qd, fields, h1, scales, offsets, inward, outward, expand, upbias, narrow, downbias,
    q, k, v, p, mix, turn, cut, spread, place, sort,
    result, adjoint, pack, dbias, turned,
):
    order, route = low(turn), low(cut)
    pieces = (qa, qb, qc, qd)
    result[...] = dot_tn(order, dot_tn(route, join_rows(pieces, 1)).astype(bf16)).astype(bf16)
    dy1 = dot_tn(route, join_rows(pieces, 0)).astype(bf16)
    _, dh1, dense, short = mlp_both(
        h1[...].astype(f32), scales[0, 1:2], offsets[0, 1:2], expand[0].astype(bf16), upbias[0:1],
        narrow[0].astype(bf16), downbias[0:1], dy1, False,
    )
    for i, part in enumerate(dense):
        put(pack, i * C, part)
    x = dot(order, fields[...])
    u = norm_fwd(x, scales[0, 0:1], offsets[0, 0:1])
    du, table, small = attend_bwd(
        dh1, u, inward, outward, spread[...], low(place), low(sort), q, k, v, p, mix, pack, dbias, turned
    )
    dx0, dgain0, dshift0 = norm_bwd(x, scales[0, 0:1], du.astype(bf16).astype(f32))
    adjoint[...] = dot_tn(order, (dh1.astype(f32) + dx0).astype(bf16)).astype(bf16)
    put_rest(pack, table, short + small + [jnp.concatenate([dgain0, dshift0], axis=1)])


def core_kernel(first, second, got_first, got_second, *refs):
    outs, (own, got, made, sems) = refs[:8], refs[8:]
    _, core, side, rep = place_of()
    part = lambda n: pl.ds((rep ^ (n // 2)) * 2 + (side ^ (n % 2)), 1)
    order = (5, 3, 7, 1, 4, 2, 6, 0)
    for k, (mine, theirs) in enumerate(((first, got_first), (second, got_second))):

        @pl.when(core == k)
        def _(mine=mine, theirs=theirs):
            for n in order:
                pltpu.make_async_copy(mine.at[part(n)], own.at[n], sems.at[n]).start()
                pltpu.make_async_copy(theirs.at[part(n)], got.at[n], sems.at[8 + n]).start()

    sent = []
    for n in order:
        pltpu.make_async_copy(first.at[part(n)], own.at[n], sems.at[n]).wait()
        pltpu.make_async_copy(got_first.at[part(n)], got.at[n], sems.at[8 + n]).wait()
        made[n] = (own[n].astype(f32) + got[n].astype(f32)).astype(bf16)
        sent.append(pltpu.make_async_copy(made.at[n], outs[n], sems.at[16 + n]))
        sent[-1].start()
    for copy in sent:
        copy.wait()


def add_kernel(*refs):
    total = refs[0][...].astype(f32)
    for ref in refs[1:-1]:
        total = total + ref[...].astype(f32)
    refs[-1][...] = total.astype(bf16)


def band_kernel(a, b, c, d, out):
    four = [ref[...].astype(f32) for ref in (a, b, c, d)]
    total = four[0] + four[1] + four[2] + four[3]
    out[:ROWS] = total[:ROWS].astype(bf16)
    if a.shape[0] == CHUNK:
        aside = jnp.concatenate([total[ROWS + 8 :], jnp.zeros((8, 2 * C), f32)], axis=0)
        out[ROWS:CHUNK] = aside.astype(bf16)
        out[CHUNK:] = jnp.concatenate([m[ROWS : ROWS + 8] for m in four], axis=0).astype(bf16)
    else:
        out[ROWS:CHUNK] = total[ROWS:CHUNK].astype(bf16)
        for i, ref in enumerate((a, b, c, d)):
            out[CHUNK + 32 * i : CHUNK + 32 * i + 32] = ref[CHUNK:]


def final_kernel(factor, types, own_near, own_far, got_near, got_far, *refs):
    own, got = (own_near, own_far), (got_near, got_far)
    big, short = refs[:5], refs[5:11]
    inward, outward, expand, narrow, tables, dense, sems = refs[11:]
    scales, offsets, inbias, outbias, upbias, downbias = short
    band, core, side, rep = place_of()
    lane = lax.broadcasted_iota(jnp.int32, (1, 128), 1)
    row = lax.broadcasted_iota(jnp.int32, (96, 128), 0)
    part = lax.broadcasted_iota(jnp.int32, (96, 128), 1) & 7
    head = row >> 4

    def unpack(k, sides, s):
        kind = jnp.zeros((1, 128), jnp.int32)
        for e in range(16):
            kind = kind + jnp.where((lane >> 3) == e, types[k, 0, band ^ e], 0)
        match = (row & 15) == kind
        made = [match & (part == head)]
        for i in range(3):
            made.append(match & ((head >> 1) == i) & (part == 6 + (head & 1)))
        route = [jnp.where(m, 1.0, 0.0).astype(bf16) for m in made]
        small = []
        for chunk in range(8):
            y, ref = rep ^ (chunk // 2), sides[s ^ (chunk % 2)]
            dense[chunk * ROWS : (chunk + 1) * ROWS] = ref[y, :ROWS]
            small.append(ref[y, ROWS:CHUNK].astype(f32)[0:1] * factor)
            here = ref[y, CHUNK:]
            rows = dot(route[0], here) * factor
            for h in range(HEADS):
                tables[k, h, :, 384 * chunk : 384 * chunk + 384] = rows[16 * h : 16 * h + 16]
            if chunk < 2:
                left = sum(dot(route[1 + i], here[:, 128 * i : 128 * i + 128]) for i in range(3)) * factor
                start = 3072 + 128 * chunk
                size = min(128, REL - start)
                for h in range(HEADS):
                    tables[k, h, :, start : start + size] = left[16 * h : 16 * h + 16, :size]
        load = lambda i: dense[i * C : (i + 1) * C].astype(f32) * factor
        expand[k, :, : 2 * C] = load(0)
        expand[k, :, 2 * C :] = load(1)
        narrow[k, :, : 2 * C] = load(2)
        narrow[k, :, 2 * C :] = load(3)
        inward[k, :, : 2 * C] = load(4)
        both = load(5)
        inward[k, :, 2 * C :] = both[:, :C]
        outward[k] = both[:, C:]
        upbias[k : k + 1, : 2 * C] = small[0]
        upbias[k : k + 1, 2 * C :] = small[1]
        downbias[k : k + 1] = small[2][:, :C]
        scales[k, 1:2] = small[2][:, C:]
        offsets[k, 1:2] = small[3][:, :C]
        inbias[k : k + 1, : 2 * C] = small[4]
        inbias[k : k + 1, 2 * C :] = small[5][:, :C]
        outbias[k : k + 1] = small[5][:, C:]
        scales[k, 0:1] = small[6][:, :C]
        offsets[k, 0:1] = small[6][:, C:]

    sent = []
    for k in range(2):
        for source, wanted in ((own, core == k), (got, core != k)):

            for s in range(2):

                @pl.when(wanted & (side == s))
                def _(k=k, source=source, s=s):
                    unpack(k, source, s)

        for n, array in enumerate((inward, outward, expand, narrow, tables)):
            sent.append(pltpu.make_async_copy(array.at[k], big[n].at[k], sems.at[5 * k + n]))
            sent[-1].start()
    for copy in sent:
        copy.wait()


def call(kernel, ins, outs, scratch=(), far_outs=0, raw_outs=0, aliases={}, limit=VMEM):
    specs, fetched, slots = [], [], []
    for array, block, far in ins:
        dims = array.ndim
        shape = array.shape if block in (None, "smem", "raw") else (1,) + array.shape[1:]
        if block == "smem":
            specs.append(pl.BlockSpec(memory_space=pltpu.SMEM))
        elif block == "raw":
            specs.append(pl.BlockSpec(memory_space=pltpu.HBM))
        elif far:
            specs.append(pl.BlockSpec(memory_space=pltpu.HBM))
            fetched.append((len(specs) - 1, block))
            slots.append(pltpu.VMEM(shape, array.dtype))
        else:
            specs.append(pl.BlockSpec(array.shape, lambda i, dims=dims: (0,) * dims))
    out_specs = []
    for i, o in enumerate(outs):
        if i < raw_outs:
            out_specs.append(pl.BlockSpec(memory_space=pltpu.HBM))
        elif i < far_outs:
            out_specs.append(pl.BlockSpec(memory_space=pltpu.HBM))
            slots.append(pltpu.VMEM(o.shape, o.dtype))
        else:
            out_specs.append(pl.BlockSpec(o.shape, lambda i, dims=len(o.shape): (0,) * dims))

    def wrapped(*refs):
        in_refs, refs = list(refs[: len(ins)]), refs[len(ins) :]
        out_refs, refs = list(refs[: len(outs)]), refs[len(outs) :]
        own, refs = refs[: len(scratch)], refs[len(scratch) :]
        copies = []
        for n, (at, block) in enumerate(fetched):
            source = in_refs[at] if block is None else in_refs[at].at[block : block + 1]
            copies.append(pltpu.make_async_copy(source, refs[n], refs[-1].at[n]))
            in_refs[at] = refs[n]
        for copy in copies:
            copy.start()
        for copy in copies:
            copy.wait()
        targets = out_refs[:far_outs]
        out_refs[:far_outs] = refs[len(fetched) : len(fetched) + far_outs]
        kernel(*in_refs, *out_refs, *own)
        copies = [
            pltpu.make_async_copy(out_refs[n], targets[n], refs[-1].at[len(fetched) + n]) for n in range(far_outs)
        ]
        for copy in copies:
            copy.start()
        for copy in copies:
            copy.wait()

    size = lambda s: math.prod(s.shape) * jnp.dtype(s.dtype).itemsize
    moved = sum(size(o) for o in outs) + sum(size(a) for a, b, _ in ins)
    if slots:
        slots.append(pltpu.SemaphoreType.DMA((len(slots),)))
    return pl.pallas_call(
        wrapped,
        grid=(1,),
        in_specs=specs,
        out_specs=out_specs,
        out_shape=outs,
        scratch_shapes=list(scratch) + slots,
        input_output_aliases=aliases,
        compiler_params=pltpu.CompilerParams(vmem_limit_bytes=limit),
        cost_estimate=pl.CostEstimate(flops=10**9, bytes_accessed=moved, transcendentals=0),
    )(*[array for array, _, _ in ins])


def send_pieces(pieces, step):
    lat, lon = lax.axis_size("lat"), lax.axis_size("lon")
    rows = [(i, (i + step) % lat) for i in range(lat)]
    cols = [(i, (i + step) % lon) for i in range(lon)]
    both = [(i * lon + j, (i + step) % lat * lon + (j + step) % lon) for i in range(lat) for j in range(lon)]
    return (
        pieces[0],
        lax.ppermute(pieces[1], "lat", rows),
        lax.ppermute(pieces[2], "lon", cols),
        lax.ppermute(pieces[3], ("lat", "lon"), both),
    )


def swap(array, axis, distance):
    return lax.ppermute(array, axis, [(i, i ^ distance) for i in range(lax.axis_size(axis))])


def body(
    fields, upstream, scales, offsets, inward, inbias, outward, outbias, expand, upbias, narrow, downbias,
    tables, window_type, row_valid,
):
    const = constants()
    levels, row_count, col_count = fields.shape[1:4]
    total_rows = row_valid.shape[0]
    x = fields[0].transpose(1, 2, 0, 3).reshape(TOK, C)
    cotangent = upstream[0].transpose(1, 2, 0, 3).reshape(TOK, C)
    narrow = jnp.swapaxes(narrow, 1, 2)
    tables = jnp.swapaxes(tables, 1, 2)
    of = jax.ShapeDtypeStruct
    piece = [of((2 * QUAD, C), bf16)] * 4
    token = of((TOK, C), bf16)
    state = [token, of((KEYS, C), bf16), of((KEYS, C), bf16), of((HEADS, TOK, KEYS), bf16), token]
    pack = of((8, CHUNK, 2 * C), bf16)
    turned = pltpu.VMEM((192, 1536), bf16)
    dbias = pltpu.VMEM((TOK, 1536), bf16)
    rows = pltpu.VMEM((8, 3456), f32)
    near = lambda *arrays: [(m, None, False) for m in arrays]
    far = lambda *arrays: [(m, None, True) for m in arrays]
    block = lambda k, *arrays: [(m, k, True) for m in arrays]
    raw = lambda *arrays: [(m, "raw", True) for m in arrays]
    fixed = lambda *names: far(*[const[name] for name in names])
    scalars = [(window_type, "smem", False), (row_valid, "smem", False)]

    def weights(k):
        return (
            far(scales, offsets) + block(k, inward) + far(inbias) + block(k, outward) + far(outbias)
            + block(k, expand) + far(upbias) + block(k, narrow) + far(downbias)
        )

    *state0, h1, pa, pb, pc, pd = call(
        first_kernel,
        scalars + far(x, cotangent) + weights(0) + block(0, tables) + fixed("turn", "cut", "spread", "place", "sort"),
        state + [token] + piece,
        (pltpu.VMEM((TOK, 1536), f32), turned, rows),
        6,
    )
    pieces = send_pieces((pa, pb, pc, pd), -1)
    (bias1,) = call(
        bias_kernel,
        scalars + block(1, tables) + fixed("spread", "place", "sort"),
        [of((TOK, 1536), f32)],
        (turned, rows),
    )
    pack1, *pieces = call(
        second_kernel,
        far(*pieces) + weights(1) + far(bias1) + fixed("join", "spread", "place", "sort"),
        [pack] + piece,
        [pltpu.VMEM(m.shape, m.dtype) for m in state] + [dbias, turned],
    )
    pieces = send_pieces(pieces, 1)
    got1 = swap(pack1, "lon", 1)
    result, adjoint, pack0 = call(
        first_back_kernel,
        far(*pieces, x, h1, scales, offsets) + block(0, inward, outward, expand) + far(upbias)
        + block(0, narrow) + far(downbias, *state0) + fixed("turn", "cut", "spread", "place", "sort"),
        [token, token, pack],
        (dbias, turned),
    )
    got0 = swap(pack0, "lon", 1)

    part = of((1, CHUNK, 2 * C), bf16)
    dealt = call(
        core_kernel,
        raw(pack0, pack1, got0, got1),
        [part] * 8,
        [pltpu.VMEM((8,) + part.shape, bf16)] * 3 + [pltpu.SemaphoreType.DMA((24,))],
        raw_outs=8,
    )
    over = lambda parts: [parts[0]] + [swap(parts[d], "rep", d) for d in (1, 2, 3)]
    give = call(add_kernel, near(*over(dealt[1::2])), [part], limit=SMALL)[0]
    a = call(add_kernel, near(*over(dealt[0::2]), swap(give, "lon", 2)), [part], limit=SMALL)[0][0]
    for step, height in ((1, CHUNK + 32), (4, CHUNK + 128)):
        others = [swap(a, "lat", step * i) for i in (1, 2, 3)]
        (a,) = call(band_kernel, near(a, *others), [of((height, 2 * C), bf16)], limit=SMALL)
    beside = swap(a, "lon", 2)
    own = [jnp.stack(over([m] * 4)) for m in (a, beside)]
    got = [swap(m, "lon", 1) for m in own]

    factor = 1.0 / math.sqrt(lax.axis_size("rep") * levels * total_rows * col_count * lax.axis_size("lon"))

    wide = [(2, C, 3 * C), (2, C, C), (2, C, FFN), (2, C, FFN), tables.shape]
    short = [(2, 2, C), (2, 2, C), (2, 3 * C), (2, C), (2, FFN), (2, C)]
    joined = call(
        functools.partial(final_kernel, factor),
        scalars[:1] + near(*own, *got),
        [of(m, f32) for m in wide + short],
        [pltpu.VMEM(m, f32) for m in wide]
        + [pltpu.VMEM((8 * ROWS, 2 * C), bf16), pltpu.SemaphoreType.DMA((10,))],
        raw_outs=5,
        limit=2 * SMALL,
    )
    inward_out, outward_out, expand_out, narrow_out, tables_out = joined[:5]
    scales_out, offsets_out, inbias_out, outbias_out, upbias_out, downbias_out = joined[5:]
    back = lambda m: m.reshape(row_count, col_count, levels, C).transpose(2, 0, 1, 3)[None]
    return (
        back(result), back(adjoint), scales_out, offsets_out, inward_out, inbias_out, outward_out, outbias_out,
        expand_out, upbias_out, jnp.swapaxes(narrow_out, 1, 2), downbias_out, jnp.swapaxes(tables_out, 1, 2),
    )


def solution(mesh):
    grid = P("rep", None, "lat", "lon", None)
    return jax.shard_map(
        body, mesh=mesh, in_specs=(grid, grid) + (P(),) * 13, out_specs=(grid, grid) + (P(),) * 11, check_vma=False
    )
```
